32 devices in a mesh: wide: 8 (over y, x, core), narrow: 4 (over z).
Axes of the slice: x: 2, y: 2, z: 4, core: 2. Of those that a mesh axis runs over, the one named last changes fastest.
Arguments:
- amplitudes: float32 [1024, 8192], P(('wide', 'narrow')), may hold values from -6 to 6
- integrals: float32 [8192, 8192], P('narrow', 'wide'), may hold values from -0.125 to 0.125
- bare_terms: float32 [1024, 8192], P('wide', 'narrow'), may hold values from -6 to 6
- pattern: int32 [8, 64], replicated, may hold values 0 or 1
- block_order: int32 [8], replicated, may hold values from 0 to 7, each once
- occ_gap: float32 [1024], P('wide'), may hold values from 0.3 to 3
- virt_gap: float32 [8192], P('narrow'), may hold values from 0.3 to 3
Outputs:
- update: float32 [1024, 8192], P('wide', 'narrow')
The draws below stay inside these ranges and needn't reach their ends.
All inputs are finite; a program needn't handle non-finite values.
Results may differ from the reference program's by a relative error of at most 0.000054.
Values sent between devices are 32-bit elements; how exact they have to be, the bound alone decides.
No kernel may reach another device: no remote copies, remote signals or barrier semaphores. Data moves between devices by JAX's collectives and lax.ppermute only.
A program may use at most 192 MiB of HBM per device.

```python
import math
import jax
import jax.numpy as jnp
from jax import lax

TILE = 128
VIR_TILES = 64
OCC_TILES = 8
PAIR_ROWS = 1024
VIRT_COLS = 8192


def plant(array, rng, low, largest):
    shape = array.shape
    place = [jax.random.randint(jax.random.fold_in(rng, axis), (), 0, shape[axis]) for axis in range(len(shape))]
    array = array.at[tuple(place)].set(low)
    longest = shape.index(max(shape))
    place[longest] = (place[longest] + 1) % shape[longest]
    return array.at[tuple(place)].set(largest)


def with_spikes(values, rng, source, target, shards_of, factor):
    def block_of(dim):
        return (jnp.arange(values.shape[dim]) // (values.shape[dim] // shards_of)).reshape((-1,) + (1,) * (values.ndim - 1 - dim))

    near = jax.random.permutation(rng, shards_of)[block_of(target)]
    far = (block_of(target) + shards_of // 2) % shards_of
    return jnp.where((block_of(source) == near) | (block_of(source) == far), factor * values, values)


def steps_of(own_key, extent, shards, least, high):
    def one(position, shards_of):
        steps = jax.random.uniform(jax.random.fold_in(jax.random.fold_in(own_key, 6), position), (shards_of,), jnp.float32, least / len(shards), high / len(shards))
        return jnp.repeat(jnp.exp(steps), extent[position] // shards_of).reshape((-1,) + (1,) * (len(extent) - position - 1))

    level = one(*shards[0])
    for cut in shards[1:]:
        level = level * one(*cut)
    return level


def noise(stream_key, dims, spread, reach, cuts=(), dtype=jnp.bfloat16):
    entries = spread * jax.random.normal(stream_key, dims, jnp.float32)
    if cuts:
        entries = entries * steps_of(stream_key, dims, cuts, -0.22, 0.18)
    return jnp.clip(entries, -reach, reach).astype(dtype)


def bell_draw_with(key, shape, spread, bound, shards, heavy, dtype=jnp.bfloat16):
    result = spread * jax.random.normal(key, shape, jnp.float32)
    if shards:
        result = result * steps_of(key, shape, shards, -0.22, 0.18)
    return jnp.clip(with_spikes(result, jax.random.fold_in(key, 3), *heavy), -bound, bound).astype(dtype)


def setup_inputs(seed: int = 0) -> dict:
    keys = jax.random.split(jax.random.key(seed), 8)
    return {
        "amplitudes": noise(keys[0], (PAIR_ROWS, VIRT_COLS), 1.0, 6.0, ((0, 32),), jnp.float32),
        "integrals": bell_draw_with(keys[1], (VIRT_COLS, VIRT_COLS), (VIRT_COLS // 2) ** -0.5, 0.125, ((0, 4), (1, 8)), (0, 1, 8, 2.0), jnp.float32),
        "bare_terms": noise(keys[2], (PAIR_ROWS, VIRT_COLS), 1.0, 6.0, ((0, 8), (1, 4)), jnp.float32),
        "pattern": plant((jax.random.randint(keys[3], (OCC_TILES, VIR_TILES), 0, 2) < 1).astype(jnp.int32), jax.random.fold_in(keys[3], 1), 0, 1),
        "block_order": jax.random.permutation(keys[4], OCC_TILES).astype(jnp.int32),
        "occ_gap": jnp.clip(jnp.exp(math.log(3.0) - 2.3025851 * jax.random.uniform(keys[5], (PAIR_ROWS,), jnp.float32) ** steps_of(keys[5], (PAIR_ROWS,), ((0, 8),), -0.2, 0.2)), 0.3, 3.0),
        "virt_gap": jnp.clip(jnp.exp(math.log(3.0) - 2.3025851 * jax.random.uniform(keys[6], (VIRT_COLS,), jnp.float32) ** steps_of(keys[6], (VIRT_COLS,), ((0, 4),), -0.2, 0.2)), 0.3, 3.0),
    }


def reference(amplitudes, integrals, bare_terms, pattern, block_order, occ_gap, virt_gap):
    row_pattern = pattern[block_order.astype(jnp.int32)].astype(jnp.float32)
    full_mask = jnp.repeat(jnp.repeat(row_pattern, TILE, axis=0), TILE, axis=1)
    screened = amplitudes * full_mask
    ladder = jnp.dot(screened, integrals, preferred_element_type=jnp.float32, precision=lax.Precision.HIGHEST)
    return -(bare_terms + ladder) / (occ_gap[:, None] + virt_gap[None, :])
```

```python
import jax
import jax.numpy as jnp
from jax import lax
from jax.sharding import PartitionSpec as P

TILE = 128
CHUNKS = 4


def shards(amplitudes, integrals, bare_terms, pattern, block_order, occ_gap, virt_gap):
    rows_local, columns = amplitudes.shape
    vir_count = pattern.shape[1]
    wide_count = lax.axis_size("wide")
    narrow_count = lax.axis_size("narrow")
    position = lax.axis_index("wide") * narrow_count + lax.axis_index("narrow")
    tile = position * rows_local // TILE
    row_pattern = pattern[block_order[tile]].astype(jnp.float32)
    screened = (
        amplitudes.reshape(rows_local, vir_count, TILE) * row_pattern[None, :, None]
    ).reshape(rows_local, columns)
    part = rows_local // CHUNKS
    rows_out, columns_out = bare_terms.shape
    ladders = []
    for chunk in range(CHUNKS):
        piece = screened[chunk * part : (chunk + 1) * part]
        transposed = lax.all_to_all(piece, "narrow", split_axis=1, concat_axis=0, tiled=True)
        stacked = jnp.dot(
            lax.all_gather(transposed, "wide", axis=0, tiled=True),
            integrals,
            preferred_element_type=jnp.float32,
            precision=lax.Precision.HIGH,
        )
        partial_value = lax.all_to_all(stacked, "wide", split_axis=0, concat_axis=1, tiled=True)
        ladder = lax.psum_scatter(partial_value, "narrow", scatter_dimension=1, tiled=True)
        ladders.append(ladder.reshape(narrow_count, part, columns_out))
    ladder = jnp.stack(ladders, axis=1).reshape(rows_out, columns_out)
    denominator = occ_gap[:, None] + virt_gap[None, :]
    return -(bare_terms + ladder) / denominator


def solution(mesh):
    placed = (
        P(("wide", "narrow"), None),
        P("narrow", "wide"),
        P("wide", "narrow"),
        P(),
        P(),
        P("wide"),
        P("narrow"),
    )
    return jax.shard_map(
        shards, mesh=mesh, in_specs=placed, out_specs=P("wide", "narrow"), check_vma=False
    )
```

```python
import functools

import jax
import jax.numpy as jnp
from jax import lax
from jax.experimental import pallas as pl
from jax.experimental.pallas import tpu as pltpu
from jax.sharding import PartitionSpec as P

TILE = 128
CHUNKS = 4
CORES = 2


def split_kernel(whole_ref, high_ref, low_ref):
    whole = whole_ref[...]
    high = whole.astype(jnp.bfloat16)
    high_ref[...] = high
    low_ref[...] = (whole - high.astype(jnp.float32)).astype(jnp.bfloat16)


def split(whole):
    rows, columns = whole.shape
    block = pl.BlockSpec((256, columns), lambda i: (i, 0))
    half = jax.ShapeDtypeStruct((rows, columns), jnp.bfloat16)
    return pl.pallas_call(
        split_kernel,
        grid=(rows // 256,),
        in_specs=[block],
        out_specs=[block, block],
        out_shape=[half, half],
        cost_estimate=pl.CostEstimate(
            flops=rows * columns, bytes_accessed=8 * rows * columns, transcendentals=0
        ),
        compiler_params=pltpu.CompilerParams(vmem_limit_bytes=16 * 2**20),
        name="split",
    )(whole)


def product_kernel(count, steps, *refs):
    lefts = refs[:count]
    own_high, own_low, other_high, other_low = refs[count : count + 4]
    outs = refs[count + 4 : 2 * count + 4]
    left = refs[2 * count + 4]
    rows = lefts[0].shape[0]
    total = count * rows
    step = pl.program_id(0)

    @pl.when(step == 0)
    def _():
        for k in range(count):
            value = lefts[k][...]
            high = value.astype(jnp.bfloat16)
            left[k * rows : (k + 1) * rows, :] = high
            left[total + k * rows : total + (k + 1) * rows, :] = (
                value - high.astype(jnp.float32)
            ).astype(jnp.bfloat16)

    def multiply(high_ref, low_ref):
        both = jnp.dot(left[...], high_ref[...], preferred_element_type=jnp.float32)
        small = jnp.dot(left[:total, :], low_ref[...], preferred_element_type=jnp.float32)
        result = both[:total] + (both[total:] + small)
        for k in range(count):
            outs[k][...] = result[k * rows : (k + 1) * rows]

    @pl.when(step < steps)
    def _():
        multiply(own_high, own_low)

    @pl.when(step >= steps)
    def _():
        multiply(other_high, other_low)


def product(lefts, own, other):
    count = len(lefts)
    rows, depth = lefts[0].shape
    columns = own[0].shape[1]
    width = min(512, columns)
    steps = columns // width
    total = count * rows
    left_spec = pl.BlockSpec((rows, depth), lambda j: (0, 0))
    own_spec = pl.BlockSpec((depth, width), lambda j: (0, jnp.minimum(j, steps - 1)))
    other_spec = pl.BlockSpec((depth, width), lambda j: (0, jnp.maximum(j - steps, 0)))
    out_spec = pl.BlockSpec((rows, width), lambda j: (0, j))
    return pl.pallas_call(
        functools.partial(product_kernel, count, steps),
        grid=(2 * steps,),
        in_specs=[left_spec] * count + [own_spec] * 2 + [other_spec] * 2,
        out_specs=[out_spec] * count,
        out_shape=[jax.ShapeDtypeStruct((rows, 2 * columns), jnp.float32)] * count,
        scratch_shapes=[pltpu.VMEM((2 * total, depth), jnp.bfloat16)],
        cost_estimate=pl.CostEstimate(
            flops=6 * total * depth * 2 * columns,
            bytes_accessed=8 * depth * columns + 8 * total * depth,
            transcendentals=0,
        ),
        compiler_params=pltpu.CompilerParams(vmem_limit_bytes=40 * 2**20),
        name="product",
    )(*lefts, *own, *other)


def choose(index, arrays):
    chosen = arrays[0]
    for k in range(1, len(arrays)):
        chosen = jnp.where(index == k, arrays[k], chosen)
    return chosen


def shards(amplitudes, integrals, bare_terms, pattern, block_order, occ_gap, virt_gap):
    rows_local, columns = amplitudes.shape
    depth, columns_local = integrals.shape
    rows_out, columns_out = bare_terms.shape
    wide_count = lax.axis_size("wide")
    narrow_count = lax.axis_size("narrow")
    chips = wide_count // CORES
    wide = lax.axis_index("wide")
    z = lax.axis_index("narrow")
    chip = wide // CORES
    core = wide % CORES
    part = rows_local // CHUNKS
    group = chips // narrow_count

    def across(value, mask):
        return lax.ppermute(value, "wide", [(w, w ^ mask) for w in range(wide_count)])

    def across_chips(value, mask):
        return across(value, mask * CORES)

    def along(value, mask):
        return lax.ppermute(value, "narrow", [(n, n ^ mask) for n in range(narrow_count)])

    own = split(integrals)
    other = split(across(integrals, 1))

    tile = (wide * narrow_count + z) * rows_local // TILE
    row_pattern = pattern[block_order[tile]].astype(jnp.float32)
    screen = jnp.repeat(row_pattern, TILE)[None, :]

    def gather(chunk):
        piece = amplitudes[chunk * part : (chunk + 1) * part]

        def slice_for(n):
            return lax.dynamic_slice_in_dim(piece, n * depth, depth, 1) * lax.dynamic_slice_in_dim(
                screen, n * depth, depth, 1
            )

        blocks = [slice_for(z)]
        for mask in range(1, narrow_count):
            blocks.append(along(slice_for(z ^ mask), mask))
        mine = jnp.concatenate([choose(z ^ n, blocks) for n in range(narrow_count)], axis=0)
        lefts = [mine]
        if chips == 4:
            lefts.append(across_chips(mine, 1))
            lefts.append(across_chips(mine, 2))
            if chunk % 2 == 0:
                lefts.append(across_chips(lefts[1], 2))
            else:
                lefts.append(across_chips(lefts[2], 1))
        else:
            for mask in range(1, chips):
                lefts.append(across_chips(mine, mask))
        return lefts

    def reduce(partials):
        arrived = [partials[0]]
        for mask in range(1, chips):
            arrived.append(across_chips(partials[mask], mask))

        def share(n):
            return jnp.concatenate(
                [choose(chip ^ (n * group + j), arrived) for j in range(group)], axis=1
            )

        up = down = None
        for step in range(1, narrow_count):
            send_up = share(z + narrow_count - step)
            send_down = share(z - narrow_count + step)
            if step > 1:
                send_up = send_up + up
                send_down = send_down + down
            up = lax.ppermute(send_up, "narrow", [(n, n + 1) for n in range(step)])
            down = lax.ppermute(
                send_down,
                "narrow",
                [(narrow_count - 1 - n, narrow_count - 2 - n) for n in range(step)],
            )
        return share(z) + (up + down)

    ladders = []
    for chunk in range(CHUNKS):
        partials = product(gather(chunk), own, other)
        ladder = reduce(partials).reshape(narrow_count, part, -1, CORES, columns_local)
        ladder = jnp.where(core == 0, ladder, ladder[:, :, :, ::-1])
        ladders.append(ladder.reshape(narrow_count, part, columns_out))
    ladder = jnp.stack(ladders, axis=1).reshape(rows_out, columns_out)
    denominator = occ_gap[:, None] + virt_gap[None, :]
    return -(bare_terms + ladder) / denominator


def solution(mesh):
    placed = (
        P(("wide", "narrow"), None),
        P("narrow", "wide"),
        P("wide", "narrow"),
        P(),
        P(),
        P("wide"),
        P("narrow"),
    )
    return jax.shard_map(
        shards, mesh=mesh, in_specs=placed, out_specs=P("wide", "narrow"), check_vma=False
    )
```

```python
import functools

import jax
import jax.numpy as jnp
from jax import lax
from jax.experimental import pallas as pl
from jax.experimental.pallas import tpu as pltpu
from jax.sharding import PartitionSpec as P

TILE = 128
CHUNKS = 4
CORES = 2


def split(whole):
    high = lax.reduce_precision(whole, 8, 7)
    return high.astype(jnp.bfloat16), (whole - high).astype(jnp.bfloat16)


def product_kernel(count, place_ref, pattern_ref, order_ref, *refs):
    lefts = refs[:count]
    factors = refs[count : count + 4]
    outs = refs[count + 4 : 2 * count + 4]
    left = refs[2 * count + 4]
    rows, depth = lefts[0].shape
    total = count * rows
    chip, core, z = place_ref[0], place_ref[1], place_ref[2]
    tiles = depth // TILE
    for k in range(count):
        kind = order_ref[(chip ^ k) * CORES + core]
        for t in range(tiles):
            kept = pattern_ref[kind, z * tiles + t].astype(jnp.float32)
            here = slice(t * TILE, (t + 1) * TILE)
            value = lefts[k][:, here] * kept
            high = value.astype(jnp.bfloat16)
            left[k * rows : (k + 1) * rows, here] = high
            left[total + k * rows : total + (k + 1) * rows, here] = (
                value - high.astype(jnp.float32)
            ).astype(jnp.bfloat16)
    columns = factors[0].shape[1]
    width = min(512, columns)
    for half in range(2):
        high_ref, low_ref = factors[2 * half : 2 * half + 2]
        for j in range(columns // width):
            here = slice(j * width, (j + 1) * width)
            both = jnp.dot(left[...], high_ref[:, here], preferred_element_type=jnp.float32)
            small = jnp.dot(
                left[:total, :], low_ref[:, here], preferred_element_type=jnp.float32
            )
            result = both[:total] + (both[total:] + small)
            there = slice(half * columns + j * width, half * columns + (j + 1) * width)
            for k in range(count):
                outs[k][:, there] = result[k * rows : (k + 1) * rows]


def product(lefts, own, other, place, pattern, block_order):
    count = len(lefts)
    rows, depth = lefts[0].shape
    columns = own[0].shape[1]
    total = count * rows
    small = pl.BlockSpec(memory_space=pltpu.SMEM)
    large = pl.BlockSpec(memory_space=pltpu.VMEM)
    return pl.pallas_call(
        functools.partial(product_kernel, count),
        in_specs=[small] * 3 + [large] * (count + 4),
        out_specs=[large] * count,
        out_shape=[jax.ShapeDtypeStruct((rows, 2 * columns), jnp.float32)] * count,
        scratch_shapes=[pltpu.VMEM((2 * total, depth), jnp.bfloat16)],
        cost_estimate=pl.CostEstimate(
            flops=6 * total * depth * 2 * columns,
            bytes_accessed=8 * total * depth,
            transcendentals=0,
        ),
        compiler_params=pltpu.CompilerParams(vmem_limit_bytes=24 * 2**20),
        name="product",
    )(place, pattern, block_order, *lefts, *own, *other)


def after(value, *others):
    return lax.optimization_barrier((value, *others))[0]


def choose(index, arrays):
    chosen = arrays[0]
    for k in range(1, len(arrays)):
        chosen = jnp.where(index == k, arrays[k], chosen)
    return chosen


def shards(amplitudes, integrals, bare_terms, pattern, block_order, occ_gap, virt_gap):
    rows_local, columns = amplitudes.shape
    depth, columns_local = integrals.shape
    rows_out, columns_out = bare_terms.shape
    wide_count = lax.axis_size("wide")
    narrow_count = lax.axis_size("narrow")
    chips = wide_count // CORES
    wide = lax.axis_index("wide")
    z = lax.axis_index("narrow")
    chip = wide // CORES
    core = wide % CORES
    part = rows_local // CHUNKS
    group = chips // narrow_count

    def across(value, mask):
        return lax.ppermute(value, "wide", [(w, w ^ mask) for w in range(wide_count)])

    def across_chips(value, mask):
        return across(value, mask * CORES)

    def along(value, mask):
        return lax.ppermute(value, "narrow", [(n, n ^ mask) for n in range(narrow_count)])

    place = jnp.stack([chip, core, z])
    own = split(integrals)
    other = split(across(integrals, 1))

    def spread(piece):
        def slice_for(n):
            return lax.dynamic_slice_in_dim(piece, n * depth, depth, 1)

        blocks = [slice_for(z)]
        for mask in range(1, narrow_count):
            blocks.append(along(slice_for(z ^ mask), mask))
        return blocks

    first = spread(amplitudes[:part])
    rest = spread(amplitudes[part:])

    def gather(chunk, *hold):
        if chunk == 0:
            blocks = first
        else:
            blocks = [block[(chunk - 1) * part : chunk * part] for block in rest]
        mine = jnp.concatenate([choose(z ^ n, blocks) for n in range(narrow_count)], axis=0)
        if hold:
            mine = after(mine, *hold)
        lefts = [mine]
        if chips == 4:
            lefts.append(across_chips(mine, 1))
            lefts.append(across_chips(mine, 2))
            if chunk % 2 == 0:
                lefts.append(across_chips(lefts[1], 2))
            else:
                lefts.append(across_chips(lefts[2], 1))
        else:
            for mask in range(1, chips):
                lefts.append(across_chips(mine, mask))
        return lefts

    arrivals = {}

    def reduce(chunk, partials):
        arrived = [partials[0]]
        for mask in range(1, chips):
            arrived.append(across_chips(partials[mask], mask))

        def share(n):
            return jnp.concatenate(
                [choose(chip ^ (n * group + j), arrived) for j in range(group)], axis=1
            )

        up = down = None
        for step in range(1, narrow_count):
            send_up = share(z + narrow_count - step)
            send_down = share(z - narrow_count + step)
            if step > 1:
                send_up = send_up + up
                send_down = send_down + down
            up = lax.ppermute(send_up, "narrow", [(n, n + 1) for n in range(step)])
            down = lax.ppermute(
                send_down,
                "narrow",
                [(narrow_count - 1 - n, narrow_count - 2 - n) for n in range(step)],
            )
            arrivals[chunk, step] = (up, down)
        return share(z) + (up + down)

    ladders = []
    products = []
    for chunk in range(CHUNKS):
        hold = [products[chunk - 2][0]] if chunk >= 2 else []
        lefts = gather(chunk, *hold)
        if chunk >= 2:
            lefts[0] = after(lefts[0], *arrivals[chunk - 2, 1])
        partials = product(lefts, own, other, place, pattern, block_order)
        products.append(partials)
        ladder = reduce(chunk, partials).reshape(narrow_count, part, -1, CORES, columns_local)
        ladder = jnp.where(core == 0, ladder, ladder[:, :, :, ::-1])
        ladders.append(ladder.reshape(narrow_count, part, columns_out))
    ladder = jnp.stack(ladders, axis=1).reshape(rows_out, columns_out)
    denominator = occ_gap[:, None] + virt_gap[None, :]
    return -(bare_terms + ladder) / denominator


def solution(mesh):
    placed = (
        P(("wide", "narrow"), None),
        P("narrow", "wide"),
        P("wide", "narrow"),
        P(),
        P(),
        P("wide"),
        P("narrow"),
    )
    return jax.shard_map(
        shards, mesh=mesh, in_specs=placed, out_specs=P("wide", "narrow"), check_vma=False
    )
```

```python
import functools

import jax
import jax.numpy as jnp
from jax import lax
from jax.experimental import pallas as pl
from jax.experimental.pallas import tpu as pltpu
from jax.sharding import PartitionSpec as P

TILE = 128
CHUNKS = 4
CORES = 2
PERIOD = 3.0


def split(whole):
    high = lax.reduce_precision(whole, 8, 7)
    return high.astype(jnp.bfloat16), (whole - high).astype(jnp.bfloat16)


def product_kernel(count, rows, place_ref, pattern_ref, order_ref, *refs):
    inputs = len(refs) - count - 5
    lefts = refs[:inputs]
    factors = refs[inputs : inputs + 4]
    outs = refs[inputs + 4 : inputs + 4 + count]
    left = refs[-1]
    depth = lefts[0].shape[1]
    total = count * rows
    chip, core, z = place_ref[0], place_ref[1], place_ref[2]
    tiles = depth // TILE
    k = 0
    for held in lefts:
        for block in range(held.shape[0] // rows):
            kind = order_ref[(chip ^ k) * CORES + core]
            for t in range(tiles):
                kept = pattern_ref[kind, z * tiles + t].astype(jnp.float32)
                here = slice(t * TILE, (t + 1) * TILE)
                value = held[block * rows : (block + 1) * rows, here] * kept
                high = value.astype(jnp.bfloat16)
                left[k * rows : (k + 1) * rows, here] = high
                left[total + k * rows : total + (k + 1) * rows, here] = (
                    value - high.astype(jnp.float32)
                ).astype(jnp.bfloat16)
            k += 1
    columns = factors[0].shape[1]
    width = min(512, columns)
    for half in range(2):
        high_ref, low_ref = factors[2 * half : 2 * half + 2]
        for j in range(columns // width):
            here = slice(j * width, (j + 1) * width)
            both = jnp.dot(left[...], high_ref[:, here], preferred_element_type=jnp.float32)
            small = jnp.dot(
                left[:total, :], low_ref[:, here], preferred_element_type=jnp.float32
            )
            result = both[:total] + (both[total:] + small)
            there = slice(half * columns + j * width, half * columns + (j + 1) * width)
            for k in range(count):
                outs[k][:, there] = result[k * rows : (k + 1) * rows]


def product(lefts, own, other, place, pattern, block_order):
    rows, depth = lefts[0].shape
    count = sum(held.shape[0] for held in lefts) // rows
    columns = own[0].shape[1]
    total = count * rows
    small = pl.BlockSpec(memory_space=pltpu.SMEM)
    large = pl.BlockSpec(memory_space=pltpu.VMEM)
    return pl.pallas_call(
        functools.partial(product_kernel, count, rows),
        in_specs=[small] * 3 + [large] * (len(lefts) + 4),
        out_specs=[large] * count,
        out_shape=[jax.ShapeDtypeStruct((rows, 2 * columns), jnp.float32)] * count,
        scratch_shapes=[pltpu.VMEM((2 * total, depth), jnp.bfloat16)],
        cost_estimate=pl.CostEstimate(
            flops=6 * total * depth * 2 * columns,
            bytes_accessed=8 * total * depth,
            transcendentals=0,
        ),
        compiler_params=pltpu.CompilerParams(vmem_limit_bytes=16 * 2**20),
        name="product",
    )(place, pattern, block_order, *lefts, *own, *other)


def after(value, *others):
    return lax.optimization_barrier((value, *others))[0]


def choose(index, arrays):
    chosen = arrays[0]
    for k in range(1, len(arrays)):
        chosen = jnp.where(index == k, arrays[k], chosen)
    return chosen


def shards(amplitudes, integrals, bare_terms, pattern, block_order, occ_gap, virt_gap):
    rows_local, columns = amplitudes.shape
    depth, columns_local = integrals.shape
    rows_out, columns_out = bare_terms.shape
    wide_count = lax.axis_size("wide")
    narrow_count = lax.axis_size("narrow")
    chips = wide_count // CORES
    wide = lax.axis_index("wide")
    z = lax.axis_index("narrow")
    chip = wide // CORES
    core = wide % CORES
    part = rows_local // CHUNKS
    group = chips // narrow_count

    def across(value, mask):
        return lax.ppermute(value, "wide", [(w, w ^ mask) for w in range(wide_count)])

    def across_chips(value, mask):
        return across(value, mask * CORES)

    def along(value, mask):
        return lax.ppermute(value, "narrow", [(n, n ^ mask) for n in range(narrow_count)])

    place = jnp.stack([chip, core, z])
    own = split(integrals)
    other = split(across(integrals, 1))

    def spread(piece):
        def slice_for(n):
            return lax.dynamic_slice_in_dim(piece, n * depth, depth, 1)

        blocks = [slice_for(z)]
        for mask in range(1, narrow_count):
            blocks.append(along(slice_for(z ^ mask), mask))
        return blocks

    first = spread(amplitudes[:part])
    rest = spread(amplitudes[part:])

    last = []

    def ordered(value):
        if last:
            value = after(value, last[-1])
        last.append(value)
        return value

    chip_bits = [1 << b for b in range(chips.bit_length() - 1)]
    narrow_bits = [1 << b for b in range(narrow_count.bit_length() - 1)]
    held = {}
    state = {}

    def gather_step(chunk, number):
        if number == 0:
            if chunk == 0:
                blocks = first
            else:
                blocks = [block[(chunk - 1) * part : chunk * part] for block in rest]
            mine = jnp.concatenate([choose(z ^ n, blocks) for n in range(narrow_count)], axis=0)
            held[chunk] = [mine]
        if number < len(chip_bits):
            send = ordered(jnp.concatenate(held[chunk], axis=0))
            held[chunk].append(across_chips(send, chip_bits[number]))

    def multiply(chunk):
        lefts = held[chunk]
        lefts[0] = ordered(lefts[0])
        partials = product(lefts, own, other, place, pattern, block_order)
        state[chunk] = {(k, 0): block for k, block in enumerate(partials)}

    def exchange_step(chunk, bit):
        now = state[chunk]
        keys = [key for key in now if key[0] & bit]
        send = ordered(jnp.concatenate([now[key] for key in keys], axis=0))
        arrived = across_chips(send, bit)
        rows = send.shape[0] // len(keys)
        state[chunk] = {key: now[key] for key in now if not key[0] & bit}
        for place_in, (r, s) in enumerate(keys):
            state[chunk][r ^ bit, s | bit] = arrived[place_in * rows : (place_in + 1) * rows]

    def reduce_step(chunk, bit, narrow_bit):
        now = state[chunk]
        same = ((chip // bit) & 1) == ((z // narrow_bit) & 1)
        keys = [key for key in now if not key[1] & bit]
        pairs = [(now[r, s], now[r, s | bit]) for r, s in keys]
        send = ordered(
            jnp.concatenate([jnp.where(same, theirs, mine) for mine, theirs in pairs], axis=0)
        )
        arrived = along(send, narrow_bit)
        rows = send.shape[0] // len(keys)
        state[chunk] = {}
        for place_in, (key, (mine, theirs)) in enumerate(zip(keys, pairs)):
            part_in = arrived[place_in * rows : (place_in + 1) * rows]
            state[chunk][key] = jnp.where(same, mine, theirs) + part_in

    def finish(chunk):
        blocks = [state[chunk][0, s] for s in range(group)]
        ladder = jnp.concatenate([choose((chip % group) ^ j, blocks) for j in range(group)], axis=1)
        ladder = ladder.reshape(narrow_count, part, group, CORES, columns_local)
        ladder = jnp.where(core == 0, ladder, ladder[:, :, :, ::-1])
        return ladder.reshape(narrow_count, part, columns_out)

    stages = []
    clock = 0.0
    for number in range(max(1, len(chip_bits))):
        stages.append((clock, functools.partial(gather_step, number=number)))
        clock += 2.0**number
    stages.append((clock + 0.8, multiply))
    for bit in chip_bits:
        if bit < group:
            stages.append((clock + 0.8, functools.partial(exchange_step, bit=bit)))
            clock += 2.0
    clock += 0.8
    length = 2.0
    for narrow_bit in narrow_bits:
        bit = group * narrow_bit
        stages.append((clock, functools.partial(exchange_step, bit=bit)))
        clock += length + 0.2
        stages.append((clock, functools.partial(reduce_step, bit=bit, narrow_bit=narrow_bit)))
        clock += length + 0.2
        length /= 2.0

    order = sorted(
        (start + PERIOD * chunk, number, chunk)
        for chunk in range(CHUNKS)
        for number, (start, _) in enumerate(stages)
    )
    for _, number, chunk in order:
        stages[number][1](chunk)
    ladder = jnp.stack([finish(chunk) for chunk in range(CHUNKS)], axis=1)
    ladder = ladder.reshape(rows_out, columns_out)
    denominator = occ_gap[:, None] + virt_gap[None, :]
    return -(bare_terms + ladder) / denominator


def solution(mesh):
    placed = (
        P(("wide", "narrow"), None),
        P("narrow", "wide"),
        P("wide", "narrow"),
        P(),
        P(),
        P("wide"),
        P("narrow"),
    )
    return jax.shard_map(
        shards, mesh=mesh, in_specs=placed, out_specs=P("wide", "narrow"), check_vma=False
    )
```

```python
import functools

import jax
import jax.numpy as jnp
from jax import lax
from jax.experimental import pallas as pl
from jax.experimental.pallas import tpu as pltpu
from jax.sharding import PartitionSpec as P

TILE = 128
CHUNKS = 4
CORES = 2
GROUPS = ((0,), (1,), (2, 3))
UNITS = ((0, (0,)), (0, (1,)), (1, (0, 1)), (2, (0, 1)), (3, (0,)), (3, (1,)))
LATENCY = 0.5

SMEM = pl.BlockSpec(memory_space=pltpu.SMEM)
VMEM = pl.BlockSpec(memory_space=pltpu.VMEM)
ANY = pl.BlockSpec(memory_space=pl.ANY)


def after(value, *others):
    return lax.optimization_barrier((value, *others))[0]


def cut_kernel(count, bounds, place_ref, whole_ref, *outs):
    z = place_ref[2]
    depth = outs[0].shape[1]
    for g, (low, high) in enumerate(bounds):
        for m in range(count):
            start = pl.multiple_of((z ^ m) * depth, depth)
            outs[g * count + m][...] = whole_ref[low:high, pl.ds(start, depth)]


def cut(whole, count, depth, part, place):
    bounds = [(group[0] * part, (group[-1] + 1) * part) for group in GROUPS]
    shapes = [
        jax.ShapeDtypeStruct((high - low, depth), whole.dtype)
        for low, high in bounds
        for _ in range(count)
    ]
    outs = pl.pallas_call(
        functools.partial(cut_kernel, count, bounds),
        in_specs=[SMEM, VMEM],
        out_specs=[VMEM] * len(shapes),
        out_shape=shapes,
        cost_estimate=pl.CostEstimate(flops=0, bytes_accessed=4 * whole.size, transcendentals=0),
        name="cut",
    )(place, whole)
    return [outs[g * count : (g + 1) * count] for g in range(len(bounds))]


def pack_kernel(count, part, *refs):
    for c, out in enumerate(refs[count:]):
        for m in range(count):
            out[m * part : (m + 1) * part, :] = refs[m][c * part : (c + 1) * part, :]


def pack(blocks, part):
    count = len(blocks)
    rows, depth = blocks[0].shape
    shape = jax.ShapeDtypeStruct((count * part, depth), blocks[0].dtype)
    return pl.pallas_call(
        functools.partial(pack_kernel, count, part),
        in_specs=[VMEM] * count,
        out_specs=[VMEM] * (rows // part),
        out_shape=[shape] * (rows // part),
        cost_estimate=pl.CostEstimate(flops=0, bytes_accessed=rows * depth, transcendentals=0),
        name="pack",
    )(*blocks)


def split_kernel(step, whole_ref, high_ref, low_ref, buffer, sems):
    count = whole_ref.shape[0] // step

    def copy(i):
        return pltpu.make_async_copy(
            whole_ref.at[pl.ds(i * step, step)], buffer.at[i % 2], sems.at[i % 2]
        )

    copy(0).start()
    for i in range(count):
        if i + 1 < count:
            copy(i + 1).start()
        copy(i).wait()
        whole = buffer[i % 2]
        high = whole.astype(jnp.bfloat16)
        here = slice(i * step, (i + 1) * step)
        high_ref[here, :] = high
        low_ref[here, :] = (whole - high.astype(jnp.float32)).astype(jnp.bfloat16)


def split(whole):
    rows, columns = whole.shape
    step = min(256, rows)
    half = jax.ShapeDtypeStruct((rows, columns), jnp.bfloat16)
    return pl.pallas_call(
        functools.partial(split_kernel, step),
        in_specs=[ANY],
        out_specs=[VMEM, VMEM],
        out_shape=[half, half],
        scratch_shapes=[
            pltpu.VMEM((2, step, columns), jnp.float32),
            pltpu.SemaphoreType.DMA((2,)),
        ],
        cost_estimate=pl.CostEstimate(
            flops=rows * columns, bytes_accessed=4 * rows * columns, transcendentals=0
        ),
        compiler_params=pltpu.CompilerParams(vmem_limit_bytes=8 * 2**20),
        name="split",
    )(whole)


def product_kernel(count, rows, layout, halves, place_ref, pattern_ref, order_ref, *refs):
    lefts = refs[: len(layout)]
    factors = refs[len(layout) : len(layout) + 2 * halves]
    outs = refs[len(layout) + 2 * halves : -1]
    left = refs[-1]
    depth = lefts[0].shape[1]
    total = count * rows
    chip, core, z = place_ref[0], place_ref[1], place_ref[2]
    tiles = depth // TILE
    for held, pieces in zip(lefts, layout):
        start = 0
        for k, first, size in pieces:
            kind = order_ref[(chip ^ k) * CORES + core]
            high_rows = slice(k * rows + first, k * rows + first + size)
            low_rows = slice(total + k * rows + first, total + k * rows + first + size)
            for t in range(tiles):
                kept = pattern_ref[kind, z * tiles + t].astype(jnp.float32)
                here = slice(t * TILE, (t + 1) * TILE)
                value = held[start : start + size, here] * kept
                high = value.astype(jnp.bfloat16)
                left[high_rows, here] = high
                left[low_rows, here] = (value - high.astype(jnp.float32)).astype(jnp.bfloat16)
            start += size
    columns = factors[0].shape[1]
    width = min(512, columns)
    for half in range(halves):
        high_ref, low_ref = factors[2 * half : 2 * half + 2]
        for j in range(columns // width):
            here = slice(j * width, (j + 1) * width)
            both = jnp.dot(left[...], high_ref[:, here], preferred_element_type=jnp.float32)
            small = jnp.dot(
                left[:total, :], low_ref[:, here], preferred_element_type=jnp.float32
            )
            result = both[:total] + (both[total:] + small)
            there = slice(half * columns + j * width, half * columns + (j + 1) * width)
            for k in range(count):
                outs[k][:, there] = result[k * rows : (k + 1) * rows]


def product(lefts, layout, factors, place, pattern, block_order):
    rows, depth = lefts[0].shape
    count = sum(held.shape[0] for held in lefts) // rows
    halves = len(factors)
    columns = factors[0][0].shape[1]
    total = count * rows
    return pl.pallas_call(
        functools.partial(product_kernel, count, rows, layout, halves),
        in_specs=[SMEM] * 3 + [VMEM] * (len(lefts) + 2 * halves),
        out_specs=[VMEM] * count,
        out_shape=[jax.ShapeDtypeStruct((rows, halves * columns), jnp.float32)] * count,
        scratch_shapes=[pltpu.VMEM((2 * total, depth), jnp.bfloat16)],
        cost_estimate=pl.CostEstimate(
            flops=6 * total * depth * halves * columns,
            bytes_accessed=8 * total * depth,
            transcendentals=0,
        ),
        compiler_params=pltpu.CompilerParams(vmem_limit_bytes=16 * 2**20),
        name="product",
    )(place, pattern, block_order, *lefts, *[part for pair in factors for part in pair])


def finish_kernel(spec, group, count, part, width, place_ref, bare_ref, occ_ref, virt_ref, *refs):
    out_ref = refs[-1]
    chip, core, z = place_ref[0], place_ref[1], place_ref[2]
    rows_local = CHUNKS * part
    for number, (chunk, halves, s) in enumerate(spec):
        kept, arrived = refs[2 * number], refs[2 * number + 1]
        for position, half in enumerate(halves):
            column = (((chip % group) ^ s) * CORES + (half ^ core)) * width
            columns = pl.ds(pl.multiple_of(column, width), width)
            here = slice(position * width, (position + 1) * width)
            for m in range(count):
                rows = pl.ds(pl.multiple_of((z ^ m) * rows_local + chunk * part, part), part)
                block = slice(m * part, (m + 1) * part)
                ladder = kept[block, here] + arrived[block, here]
                gap = occ_ref[rows, :] + virt_ref[:, columns]
                out_ref[rows, columns] = -(bare_ref[rows, columns] + ladder) / gap


def finish(spec, pairs, group, count, part, width, place, bare, occ, virt):
    return pl.pallas_call(
        functools.partial(finish_kernel, spec, group, count, part, width),
        in_specs=[SMEM] + [VMEM] * (3 + 2 * len(pairs)),
        out_specs=VMEM,
        out_shape=jax.ShapeDtypeStruct(bare.shape, bare.dtype),
        cost_estimate=pl.CostEstimate(
            flops=5 * bare.size, bytes_accessed=8 * bare.size, transcendentals=0
        ),
        compiler_params=pltpu.CompilerParams(vmem_limit_bytes=8 * 2**20),
        name="finish",
    )(place, bare, occ[:, None], virt[None, :], *[part_in for pair in pairs for part_in in pair])


def event_order(events):
    free = {}
    done = {}
    order = []
    waiting = dict(events)
    while waiting:
        best = None
        for rank, (name, (needs, uses, length)) in enumerate(waiting.items()):
            if any(need not in done for need in needs):
                continue
            start = max([done[need] for need in needs] + [free.get(r, 0.0) for r, _ in uses] + [0.0])
            if best is None or start < best[0] - 1e-9:
                best = (start, name)
        start, name = best
        needs, uses, length = waiting.pop(name)
        for resource, busy in uses:
            free[resource] = start + busy
        done[name] = start + length
        order.append(name)
    return order


def shards(amplitudes, integrals, bare_terms, pattern, block_order, occ_gap, virt_gap):
    rows_local, columns = amplitudes.shape
    depth, columns_local = integrals.shape
    wide_count = lax.axis_size("wide")
    narrow_count = lax.axis_size("narrow")
    chips = wide_count // CORES
    wide = lax.axis_index("wide")
    z = lax.axis_index("narrow")
    chip = wide // CORES
    core = wide % CORES
    part = rows_local // CHUNKS
    rows = narrow_count * part
    group = chips // narrow_count
    place = jnp.stack([chip, core, z]).astype(jnp.int32)
    chip_bits = [1 << b for b in range(chips.bit_length() - 1)]
    narrow_bits = [1 << b for b in range(narrow_count.bit_length() - 1)]
    lane = {bit: "x" if n < len(chip_bits) // 2 else "y" for n, bit in enumerate(chip_bits)}

    def across(value, mask):
        return lax.ppermute(value, "wide", [(w, w ^ mask) for w in range(wide_count)])

    def across_chips(value, mask):
        return across(value, mask * CORES)

    def along(value, mask):
        return lax.ppermute(value, "narrow", [(n, n ^ mask) for n in range(narrow_count)])

    last = []

    def ordered(value):
        if last:
            value = after(value, last[-1])
        last.append(value)
        return value

    swapped = across(integrals, 1)
    pieces = cut(amplitudes, narrow_count, depth, part, place)
    spread = {}
    mine = {}
    held = {}
    layouts = {}
    factors = {}
    state = {}

    def spread_step(g):
        blocks = [pieces[g][0]]
        for mask in range(1, narrow_count):
            blocks.append(along(ordered(pieces[g][mask]), mask))
        spread[g] = blocks

    def gather_step(chunk, number):
        g = [n for n, group_of in enumerate(GROUPS) if chunk in group_of][0]
        if number == 0:
            if GROUPS[g][0] == chunk:
                for c, packed in zip(GROUPS[g], pack(spread[g], part)):
                    mine[c] = packed
            held[chunk] = [mine[chunk]]
            layouts[chunk] = [[(0, 0, rows)]]
        direct = chunk == 0 and chips == 4
        if direct and number == 0:
            send = ordered(mine[chunk])
            held[chunk] += [across_chips(send, 1), across_chips(send, 2)]
            layouts[chunk] += [[(1, 0, rows)], [(2, 0, rows)]]
        elif direct:
            near, far = held[chunk][1], held[chunk][2]
            first = across_chips(ordered(near[: rows // 2]), 2)
            second = across_chips(ordered(far[rows // 2 :]), 1)
            held[chunk] += [first, second]
            layouts[chunk] += [[(3, 0, rows // 2)], [(3, rows // 2, rows // 2)]]
        else:
            bit = chip_bits[number]
            send = ordered(jnp.concatenate(held[chunk], axis=0))
            held[chunk].append(across_chips(send, bit))
            layouts[chunk].append([(k | bit, 0, rows) for k in range(bit)])

    def split_step(half):
        factors[half] = split(ordered(integrals if half == 0 else swapped))

    def multiply(unit):
        chunk, halves = UNITS[unit]
        lefts = list(held[chunk])
        lefts[0] = ordered(lefts[0])
        partials = product(
            lefts, layouts[chunk], [factors[half] for half in halves], place, pattern, block_order
        )
        state[unit] = {(k, 0): block for k, block in enumerate(partials)}

    def exchange_step(unit, bit):
        now = state[unit]
        keys = [key for key in now if key[0] & bit]
        send = ordered(jnp.concatenate([now[key] for key in keys], axis=0))
        arrived = across_chips(send, bit)
        state[unit] = {key: now[key] for key in now if not key[0] & bit}
        for n, (r, s) in enumerate(keys):
            state[unit][r ^ bit, s | bit] = arrived[n * rows : (n + 1) * rows]

    def reduce_step(unit, bit, narrow_bit):
        now = state[unit]
        same = ((chip // bit) & 1) == ((z // narrow_bit) & 1)
        keys = [key for key in now if not key[1] & bit]
        pairs = [(now[r, s], now[r, s | bit]) for r, s in keys]
        leaving = jnp.concatenate([jnp.where(same, b, a) for a, b in pairs], axis=0)
        width = leaving.shape[1]
        leaving = leaving.reshape(-1, 2, narrow_bit * part, width)[:, ::-1].reshape(-1, width)
        arrived = along(ordered(leaving), narrow_bit)
        state[unit] = {}
        for n, (key, (a, b)) in enumerate(zip(keys, pairs)):
            kept = jnp.where(same, a, b)
            came = arrived[n * rows : (n + 1) * rows]
            state[unit][key] = (kept, came) if narrow_bit == narrow_bits[-1] else kept + came

    events = {}
    actions = {}

    def event(name, action, needs, uses):
        length = max(busy for _, busy in uses)
        on_core = all(resource == "core" for resource, _ in uses)
        events[name] = (needs, uses, length if on_core else length + LATENCY)
        actions[name] = action

    for g, chunks in enumerate(GROUPS):
        event(
            ("spread", g),
            functools.partial(spread_step, g),
            [],
            [("mid", 1.0 * len(chunks)), ("end", 0.75 * len(chunks)), ("core", 0.7)],
        )
    for half in range(2):
        needs = [("gather", 0, 0)] if half == 0 else [("multiply", 0)]
        event(("split", half), functools.partial(split_step, half), needs, [("core", 0.8)])
    for unit, (chunk, halves) in enumerate(UNITS):
        if unit == 0 or UNITS[unit - 1][0] != chunk:
            for number, bit in enumerate(chip_bits):
                g = [n for n, group_of in enumerate(GROUPS) if chunk in group_of][0]
                needs = [("gather", chunk, number - 1)] if number else [("spread", g)]
                uses = [(lane[bit], 1.0 * bit)]
                if chunk == 0 and chips == 4:
                    uses = [("x", 1.0 / bit), ("y", 1.0 / bit)]
                event(
                    ("gather", chunk, number),
                    functools.partial(gather_step, chunk, number),
                    needs,
                    uses,
                )
        share = len(halves) / CORES
        before = ("multiply", unit)
        needs = [("gather", chunk, len(chip_bits) - 1)] + [("split", half) for half in halves]
        event(before, functools.partial(multiply, unit), needs, [("core", 0.8 * share)])
        length = 2.0 * share
        for bit in chip_bits:
            if bit < group:
                now = ("exchange", unit, bit)
                event(
                    now, functools.partial(exchange_step, unit, bit), [before], [(lane[bit], length)]
                )
                before = now
        for narrow_bit in narrow_bits:
            bit = group * narrow_bit
            now = ("exchange", unit, bit)
            event(
                now, functools.partial(exchange_step, unit, bit), [before], [(lane[bit], length)]
            )
            before = now
            now = ("reduce", unit, narrow_bit)
            uses = [("end", length), ("mid", length * (0 if narrow_bit == 1 else narrow_bit))]
            event(now, functools.partial(reduce_step, unit, bit, narrow_bit), [before], uses)
            before = now
            length /= 2.0

    for name in event_order(events):
        actions[name]()

    spec = [(*UNITS[unit], s) for unit in range(len(UNITS)) for s in range(group)]
    pairs = [state[unit][0, s] for unit in range(len(UNITS)) for s in range(group)]
    return finish(
        spec,
        pairs,
        group,
        narrow_count,
        part,
        columns_local,
        place,
        bare_terms,
        occ_gap,
        virt_gap,
    )


def solution(mesh):
    placed = (
        P(("wide", "narrow"), None),
        P("narrow", "wide"),
        P("wide", "narrow"),
        P(),
        P(),
        P("wide"),
        P("narrow"),
    )
    return jax.shard_map(
        shards, mesh=mesh, in_specs=placed, out_specs=P("wide", "narrow"), check_vma=False
    )
```

```python
import functools

import jax
import jax.numpy as jnp
from jax import lax
from jax.experimental import pallas as pl
from jax.experimental.pallas import tpu as pltpu
from jax.sharding import PartitionSpec as P

TILE = 128
CHUNKS = 4
CORES = 2
GROUPS = ((0,), (1,), (2, 3))
UNITS = ((0, (0,)), (0, (1,)), (1, (0, 1)), (2, (0, 1)), (3, (0,)), (3, (1,)))
LATENCY = 0.5

SMEM = pl.BlockSpec(memory_space=pltpu.SMEM)
VMEM = pl.BlockSpec(memory_space=pltpu.VMEM)
ANY = pl.BlockSpec(memory_space=pl.ANY)


def after(value, *others):
    return lax.optimization_barrier((value, *others))[0]


def cut_kernel(count, bounds, place_ref, whole_ref, *outs):
    z = place_ref[2]
    depth = outs[0].shape[1]
    for g, (low, high) in enumerate(bounds):
        for m in range(count):
            start = pl.multiple_of((z ^ m) * depth, depth)
            outs[g * count + m][...] = whole_ref[low:high, pl.ds(start, depth)]


def cut(whole, count, depth, part, place):
    bounds = [(group[0] * part, (group[-1] + 1) * part) for group in GROUPS]
    shapes = [
        jax.ShapeDtypeStruct((high - low, depth), whole.dtype)
        for low, high in bounds
        for _ in range(count)
    ]
    outs = pl.pallas_call(
        functools.partial(cut_kernel, count, bounds),
        in_specs=[SMEM, VMEM],
        out_specs=[VMEM] * len(shapes),
        out_shape=shapes,
        cost_estimate=pl.CostEstimate(flops=0, bytes_accessed=4 * whole.size, transcendentals=0),
        compiler_params=pltpu.CompilerParams(vmem_limit_bytes=2**20),
        name="cut",
    )(place, whole)
    return [outs[g * count : (g + 1) * count] for g in range(len(bounds))]


def pack_kernel(count, part, *refs):
    for c, out in enumerate(refs[count:]):
        for m in range(count):
            out[m * part : (m + 1) * part, :] = refs[m][c * part : (c + 1) * part, :]


def pack(blocks, part):
    count = len(blocks)
    rows, depth = blocks[0].shape
    shape = jax.ShapeDtypeStruct((count * part, depth), blocks[0].dtype)
    return pl.pallas_call(
        functools.partial(pack_kernel, count, part),
        in_specs=[VMEM] * count,
        out_specs=[VMEM] * (rows // part),
        out_shape=[shape] * (rows // part),
        cost_estimate=pl.CostEstimate(flops=0, bytes_accessed=rows * depth, transcendentals=0),
        compiler_params=pltpu.CompilerParams(vmem_limit_bytes=2**20),
        name="pack",
    )(*blocks)


def split_kernel(step, whole_ref, high_ref, low_ref, buffer, sems):
    count = whole_ref.shape[0] // step

    def copy(i):
        return pltpu.make_async_copy(
            whole_ref.at[pl.ds(i * step, step)], buffer.at[i % 2], sems.at[i % 2]
        )

    copy(0).start()
    for i in range(count):
        if i + 1 < count:
            copy(i + 1).start()
        copy(i).wait()
        whole = buffer[i % 2]
        high = whole.astype(jnp.bfloat16)
        here = slice(i * step, (i + 1) * step)
        high_ref[here, :] = high
        low_ref[here, :] = (whole - high.astype(jnp.float32)).astype(jnp.bfloat16)


def split(whole):
    rows, columns = whole.shape
    step = min(256, rows)
    half = jax.ShapeDtypeStruct((rows, columns), jnp.bfloat16)
    return pl.pallas_call(
        functools.partial(split_kernel, step),
        in_specs=[ANY],
        out_specs=[VMEM, VMEM],
        out_shape=[half, half],
        scratch_shapes=[
            pltpu.VMEM((2, step, columns), jnp.float32),
            pltpu.SemaphoreType.DMA((2,)),
        ],
        cost_estimate=pl.CostEstimate(
            flops=rows * columns, bytes_accessed=4 * rows * columns, transcendentals=0
        ),
        compiler_params=pltpu.CompilerParams(vmem_limit_bytes=3 * 2**20),
        name="split",
    )(whole)


def product_kernel(count, rows, layout, halves, place_ref, pattern_ref, order_ref, *refs):
    lefts = refs[: len(layout)]
    factors = refs[len(layout) : len(layout) + 2 * halves]
    outs = refs[len(layout) + 2 * halves : -1]
    left = refs[-1]
    depth = lefts[0].shape[1]
    total = count * rows
    chip, core, z = place_ref[0], place_ref[1], place_ref[2]
    tiles = depth // TILE
    for held, pieces in zip(lefts, layout):
        start = 0
        for k, first, size in pieces:
            kind = order_ref[(chip ^ k) * CORES + core]
            high_rows = slice(k * rows + first, k * rows + first + size)
            low_rows = slice(total + k * rows + first, total + k * rows + first + size)
            for t in range(tiles):
                kept = pattern_ref[kind, z * tiles + t].astype(jnp.float32)
                here = slice(t * TILE, (t + 1) * TILE)
                value = held[start : start + size, here] * kept
                high = value.astype(jnp.bfloat16)
                left[high_rows, here] = high
                left[low_rows, here] = (value - high.astype(jnp.float32)).astype(jnp.bfloat16)
            start += size
    columns = factors[0].shape[1]
    width = min(512, columns)
    for half in range(halves):
        high_ref, low_ref = factors[2 * half : 2 * half + 2]
        for j in range(columns // width):
            here = slice(j * width, (j + 1) * width)
            both = jnp.dot(left[...], high_ref[:, here], preferred_element_type=jnp.float32)
            small = jnp.dot(
                left[:total, :], low_ref[:, here], preferred_element_type=jnp.float32
            )
            result = both[:total] + (both[total:] + small)
            there = slice(half * columns + j * width, half * columns + (j + 1) * width)
            for k in range(count):
                outs[k][:, there] = result[k * rows : (k + 1) * rows]


def product(lefts, layout, factors, place, pattern, block_order):
    rows, depth = lefts[0].shape
    count = sum(held.shape[0] for held in lefts) // rows
    halves = len(factors)
    columns = factors[0][0].shape[1]
    total = count * rows
    return pl.pallas_call(
        functools.partial(product_kernel, count, rows, layout, halves),
        in_specs=[SMEM] * 3 + [VMEM] * (len(lefts) + 2 * halves),
        out_specs=[VMEM] * count,
        out_shape=[jax.ShapeDtypeStruct((rows, halves * columns), jnp.float32)] * count,
        scratch_shapes=[pltpu.VMEM((2 * total, depth), jnp.bfloat16)],
        cost_estimate=pl.CostEstimate(
            flops=6 * total * depth * halves * columns,
            bytes_accessed=8 * total * depth,
            transcendentals=0,
        ),
        compiler_params=pltpu.CompilerParams(vmem_limit_bytes=8 * total * depth + 3 * 2**20),
        name="product",
    )(place, pattern, block_order, *lefts, *[part for pair in factors for part in pair])


def finish_kernel(spec, group, count, part, width, place_ref, bare_ref, occ_ref, virt_ref, *refs):
    out_ref = refs[-1]
    chip, core, z = place_ref[0], place_ref[1], place_ref[2]
    rows_local = CHUNKS * part
    for number, (chunk, halves, s) in enumerate(spec):
        kept, arrived = refs[2 * number], refs[2 * number + 1]
        for position, half in enumerate(halves):
            column = (((chip % group) ^ s) * CORES + (half ^ core)) * width
            columns = pl.ds(pl.multiple_of(column, width), width)
            here = slice(position * width, (position + 1) * width)
            for m in range(count):
                rows = pl.ds(pl.multiple_of((z ^ m) * rows_local + chunk * part, part), part)
                block = slice(m * part, (m + 1) * part)
                ladder = kept[block, here] + arrived[block, here]
                gap = occ_ref[rows, :] + virt_ref[:, columns]
                out_ref[rows, columns] = -(bare_ref[rows, columns] + ladder) / gap


def finish(spec, pairs, group, count, part, width, place, bare, occ, virt):
    return pl.pallas_call(
        functools.partial(finish_kernel, spec, group, count, part, width),
        in_specs=[SMEM] + [VMEM] * (3 + 2 * len(pairs)),
        out_specs=VMEM,
        out_shape=jax.ShapeDtypeStruct(bare.shape, bare.dtype),
        cost_estimate=pl.CostEstimate(
            flops=5 * bare.size, bytes_accessed=8 * bare.size, transcendentals=0
        ),
        compiler_params=pltpu.CompilerParams(vmem_limit_bytes=2 * 2**20),
        name="finish",
    )(place, bare, occ[:, None], virt[None, :], *[part_in for pair in pairs for part_in in pair])


def event_order(events):
    taken = {}
    done = {}
    starts = {}
    for name, (needs, uses, length) in events.items():
        start = max([done[need] for need in needs] + [0.0])
        moved = True
        while moved:
            moved = False
            for resource, busy in uses:
                for low, high in taken.get(resource, ()):
                    if low < start + busy - 1e-6 and start < high - 1e-6:
                        start = high
                        moved = True
        for resource, busy in uses:
            taken.setdefault(resource, []).append((start, start + busy))
        done[name] = start + length
        starts[name] = start
    return sorted(events, key=lambda name: starts[name])


def shards(amplitudes, integrals, bare_terms, pattern, block_order, occ_gap, virt_gap):
    rows_local, columns = amplitudes.shape
    depth, columns_local = integrals.shape
    wide_count = lax.axis_size("wide")
    narrow_count = lax.axis_size("narrow")
    chips = wide_count // CORES
    wide = lax.axis_index("wide")
    z = lax.axis_index("narrow")
    chip = wide // CORES
    core = wide % CORES
    part = rows_local // CHUNKS
    rows = narrow_count * part
    group = chips // narrow_count
    place = jnp.stack([chip, core, z]).astype(jnp.int32)
    chip_bits = [1 << b for b in range(chips.bit_length() - 1)]
    narrow_bits = [1 << b for b in range(narrow_count.bit_length() - 1)]
    lane = {bit: "x" if n < len(chip_bits) // 2 else "y" for n, bit in enumerate(chip_bits)}

    def across(value, mask):
        return lax.ppermute(value, "wide", [(w, w ^ mask) for w in range(wide_count)])

    def across_chips(value, mask):
        return across(value, mask * CORES)

    def along(value, mask):
        return lax.ppermute(value, "narrow", [(n, n ^ mask) for n in range(narrow_count)])

    last = []

    def ordered(value):
        if last:
            value = after(value, last[-1])
        last.append(value)
        return value

    swapped = across(integrals, 1)
    pieces = cut(amplitudes, narrow_count, depth, part, place)
    spread = {}
    mine = {}
    held = {}
    layouts = {}
    factors = {}
    state = {}

    def spread_step(g):
        blocks = [pieces[g][0]]
        for mask in range(1, narrow_count):
            blocks.append(along(ordered(pieces[g][mask]), mask))
        spread[g] = blocks

    def gather_step(chunk, number):
        g = [n for n, group_of in enumerate(GROUPS) if chunk in group_of][0]
        if number == 0:
            if GROUPS[g][0] == chunk:
                for c, packed in zip(GROUPS[g], pack(spread[g], part)):
                    mine[c] = packed
            held[chunk] = [mine[chunk]]
            layouts[chunk] = [[(0, 0, rows)]]
        direct = chunk == 0 and chips == 4
        if direct and number == 0:
            send = ordered(mine[chunk])
            held[chunk] += [across_chips(send, 1), across_chips(send, 2)]
            layouts[chunk] += [[(1, 0, rows)], [(2, 0, rows)]]
        elif direct:
            near, far = held[chunk][1], held[chunk][2]
            first = across_chips(ordered(near[: rows // 2]), 2)
            second = across_chips(ordered(far[rows // 2 :]), 1)
            held[chunk] += [first, second]
            layouts[chunk] += [[(3, 0, rows // 2)], [(3, rows // 2, rows // 2)]]
        else:
            bit = chip_bits[number]
            send = ordered(jnp.concatenate(held[chunk], axis=0))
            held[chunk].append(across_chips(send, bit))
            layouts[chunk].append([(k | bit, 0, rows) for k in range(bit)])

    def split_step(half):
        factors[half] = split(ordered(integrals if half == 0 else swapped))

    def multiply(unit):
        chunk, halves = UNITS[unit]
        lefts = list(held[chunk])
        lefts[0] = ordered(lefts[0])
        partials = product(
            lefts, layouts[chunk], [factors[half] for half in halves], place, pattern, block_order
        )
        state[unit] = {(k, 0): block for k, block in enumerate(partials)}

    def exchange_step(unit, bit):
        now = state[unit]
        keys = [key for key in now if key[0] & bit]
        send = ordered(jnp.concatenate([now[key] for key in keys], axis=0))
        arrived = across_chips(send, bit)
        state[unit] = {key: now[key] for key in now if not key[0] & bit}
        for n, (r, s) in enumerate(keys):
            state[unit][r ^ bit, s | bit] = arrived[n * rows : (n + 1) * rows]

    def reduce_step(unit, bit, narrow_bit):
        now = state[unit]
        same = ((chip // bit) & 1) == ((z // narrow_bit) & 1)
        keys = [key for key in now if not key[1] & bit]
        pairs = [(now[r, s], now[r, s | bit]) for r, s in keys]
        leaving = jnp.concatenate([jnp.where(same, b, a) for a, b in pairs], axis=0)
        size = narrow_bit * part
        leaving = jnp.concatenate(
            [leaving[n * size : (n + 1) * size] for m in range(0, leaving.shape[0] // size, 2) for n in (m + 1, m)],
            axis=0,
        )
        arrived = along(ordered(leaving), narrow_bit)
        state[unit] = {}
        for n, (key, (a, b)) in enumerate(zip(keys, pairs)):
            kept = jnp.where(same, a, b)
            came = arrived[n * rows : (n + 1) * rows]
            state[unit][key] = (kept, came) if narrow_bit == narrow_bits[-1] else kept + came

    events = {}
    actions = {}

    def event(name, action, needs, uses):
        length = max(busy for _, busy in uses)
        on_core = all(resource == "core" for resource, _ in uses)
        events[name] = (needs, uses, length if on_core else length + LATENCY)
        actions[name] = action

    for g, chunks in enumerate(GROUPS):
        event(
            ("spread", g),
            functools.partial(spread_step, g),
            [],
            [("mid", 1.0 * len(chunks)), ("end", 0.75 * len(chunks)), ("core", 0.7)],
        )
    for unit, (chunk, halves) in enumerate(UNITS):
        if unit == 0 or UNITS[unit - 1][0] != chunk:
            for number, bit in enumerate(chip_bits):
                g = [n for n, group_of in enumerate(GROUPS) if chunk in group_of][0]
                needs = [("gather", chunk, number - 1)] if number else [("spread", g)]
                uses = [(lane[bit], 1.0 * bit)]
                if chunk == 0 and chips == 4:
                    uses = [("x", 1.0 / bit), ("y", 1.0 / bit)]
                event(
                    ("gather", chunk, number),
                    functools.partial(gather_step, chunk, number),
                    needs,
                    uses,
                )
        for half in halves:
            if ("split", half) not in events:
                needs = [("multiply", unit - 1)] if unit else [("gather", 0, 0)]
                event(("split", half), functools.partial(split_step, half), needs, [("core", 0.8)])
        share = len(halves) / CORES
        before = ("multiply", unit)
        needs = [("gather", chunk, len(chip_bits) - 1)] + [("split", half) for half in halves]
        event(before, functools.partial(multiply, unit), needs, [("core", 0.8 * share)])
        length = 2.0 * share
        for bit in chip_bits:
            if bit < group:
                now = ("exchange", unit, bit)
                event(
                    now, functools.partial(exchange_step, unit, bit), [before], [(lane[bit], length)]
                )
                before = now
        for narrow_bit in narrow_bits:
            bit = group * narrow_bit
            now = ("exchange", unit, bit)
            event(
                now, functools.partial(exchange_step, unit, bit), [before], [(lane[bit], length)]
            )
            before = now
            now = ("reduce", unit, narrow_bit)
            uses = [("end", length), ("mid", length * (0 if narrow_bit == 1 else narrow_bit))]
            event(now, functools.partial(reduce_step, unit, bit, narrow_bit), [before], uses)
            before = now
            length /= 2.0

    for name in event_order(events):
        actions[name]()

    spec = [(*UNITS[unit], s) for unit in range(len(UNITS)) for s in range(group)]
    pairs = [state[unit][0, s] for unit in range(len(UNITS)) for s in range(group)]
    return finish(
        spec,
        pairs,
        group,
        narrow_count,
        part,
        columns_local,
        place,
        bare_terms,
        occ_gap,
        virt_gap,
    )


def solution(mesh):
    placed = (
        P(("wide", "narrow"), None),
        P("narrow", "wide"),
        P("wide", "narrow"),
        P(),
        P(),
        P("wide"),
        P("narrow"),
    )
    return jax.shard_map(
        shards, mesh=mesh, in_specs=placed, out_specs=P("wide", "narrow"), check_vma=False
    )
```

```python
import functools

import jax
import jax.numpy as jnp
from jax import lax
from jax.experimental import pallas as pl
from jax.experimental.pallas import tpu as pltpu
from jax.sharding import PartitionSpec as P

TILE = 128
CHUNKS = 4
CORES = 2
GROUPS = ((0,), (1,), (2, 3))
UNITS = ((0, (0,)), (0, (1,)), (1, (0, 1)), (2, (0, 1)), (3, (0,)), (3, (1,)))
LATENCY = 0.5
SLACK = 0.3

SMEM = pl.BlockSpec(memory_space=pltpu.SMEM)
VMEM = pl.BlockSpec(memory_space=pltpu.VMEM)
ANY = pl.BlockSpec(memory_space=pl.ANY)
SMALL = pl.CostEstimate(flops=1, bytes_accessed=1, transcendentals=0)


def after(value, *others):
    return lax.optimization_barrier((value, *others))[0]


def cut_kernel(count, bounds, place_ref, whole_ref, *outs):
    z = place_ref[2]
    depth = outs[0].shape[1]
    for g, (low, high) in enumerate(bounds):
        for m in range(count):
            start = pl.multiple_of((z ^ m) * depth, depth)
            outs[g * count + m][...] = whole_ref[low:high, pl.ds(start, depth)]


def cut(whole, count, depth, part, place):
    bounds = [(group[0] * part, (group[-1] + 1) * part) for group in GROUPS]
    shapes = [
        jax.ShapeDtypeStruct((high - low, depth), whole.dtype)
        for low, high in bounds
        for _ in range(count)
    ]
    outs = pl.pallas_call(
        functools.partial(cut_kernel, count, bounds),
        in_specs=[SMEM, VMEM],
        out_specs=[VMEM] * len(shapes),
        out_shape=shapes,
        cost_estimate=SMALL,
        compiler_params=pltpu.CompilerParams(vmem_limit_bytes=2**20),
        name="cut",
    )(place, whole)
    return [outs[g * count : (g + 1) * count] for g in range(len(bounds))]


def pack_kernel(count, part, *refs):
    for c, out in enumerate(refs[count:]):
        for m in range(count):
            out[m * part : (m + 1) * part, :] = refs[m][c * part : (c + 1) * part, :]


def pack(blocks, part):
    count = len(blocks)
    rows, depth = blocks[0].shape
    shape = jax.ShapeDtypeStruct((count * part, depth), blocks[0].dtype)
    return pl.pallas_call(
        functools.partial(pack_kernel, count, part),
        in_specs=[VMEM] * count,
        out_specs=[VMEM] * (rows // part),
        out_shape=[shape] * (rows // part),
        cost_estimate=SMALL,
        compiler_params=pltpu.CompilerParams(vmem_limit_bytes=2**20),
        name="pack",
    )(*blocks)


def split_kernel(step, whole_ref, high_ref, low_ref, buffer, sems):
    count = whole_ref.shape[0] // step

    def copy(i):
        return pltpu.make_async_copy(
            whole_ref.at[pl.ds(i * step, step)], buffer.at[i % 2], sems.at[i % 2]
        )

    copy(0).start()
    for i in range(count):
        if i + 1 < count:
            copy(i + 1).start()
        copy(i).wait()
        whole = buffer[i % 2]
        high = whole.astype(jnp.bfloat16)
        here = slice(i * step, (i + 1) * step)
        high_ref[here, :] = high
        low_ref[here, :] = (whole - high.astype(jnp.float32)).astype(jnp.bfloat16)


def split(whole):
    rows, columns = whole.shape
    step = min(256, rows)
    half = jax.ShapeDtypeStruct((rows, columns), jnp.bfloat16)
    return pl.pallas_call(
        functools.partial(split_kernel, step),
        in_specs=[ANY],
        out_specs=[VMEM, VMEM],
        out_shape=[half, half],
        scratch_shapes=[
            pltpu.VMEM((2, step, columns), jnp.float32),
            pltpu.SemaphoreType.DMA((2,)),
        ],
        cost_estimate=SMALL,
        compiler_params=pltpu.CompilerParams(vmem_limit_bytes=3 * 2**20),
        name="split",
    )(whole)


def product_kernel(count, rows, layout, halves, place_ref, pattern_ref, order_ref, *refs):
    lefts = refs[: len(layout)]
    factors = refs[len(layout) : len(layout) + 2 * halves]
    outs = refs[len(layout) + 2 * halves : -1]
    left = refs[-1]
    depth = lefts[0].shape[1]
    total = count * rows
    chip, core, z = place_ref[0], place_ref[1], place_ref[2]
    tiles = depth // TILE
    for held, pieces in zip(lefts, layout):
        start = 0
        for k, first, size in pieces:
            kind = order_ref[(chip ^ k) * CORES + core]
            high_rows = slice(k * rows + first, k * rows + first + size)
            low_rows = slice(total + k * rows + first, total + k * rows + first + size)
            for t in range(tiles):
                kept = pattern_ref[kind, z * tiles + t].astype(jnp.float32)
                here = slice(t * TILE, (t + 1) * TILE)
                value = held[start : start + size, here] * kept
                high = value.astype(jnp.bfloat16)
                left[high_rows, here] = high
                left[low_rows, here] = (value - high.astype(jnp.float32)).astype(jnp.bfloat16)
            start += size
    columns = factors[0].shape[1]
    width = min(512, columns)
    for half in range(halves):
        high_ref, low_ref = factors[2 * half : 2 * half + 2]
        for j in range(columns // width):
            here = slice(j * width, (j + 1) * width)
            both = jnp.dot(left[...], high_ref[:, here], preferred_element_type=jnp.float32)
            small = jnp.dot(
                left[:total, :], low_ref[:, here], preferred_element_type=jnp.float32
            )
            result = both[:total] + (both[total:] + small)
            there = slice(half * columns + j * width, half * columns + (j + 1) * width)
            for k in range(count):
                outs[k][:, there] = result[k * rows : (k + 1) * rows]


def product(lefts, layout, factors, place, pattern, block_order):
    rows, depth = lefts[0].shape
    count = sum(held.shape[0] for held in lefts) // rows
    halves = len(factors)
    columns = factors[0][0].shape[1]
    total = count * rows
    return pl.pallas_call(
        functools.partial(product_kernel, count, rows, layout, halves),
        in_specs=[SMEM] * 3 + [VMEM] * (len(lefts) + 2 * halves),
        out_specs=[VMEM] * count,
        out_shape=[jax.ShapeDtypeStruct((rows, halves * columns), jnp.float32)] * count,
        scratch_shapes=[pltpu.VMEM((2 * total, depth), jnp.bfloat16)],
        cost_estimate=SMALL,
        compiler_params=pltpu.CompilerParams(vmem_limit_bytes=8 * total * depth + 3 * 2**20),
        name="product",
    )(place, pattern, block_order, *lefts, *[part for pair in factors for part in pair])


def turn_kernel(count, bit, narrow_bit, part, place_ref, *refs):
    mine, theirs = refs[:count], refs[count : 2 * count]
    send, kept = refs[2 * count], refs[2 * count + 1 :]
    same = ((place_ref[0] // bit) & 1) == ((place_ref[2] // narrow_bit) & 1)
    rows = mine[0].shape[0]
    size = narrow_bit * part

    def fill(keep, leave):
        for n in range(count):
            kept[n][...] = keep[n][...]
            for m in range(rows // size):
                source = slice((m ^ 1) * size, ((m ^ 1) + 1) * size)
                send[n * rows + m * size : n * rows + (m + 1) * size, :] = leave[n][source, :]

    @pl.when(same)
    def _():
        fill(mine, theirs)

    @pl.when(jnp.logical_not(same))
    def _():
        fill(theirs, mine)


def turn(pairs, bit, narrow_bit, part, place):
    count = len(pairs)
    rows, width = pairs[0][0].shape
    kept = jax.ShapeDtypeStruct((rows, width), jnp.float32)
    send = jax.ShapeDtypeStruct((count * rows, width), jnp.float32)
    send, *kept = pl.pallas_call(
        functools.partial(turn_kernel, count, bit, narrow_bit, part),
        in_specs=[SMEM] + [VMEM] * (2 * count),
        out_specs=[VMEM] * (1 + count),
        out_shape=[send] + [kept] * count,
        cost_estimate=SMALL,
        compiler_params=pltpu.CompilerParams(vmem_limit_bytes=2**20),
        name="turn",
    )(place, *[a for a, _ in pairs], *[b for _, b in pairs])
    return send, kept


def finish_kernel(spec, group, count, part, width, place_ref, bare_ref, occ_ref, virt_ref, *refs):
    out_ref = refs[-1]
    chip, core, z = place_ref[0], place_ref[1], place_ref[2]
    rows_local = CHUNKS * part
    for number, (chunk, halves, s) in enumerate(spec):
        kept, arrived = refs[2 * number], refs[2 * number + 1]
        for position, half in enumerate(halves):
            column = (((chip % group) ^ s) * CORES + (half ^ core)) * width
            columns = pl.ds(pl.multiple_of(column, width), width)
            here = slice(position * width, (position + 1) * width)
            for m in range(count):
                rows = pl.ds(pl.multiple_of((z ^ m) * rows_local + chunk * part, part), part)
                block = slice(m * part, (m + 1) * part)
                ladder = kept[block, here] + arrived[block, here]
                gap = occ_ref[rows, :] + virt_ref[:, columns]
                out_ref[rows, columns] = -(bare_ref[rows, columns] + ladder) / gap


def finish(spec, pairs, group, count, part, width, place, bare, occ, virt):
    return pl.pallas_call(
        functools.partial(finish_kernel, spec, group, count, part, width),
        in_specs=[SMEM] + [VMEM] * (3 + 2 * len(pairs)),
        out_specs=VMEM,
        out_shape=jax.ShapeDtypeStruct(bare.shape, bare.dtype),
        cost_estimate=SMALL,
        compiler_params=pltpu.CompilerParams(vmem_limit_bytes=2 * 2**20),
        name="finish",
    )(place, bare, occ[:, None], virt[None, :], *[part_in for pair in pairs for part_in in pair])


def event_order(events):
    taken = {}
    done = {}
    starts = {}
    for name, (needs, uses, length) in events.items():
        start = max([done[need] for need in needs] + [0.0])
        moved = True
        while moved:
            moved = False
            for resource, busy in uses:
                for low, high in taken.get(resource, ()):
                    if low < start + busy - SLACK and start < high - 1e-6:
                        start = high
                        moved = True
        for resource, busy in uses:
            taken.setdefault(resource, []).append((start, start + busy))
        done[name] = start + length
        starts[name] = start
    return [(starts[name], done[name], name) for name in sorted(events, key=starts.get)]


def shards(amplitudes, integrals, bare_terms, pattern, block_order, occ_gap, virt_gap):
    rows_local, columns = amplitudes.shape
    depth, columns_local = integrals.shape
    wide_count = lax.axis_size("wide")
    narrow_count = lax.axis_size("narrow")
    chips = wide_count // CORES
    wide = lax.axis_index("wide")
    z = lax.axis_index("narrow")
    chip = wide // CORES
    core = wide % CORES
    part = rows_local // CHUNKS
    rows = narrow_count * part
    group = chips // narrow_count
    place = jnp.stack([chip, core, z]).astype(jnp.int32)
    chip_bits = [1 << b for b in range(chips.bit_length() - 1)]
    narrow_bits = [1 << b for b in range(narrow_count.bit_length() - 1)]
    lane = {bit: "x" if n < len(chip_bits) // 2 else "y" for n, bit in enumerate(chip_bits)}

    def across(value, mask):
        return lax.ppermute(value, "wide", [(w, w ^ mask) for w in range(wide_count)])

    def across_chips(value, mask):
        return across(value, mask * CORES)

    def along(value, mask):
        return lax.ppermute(value, "narrow", [(n, n ^ mask) for n in range(narrow_count)])

    last = []
    landed = []

    def ordered(value):
        if last:
            value = after(value, *last, *landed)
        last[:] = [value]
        landed.clear()
        return value

    swapped = across(integrals, 1)
    pieces = cut(amplitudes, narrow_count, depth, part, place)
    spread = {}
    mine = {}
    held = {}
    layouts = {}
    factors = {}
    state = {}

    def spread_step(g):
        blocks = [pieces[g][0]]
        for mask in range(1, narrow_count):
            blocks.append(along(ordered(pieces[g][mask]), mask))
        spread[g] = blocks

    def gather_step(chunk, number):
        g = [n for n, group_of in enumerate(GROUPS) if chunk in group_of][0]
        if number == 0:
            if GROUPS[g][0] == chunk:
                for c, packed in zip(GROUPS[g], pack(spread[g], part)):
                    mine[c] = packed
            held[chunk] = [mine[chunk]]
            layouts[chunk] = [[(0, 0, rows)]]
        direct = chunk == 0 and chips == 4
        if direct and number == 0:
            send = ordered(mine[chunk])
            held[chunk] += [across_chips(send, 1), across_chips(send, 2)]
            layouts[chunk] += [[(1, 0, rows)], [(2, 0, rows)]]
        elif direct:
            near, far = held[chunk][1], held[chunk][2]
            first = across_chips(ordered(near[: rows // 2]), 2)
            second = across_chips(ordered(far[rows // 2 :]), 1)
            held[chunk] += [first, second]
            layouts[chunk] += [[(3, 0, rows // 2)], [(3, rows // 2, rows // 2)]]
        else:
            bit = chip_bits[number]
            send = ordered(jnp.concatenate(held[chunk], axis=0))
            held[chunk].append(across_chips(send, bit))
            layouts[chunk].append([(k | bit, 0, rows) for k in range(bit)])

    def split_step(half):
        factors[half] = split(ordered(integrals if half == 0 else swapped))

    def multiply(unit):
        chunk, halves = UNITS[unit]
        lefts = list(held[chunk])
        lefts[0] = ordered(lefts[0])
        partials = product(
            lefts, layouts[chunk], [factors[half] for half in halves], place, pattern, block_order
        )
        state[unit] = {(k, 0): block for k, block in enumerate(partials)}

    def exchange_step(unit, bit):
        now = state[unit]
        keys = [key for key in now if key[0] & bit]
        send = ordered(jnp.concatenate([now[key] for key in keys], axis=0))
        arrived = across_chips(send, bit)
        state[unit] = {key: now[key] for key in now if not key[0] & bit}
        for n, (r, s) in enumerate(keys):
            state[unit][r ^ bit, s | bit] = arrived[n * rows : (n + 1) * rows]

    def reduce_step(unit, bit, narrow_bit):
        now = state[unit]
        keys = [key for key in now if not key[1] & bit]
        pairs = [(now[r, s], now[r, s | bit]) for r, s in keys]
        leaving, kept = turn(pairs, bit, narrow_bit, part, place)
        arrived = along(ordered(leaving), narrow_bit)
        state[unit] = {}
        for n, key in enumerate(keys):
            came = arrived[n * rows : (n + 1) * rows]
            final = narrow_bit == narrow_bits[-1]
            state[unit][key] = (kept[n], came) if final else kept[n] + came

    events = {}
    actions = {}

    def event(name, action, needs, uses):
        length = max(busy for _, busy in uses)
        on_core = all(resource == "core" for resource, _ in uses)
        events[name] = (needs, uses, length if on_core else length + LATENCY)
        actions[name] = action

    for g, chunks in enumerate(GROUPS):
        event(
            ("spread", g),
            functools.partial(spread_step, g),
            [],
            [("mid", 1.0 * len(chunks)), ("end", 0.75 * len(chunks)), ("core", 0.7)],
        )
    for unit, (chunk, halves) in enumerate(UNITS):
        if unit == 0 or UNITS[unit - 1][0] != chunk:
            for number, bit in enumerate(chip_bits):
                g = [n for n, group_of in enumerate(GROUPS) if chunk in group_of][0]
                needs = [("gather", chunk, number - 1)] if number else [("spread", g)]
                uses = [(lane[bit], 1.0 * bit)]
                if chunk == 0 and chips == 4:
                    uses = [("x", 1.0 / bit), ("y", 1.0 / bit)]
                event(
                    ("gather", chunk, number),
                    functools.partial(gather_step, chunk, number),
                    needs,
                    uses,
                )
        for half in halves:
            if ("split", half) not in events:
                needs = [("multiply", unit - 1)] if unit else [("gather", 0, 0)]
                event(("split", half), functools.partial(split_step, half), needs, [("core", 0.8)])
        share = len(halves) / CORES
        before = ("multiply", unit)
        needs = [("gather", chunk, len(chip_bits) - 1)] + [("split", half) for half in halves]
        event(before, functools.partial(multiply, unit), needs, [("core", 0.8 * share)])
        length = 2.0 * share
        for bit in chip_bits:
            if bit < group:
                now = ("exchange", unit, bit)
                event(
                    now, functools.partial(exchange_step, unit, bit), [before], [(lane[bit], length)]
                )
                before = now
        for narrow_bit in narrow_bits:
            bit = group * narrow_bit
            now = ("exchange", unit, bit)
            event(
                now, functools.partial(exchange_step, unit, bit), [before], [(lane[bit], length)]
            )
            before = now
            now = ("reduce", unit, narrow_bit)
            uses = [("end", length), ("mid", length * (0 if narrow_bit == 1 else narrow_bit))]
            event(now, functools.partial(reduce_step, unit, bit, narrow_bit), [before], uses)
            before = now
            length /= 2.0

    flying = []
    for start, end, name in event_order(events):
        for flight in [flight for flight in flying if flight[0] <= start]:
            flying.remove(flight)
            landed.extend(part_in for _, part_in in state[flight[1]].values())
        actions[name]()
        if name[0] == "reduce" and name[2] == narrow_bits[-1]:
            flying.append((end, name[1]))

    spec = [(*UNITS[unit], s) for unit in range(len(UNITS)) for s in range(group)]
    pairs = [state[unit][0, s] for unit in range(len(UNITS)) for s in range(group)]
    return finish(
        spec,
        pairs,
        group,
        narrow_count,
        part,
        columns_local,
        place,
        bare_terms,
        occ_gap,
        virt_gap,
    )


def solution(mesh):
    placed = (
        P(("wide", "narrow"), None),
        P("narrow", "wide"),
        P("wide", "narrow"),
        P(),
        P(),
        P("wide"),
        P("narrow"),
    )
    return jax.shard_map(
        shards, mesh=mesh, in_specs=placed, out_specs=P("wide", "narrow"), check_vma=False
    )
```

```python
import functools

import jax
import jax.numpy as jnp
from jax import lax
from jax.experimental import pallas as pl
from jax.experimental.pallas import tpu as pltpu
from jax.sharding import PartitionSpec as P

TILE = 128
CHUNKS = 4
CORES = 2
GROUPS = ((0,), (1,), (2, 3))
UNITS = tuple((chunk, (half,)) for chunk in range(CHUNKS) for half in range(CORES))

SMEM = pl.BlockSpec(memory_space=pltpu.SMEM)
VMEM = pl.BlockSpec(memory_space=pltpu.VMEM)
ANY = pl.BlockSpec(memory_space=pl.ANY)
SMALL = pl.CostEstimate(flops=1, bytes_accessed=1, transcendentals=0)


def after(value, *others):
    return lax.optimization_barrier((value, *others))[0]


def cut_kernel(count, bounds, place_ref, whole_ref, *outs):
    z = place_ref[2]
    depth = outs[0].shape[1]
    for g, (low, high) in enumerate(bounds):
        for m in range(count):
            start = pl.multiple_of((z ^ m) * depth, depth)
            outs[g * count + m][...] = whole_ref[low:high, pl.ds(start, depth)]


def cut(whole, count, depth, part, place):
    bounds = [(group[0] * part, (group[-1] + 1) * part) for group in GROUPS]
    shapes = [
        jax.ShapeDtypeStruct((high - low, depth), whole.dtype)
        for low, high in bounds
        for _ in range(count)
    ]
    outs = pl.pallas_call(
        functools.partial(cut_kernel, count, bounds),
        in_specs=[SMEM, VMEM],
        out_specs=[VMEM] * len(shapes),
        out_shape=shapes,
        cost_estimate=SMALL,
        compiler_params=pltpu.CompilerParams(vmem_limit_bytes=2**20),
        name="cut",
    )(place, whole)
    return [outs[g * count : (g + 1) * count] for g in range(len(bounds))]


def pack_kernel(count, part, place_ref, *refs):
    z = place_ref[2]
    for c, out in enumerate(refs[count:]):
        for m in range(count):
            rows = pl.ds(pl.multiple_of((z ^ m) * part, part), part)
            out[rows, :] = refs[m][c * part : (c + 1) * part, :]


def pack(blocks, part, place):
    count = len(blocks)
    rows, depth = blocks[0].shape
    shape = jax.ShapeDtypeStruct((count * part, depth), blocks[0].dtype)
    return pl.pallas_call(
        functools.partial(pack_kernel, count, part),
        in_specs=[SMEM] + [VMEM] * count,
        out_specs=[VMEM] * (rows // part),
        out_shape=[shape] * (rows // part),
        cost_estimate=SMALL,
        compiler_params=pltpu.CompilerParams(vmem_limit_bytes=2**20),
        name="pack",
    )(place, *blocks)


def split_kernel(step, whole_ref, high_ref, low_ref, buffer, sems):
    count = whole_ref.shape[0] // step

    def copy(i):
        return pltpu.make_async_copy(
            whole_ref.at[pl.ds(i * step, step)], buffer.at[i % 2], sems.at[i % 2]
        )

    copy(0).start()
    for i in range(count):
        if i + 1 < count:
            copy(i + 1).start()
        copy(i).wait()
        whole = buffer[i % 2]
        high = whole.astype(jnp.bfloat16)
        here = slice(i * step, (i + 1) * step)
        high_ref[here, :] = high
        low_ref[here, :] = (whole - high.astype(jnp.float32)).astype(jnp.bfloat16)


def split(whole):
    rows, columns = whole.shape
    step = min(256, rows)
    half = jax.ShapeDtypeStruct((rows, columns), jnp.bfloat16)
    return pl.pallas_call(
        functools.partial(split_kernel, step),
        in_specs=[ANY],
        out_specs=[VMEM, VMEM],
        out_shape=[half, half],
        scratch_shapes=[
            pltpu.VMEM((2, step, columns), jnp.float32),
            pltpu.SemaphoreType.DMA((2,)),
        ],
        cost_estimate=SMALL,
        compiler_params=pltpu.CompilerParams(vmem_limit_bytes=3 * 2**20),
        name="split",
    )(whole)


def product_kernel(count, rows, layout, targets, halves, place_ref, pattern_ref, order_ref, *refs):
    lefts = refs[: len(layout)]
    factors = refs[len(layout) : len(layout) + 2 * halves]
    outs = refs[len(layout) + 2 * halves : -1]
    left = refs[-1]
    depth = lefts[0].shape[1]
    total = count * rows
    chip, core, z = place_ref[0], place_ref[1], place_ref[2]
    tiles = depth // TILE
    for held, pieces in zip(lefts, layout):
        start = 0
        for k, first, size in pieces:
            kind = order_ref[(chip ^ k) * CORES + core]
            high_rows = slice(k * rows + first, k * rows + first + size)
            low_rows = slice(total + k * rows + first, total + k * rows + first + size)
            for t in range(tiles):
                kept = pattern_ref[kind, z * tiles + t].astype(jnp.float32)
                here = slice(t * TILE, (t + 1) * TILE)
                value = held[start : start + size, here] * kept
                high = value.astype(jnp.bfloat16)
                left[high_rows, here] = high
                left[low_rows, here] = (value - high.astype(jnp.float32)).astype(jnp.bfloat16)
            start += size
    columns = factors[0].shape[1]
    width = min(512, columns)
    for half in range(halves):
        high_ref, low_ref = factors[2 * half : 2 * half + 2]
        for j in range(columns // width):
            here = slice(j * width, (j + 1) * width)
            both = jnp.dot(left[...], high_ref[:, here], preferred_element_type=jnp.float32)
            small = jnp.dot(
                left[:total, :], low_ref[:, here], preferred_element_type=jnp.float32
            )
            result = both[:total] + (both[total:] + small)
            there = slice(half * columns + j * width, half * columns + (j + 1) * width)
            for out, blocks in zip(outs, targets):
                for n, k in enumerate(blocks):
                    out[n * rows : (n + 1) * rows, there] = result[k * rows : (k + 1) * rows]


def product(lefts, layout, targets, factors, place, pattern, block_order):
    rows, depth = lefts[0].shape
    count = sum(held.shape[0] for held in lefts) // rows
    halves = len(factors)
    columns = factors[0][0].shape[1]
    total = count * rows
    return pl.pallas_call(
        functools.partial(product_kernel, count, rows, layout, targets, halves),
        in_specs=[SMEM] * 3 + [VMEM] * (len(lefts) + 2 * halves),
        out_specs=[VMEM] * len(targets),
        out_shape=[
            jax.ShapeDtypeStruct((len(blocks) * rows, halves * columns), jnp.float32)
            for blocks in targets
        ],
        scratch_shapes=[pltpu.VMEM((2 * total, depth), jnp.bfloat16)],
        cost_estimate=SMALL,
        compiler_params=pltpu.CompilerParams(vmem_limit_bytes=8 * total * depth + 3 * 2**20),
        name="product",
    )(place, pattern, block_order, *lefts, *[part for pair in factors for part in pair])


def finish_kernel(spec, group, count, part, width, place_ref, bare_ref, occ_ref, virt_ref, *refs):
    out_ref = refs[-1]
    chip, core = place_ref[0], place_ref[1]
    rows_local = CHUNKS * part
    for number, (chunk, halves, s) in enumerate(spec):
        kept, arrived = refs[2 * number], refs[2 * number + 1]
        for position, half in enumerate(halves):
            column = (((chip % group) ^ s) * CORES + (half ^ core)) * width
            columns = pl.ds(pl.multiple_of(column, width), width)
            here = slice(position * width, (position + 1) * width)
            for m in range(count):
                rows = slice(m * rows_local + chunk * part, m * rows_local + (chunk + 1) * part)
                block = slice(m * part, (m + 1) * part)
                ladder = kept[block, here] + arrived[block, here]
                gap = occ_ref[rows, :] + virt_ref[:, columns]
                out_ref[rows, columns] = -(bare_ref[rows, columns] + ladder) / gap


def finish(spec, pairs, group, count, part, width, place, bare, occ, virt):
    return pl.pallas_call(
        functools.partial(finish_kernel, spec, group, count, part, width),
        in_specs=[SMEM] + [VMEM] * (3 + 2 * len(pairs)),
        out_specs=VMEM,
        out_shape=jax.ShapeDtypeStruct(bare.shape, bare.dtype),
        cost_estimate=SMALL,
        compiler_params=pltpu.CompilerParams(vmem_limit_bytes=2 * 2**20),
        name="finish",
    )(place, bare, occ[:, None], virt[None, :], *[part_in for pair in pairs for part_in in pair])


def shards(amplitudes, integrals, bare_terms, pattern, block_order, occ_gap, virt_gap):
    rows_local, columns = amplitudes.shape
    depth, columns_local = integrals.shape
    wide_count = lax.axis_size("wide")
    narrow_count = lax.axis_size("narrow")
    chips = wide_count // CORES
    wide = lax.axis_index("wide")
    z = lax.axis_index("narrow")
    chip = wide // CORES
    core = wide % CORES
    part = rows_local // CHUNKS
    rows = narrow_count * part
    group = chips // narrow_count
    place = jnp.stack([chip, core, z]).astype(jnp.int32)
    chip_bits = [1 << b for b in range(chips.bit_length() - 1)]
    narrow_bits = [1 << b for b in range(narrow_count.bit_length() - 1)]
    targets = [list(range(chips))]
    for bit in reversed(chip_bits):
        targets = [[k for k in targets[0] if not k & bit] + [k for k in targets[0] if k & bit]]
    targets = [targets[0][: chips // 2], targets[0][chips // 2 :]]

    def across(value, mask):
        return lax.ppermute(value, "wide", [(w, w ^ mask) for w in range(wide_count)])

    def across_chips(value, mask):
        return across(value, mask * CORES)

    def along(value, mask):
        return lax.ppermute(value, "narrow", [(n, n ^ mask) for n in range(narrow_count)])

    last = []

    def ordered(*values):
        return list(lax.optimization_barrier((*values, *last))[: len(values)])

    def mark(*values):
        last[:] = values

    swapped = across(integrals, 1)
    pieces = cut(amplitudes, narrow_count, depth, part, place)
    spread = {}
    mine = {}
    held = {}
    layouts = {}
    factors = {}
    state = {}

    def spread_step(g):
        sends = ordered(*pieces[g][1:])
        mark(*sends)
        spread[g] = [pieces[g][0]] + [along(send, n + 1) for n, send in enumerate(sends)]

    def pack_step(g):
        packed = pack(ordered(*spread[g]), part, place)
        mark(*packed)
        mine.update(zip(GROUPS[g], packed))

    def gather_step(chunk, number):
        if number == 0:
            held[chunk] = [mine[chunk]]
            layouts[chunk] = [[(0, 0, rows)]]
        direct = chunk == 0 and chips == 4
        if direct and number == 0:
            (send,) = ordered(mine[chunk])
            mark(send)
            held[chunk] += [across_chips(send, 1), across_chips(send, 2)]
            layouts[chunk] += [[(1, 0, rows)], [(2, 0, rows)]]
        elif direct:
            near, far = ordered(held[chunk][1], held[chunk][2])
            near, far = near[: rows // 2], far[rows // 2 :]
            mark(near, far)
            held[chunk] += [across_chips(near, 2), across_chips(far, 1)]
            layouts[chunk] += [[(3, 0, rows // 2)], [(3, rows // 2, rows // 2)]]
        else:
            bit = chip_bits[number]
            send = jnp.concatenate(ordered(*held[chunk]), axis=0)
            mark(send)
            held[chunk].append(across_chips(send, bit))
            layouts[chunk].append([(k | bit, 0, rows) for k in range(bit)])

    def split_step(half):
        factors[half] = split(*ordered(integrals if half == 0 else swapped))
        mark(*factors[half])

    def multiply(unit):
        chunk, halves = UNITS[unit]
        partials = product(
            ordered(*held[chunk]),
            layouts[chunk],
            targets,
            [factors[half] for half in halves],
            place,
            pattern,
            block_order,
        )
        mark(*partials)
        state[unit] = {0: partials}

    def exchange_step(unit, bit):
        names = list(state[unit])
        if bit == chip_bits[0]:
            keep, leave = [state[unit][0][0]], ordered(state[unit][0][1])
        else:
            values = ordered(*state[unit].values())
            half = values[0].shape[0] // 2
            keep = [value[:half] for value in values]
            leave = [value[half:] for value in values]
        send = jnp.concatenate(leave, axis=0)
        mark(send)
        arrived = across_chips(send, bit)
        half = keep[0].shape[0]
        state[unit] = dict(zip(names, keep))
        for n, s in enumerate(names):
            state[unit][s | bit] = arrived[n * half : (n + 1) * half]

    def reduce_step(unit, bit, narrow_bit):
        now = dict(zip(state[unit], ordered(*state[unit].values())))
        same = ((chip // bit) & 1) == ((z // narrow_bit) & 1)
        names = [s for s in now if not s & bit]
        send = jnp.concatenate([jnp.where(same, now[s | bit], now[s]) for s in names], axis=0)
        mark(send)
        arrived = along(send, narrow_bit)
        size = now[0].shape[0]
        final = narrow_bit == narrow_bits[-1]
        state[unit] = {}
        for n, s in enumerate(names):
            kept = jnp.where(same, now[s], now[s | bit])
            came = arrived[n * size : (n + 1) * size]
            state[unit][s] = (kept, came) if final else kept + came

    def land(unit):
        names = list(state[unit])
        values = ordered(*[value for name in names for value in state[unit][name]])
        mark(values[-1])
        state[unit] = {name: (values[2 * n], values[2 * n + 1]) for n, name in enumerate(names)}

    steps = []
    for bit in chip_bits:
        if bit < group:
            steps.append(functools.partial(exchange_step, bit=bit))
    for narrow_bit in narrow_bits:
        bit = group * narrow_bit
        steps.append(functools.partial(exchange_step, bit=bit))
        steps.append(functools.partial(reduce_step, bit=bit, narrow_bit=narrow_bit))
    steps.append(land)

    gathers = [(chunk, number) for chunk in range(1, CHUNKS) for number in range(len(chip_bits))]
    spread_step(0)
    spread_step(1)
    pack_step(0)
    gather_step(0, 0)
    pack_step(1)
    split_step(0)
    for number in range(1, len(chip_bits)):
        gather_step(0, number)
    spread_step(2)
    gather_step(*gathers.pop(0))
    for tick in range(len(UNITS) + len(steps) - 1):
        if tick < len(UNITS):
            multiply(tick)
            steps[0](tick)
            if tick == 0:
                split_step(1)
                pack_step(2)
            late = UNITS[tick + 1][0] if tick + 1 < len(UNITS) else 0
            while gathers and (gathers[0][0] <= late or tick % CORES == gathers[0][1] - 1):
                gather_step(*gathers.pop(0))
        for number in (*range(len(steps) - 1, 1, -1), 1):
            if 0 <= tick - number < len(UNITS):
                steps[number](tick - number)

    spec = [(*UNITS[unit], s) for unit in range(len(UNITS)) for s in range(group)]
    pairs = [state[unit][s] for unit in range(len(UNITS)) for s in range(group)]
    return finish(
        spec,
        pairs,
        group,
        narrow_count,
        part,
        columns_local,
        place,
        bare_terms,
        occ_gap,
        virt_gap,
    )


def solution(mesh):
    placed = (
        P(("wide", "narrow"), None),
        P("narrow", "wide"),
        P("wide", "narrow"),
        P(),
        P(),
        P("wide"),
        P("narrow"),
    )
    return jax.shard_map(
        shards, mesh=mesh, in_specs=placed, out_specs=P("wide", "narrow"), check_vma=False
    )
```

```python
import functools

import jax
import jax.numpy as jnp
from jax import lax
from jax.experimental import pallas as pl
from jax.experimental.pallas import tpu as pltpu
from jax.sharding import PartitionSpec as P

TILE = 128
CHUNKS = 4
CORES = 2
GROUPS = ((0,), (1,), (2, 3))
UNITS = tuple((chunk, (half,)) for chunk in range(CHUNKS) for half in range(CORES))

SMEM = pl.BlockSpec(memory_space=pltpu.SMEM)
VMEM = pl.BlockSpec(memory_space=pltpu.VMEM)
HBM = pl.BlockSpec(memory_space=pltpu.HBM)
SMALL = pl.CostEstimate(flops=1, bytes_accessed=1, transcendentals=0)


def after(value, *others):
    return lax.optimization_barrier((value, *others))[0]


def cut_kernel(count, bounds, place_ref, whole_ref, *outs):
    z = place_ref[2]
    depth = outs[0].shape[1]
    for g, (low, high) in enumerate(bounds):
        for m in range(count):
            start = pl.multiple_of((z ^ m) * depth, depth)
            outs[g * count + m][...] = whole_ref[low:high, pl.ds(start, depth)]


def cut(whole, count, depth, part, place):
    bounds = [(group[0] * part, (group[-1] + 1) * part) for group in GROUPS]
    shapes = [
        jax.ShapeDtypeStruct((high - low, depth), whole.dtype)
        for low, high in bounds
        for _ in range(count)
    ]
    outs = pl.pallas_call(
        functools.partial(cut_kernel, count, bounds),
        in_specs=[SMEM, VMEM],
        out_specs=[VMEM] * len(shapes),
        out_shape=shapes,
        cost_estimate=SMALL,
        compiler_params=pltpu.CompilerParams(vmem_limit_bytes=2**20),
        name="cut",
    )(place, whole)
    return [outs[g * count : (g + 1) * count] for g in range(len(bounds))]


def pack_kernel(count, part, place_ref, token_ref, *refs):
    del token_ref
    z = place_ref[2]
    for c, out in enumerate(refs[count:]):
        for m in range(count):
            rows = pl.ds(pl.multiple_of((z ^ m) * part, part), part)
            out[rows, :] = refs[m][c * part : (c + 1) * part, :]


def pack(blocks, part, place, token):
    count = len(blocks)
    rows, depth = blocks[0].shape
    shape = jax.ShapeDtypeStruct((count * part, depth), blocks[0].dtype)
    return pl.pallas_call(
        functools.partial(pack_kernel, count, part),
        in_specs=[SMEM, HBM] + [VMEM] * count,
        out_specs=[VMEM] * (rows // part),
        out_shape=[shape] * (rows // part),
        cost_estimate=SMALL,
        compiler_params=pltpu.CompilerParams(vmem_limit_bytes=2**20),
        name="pack",
    )(place, token, *blocks)


def split_kernel(step, whole_ref, high_ref, low_ref, token_ref, buffer, sems):
    count = whole_ref.shape[0] // step

    def copy(i):
        return pltpu.make_async_copy(
            whole_ref.at[pl.ds(i * step, step)], buffer.at[i % 2], sems.at[i % 2]
        )

    copy(0).start()
    token_ref[...] = jnp.zeros_like(token_ref)
    for i in range(count):
        if i + 1 < count:
            copy(i + 1).start()
        copy(i).wait()
        whole = buffer[i % 2]
        high = whole.astype(jnp.bfloat16)
        here = slice(i * step, (i + 1) * step)
        high_ref[here, :] = high
        low_ref[here, :] = (whole - high.astype(jnp.float32)).astype(jnp.bfloat16)


def split(whole):
    rows, columns = whole.shape
    step = min(256, rows)
    half = jax.ShapeDtypeStruct((rows, columns), jnp.bfloat16)
    return pl.pallas_call(
        functools.partial(split_kernel, step),
        in_specs=[HBM],
        out_specs=[VMEM, VMEM, VMEM],
        out_shape=[half, half, jax.ShapeDtypeStruct((8, 128), jnp.float32)],
        scratch_shapes=[
            pltpu.VMEM((2, step, columns), jnp.float32),
            pltpu.SemaphoreType.DMA((2,)),
        ],
        cost_estimate=SMALL,
        compiler_params=pltpu.CompilerParams(vmem_limit_bytes=3 * 2**20),
        name="split",
    )(whole)


def product_kernel(count, rows, layout, targets, halves, place_ref, pattern_ref, order_ref, *refs):
    lefts = refs[: len(layout)]
    factors = refs[len(layout) : len(layout) + 2 * halves]
    outs = refs[len(layout) + 2 * halves : -1]
    left = refs[-1]
    depth = lefts[0].shape[1]
    total = count * rows
    chip, core, z = place_ref[0], place_ref[1], place_ref[2]
    tiles = depth // TILE
    for held, pieces in zip(lefts, layout):
        start = 0
        for k, first, size in pieces:
            kind = order_ref[(chip ^ k) * CORES + core]
            high_rows = slice(k * rows + first, k * rows + first + size)
            low_rows = slice(total + k * rows + first, total + k * rows + first + size)
            for t in range(tiles):
                kept = pattern_ref[kind, z * tiles + t].astype(jnp.float32)
                here = slice(t * TILE, (t + 1) * TILE)
                value = held[start : start + size, here] * kept
                high = value.astype(jnp.bfloat16)
                left[high_rows, here] = high
                left[low_rows, here] = (value - high.astype(jnp.float32)).astype(jnp.bfloat16)
            start += size
    columns = factors[0].shape[1]
    width = min(512, columns)
    for half in range(halves):
        high_ref, low_ref = factors[2 * half : 2 * half + 2]
        for j in range(columns // width):
            here = slice(j * width, (j + 1) * width)
            both = jnp.dot(left[...], high_ref[:, here], preferred_element_type=jnp.float32)
            small = jnp.dot(
                left[:total, :], low_ref[:, here], preferred_element_type=jnp.float32
            )
            result = both[:total] + (both[total:] + small)
            there = slice(half * columns + j * width, half * columns + (j + 1) * width)
            for out, blocks in zip(outs, targets):
                for n, k in enumerate(blocks):
                    out[n * rows : (n + 1) * rows, there] = result[k * rows : (k + 1) * rows]


def product(lefts, layout, targets, factors, place, pattern, block_order):
    rows, depth = lefts[0].shape
    count = sum(held.shape[0] for held in lefts) // rows
    halves = len(factors)
    columns = factors[0][0].shape[1]
    total = count * rows
    return pl.pallas_call(
        functools.partial(product_kernel, count, rows, layout, targets, halves),
        in_specs=[SMEM] * 3 + [VMEM] * (len(lefts) + 2 * halves),
        out_specs=[VMEM] * len(targets),
        out_shape=[
            jax.ShapeDtypeStruct((len(blocks) * rows, halves * columns), jnp.float32)
            for blocks in targets
        ],
        scratch_shapes=[pltpu.VMEM((2 * total, depth), jnp.bfloat16)],
        cost_estimate=pl.CostEstimate(
            flops=12 * total * depth * halves * columns, bytes_accessed=1, transcendentals=0
        ),
        compiler_params=pltpu.CompilerParams(vmem_limit_bytes=8 * total * depth + 3 * 2**20),
        name="product",
    )(place, pattern, block_order, *lefts, *[part for pair in factors for part in pair])


def finish_kernel(spec, group, count, part, width, place_ref, bare_ref, occ_ref, virt_ref, *refs):
    out_ref = refs[-1]
    chip, core = place_ref[0], place_ref[1]
    rows_local = CHUNKS * part
    for number, (chunk, halves, s) in enumerate(spec):
        kept, arrived = refs[2 * number], refs[2 * number + 1]
        for position, half in enumerate(halves):
            column = (((chip % group) ^ s) * CORES + (half ^ core)) * width
            columns = pl.ds(pl.multiple_of(column, width), width)
            here = slice(position * width, (position + 1) * width)
            for m in range(count):
                rows = slice(m * rows_local + chunk * part, m * rows_local + (chunk + 1) * part)
                block = slice(m * part, (m + 1) * part)
                ladder = kept[block, here] + arrived[block, here]
                gap = occ_ref[rows, :] + virt_ref[:, columns]
                out_ref[rows, columns] = -(bare_ref[rows, columns] + ladder) / gap


def finish(spec, pairs, group, count, part, width, place, bare, occ, virt):
    return pl.pallas_call(
        functools.partial(finish_kernel, spec, group, count, part, width),
        in_specs=[SMEM] + [VMEM] * (3 + 2 * len(pairs)),
        out_specs=VMEM,
        out_shape=jax.ShapeDtypeStruct(bare.shape, bare.dtype),
        cost_estimate=SMALL,
        compiler_params=pltpu.CompilerParams(vmem_limit_bytes=2 * 2**20),
        name="finish",
    )(place, bare, occ[:, None], virt[None, :], *[part_in for pair in pairs for part_in in pair])


def shards(amplitudes, integrals, bare_terms, pattern, block_order, occ_gap, virt_gap):
    rows_local, columns = amplitudes.shape
    depth, columns_local = integrals.shape
    wide_count = lax.axis_size("wide")
    narrow_count = lax.axis_size("narrow")
    chips = wide_count // CORES
    wide = lax.axis_index("wide")
    z = lax.axis_index("narrow")
    chip = wide // CORES
    core = wide % CORES
    part = rows_local // CHUNKS
    rows = narrow_count * part
    group = chips // narrow_count
    place = jnp.stack([chip, core, z]).astype(jnp.int32)
    chip_bits = [1 << b for b in range(chips.bit_length() - 1)]
    narrow_bits = [1 << b for b in range(narrow_count.bit_length() - 1)]
    targets = [list(range(chips))]
    for bit in reversed(chip_bits):
        targets = [[k for k in targets[0] if not k & bit] + [k for k in targets[0] if k & bit]]
    targets = [targets[0][: chips // 2], targets[0][chips // 2 :]]

    def across(value, mask):
        return lax.ppermute(value, "wide", [(w, w ^ mask) for w in range(wide_count)])

    def across_chips(value, mask):
        return across(value, mask * CORES)

    def along(value, mask):
        return lax.ppermute(value, "narrow", [(n, n ^ mask) for n in range(narrow_count)])

    last = []
    token = []

    def ordered(*values):
        return list(lax.optimization_barrier((*values, *last))[: len(values)])

    def mark(*values):
        last[:] = values

    swapped = across(integrals, 1)
    pieces = cut(amplitudes, narrow_count, depth, part, place)
    spread = {}
    mine = {}
    held = {}
    layouts = {}
    factors = {}
    state = {}

    def spread_step(g):
        sends = ordered(*pieces[g][1:])
        mark(*sends)
        spread[g] = [pieces[g][0]] + [along(send, n + 1) for n, send in enumerate(sends)]

    def pack_step(g):
        packed = pack(ordered(*spread[g]), part, place, token[-1])
        mark(*packed)
        mine.update(zip(GROUPS[g], packed))

    def gather_step(chunk, number):
        if number == 0:
            held[chunk] = [mine[chunk]]
            layouts[chunk] = [[(0, 0, rows)]]
        direct = chunk == 0 and chips == 4
        if direct and number == 0:
            (send,) = ordered(mine[chunk])
            mark(send)
            held[chunk] += [across_chips(send, 1), across_chips(send, 2)]
            layouts[chunk] += [[(1, 0, rows)], [(2, 0, rows)]]
        elif direct:
            near, far = ordered(held[chunk][1], held[chunk][2])
            near, far = near[: rows // 2], far[rows // 2 :]
            mark(near, far)
            held[chunk] += [across_chips(near, 2), across_chips(far, 1)]
            layouts[chunk] += [[(3, 0, rows // 2)], [(3, rows // 2, rows // 2)]]
        else:
            bit = chip_bits[number]
            send = jnp.concatenate(ordered(*held[chunk]), axis=0)
            mark(send)
            held[chunk].append(across_chips(send, bit))
            layouts[chunk].append([(k | bit, 0, rows) for k in range(bit)])

    def split_step(half):
        *factors[half], done = split(*ordered(integrals if half == 0 else swapped))
        token.append(done)

    def multiply(unit):
        chunk, halves = UNITS[unit]
        partials = product(
            ordered(*held[chunk]),
            layouts[chunk],
            targets,
            [factors[half] for half in halves],
            place,
            pattern,
            block_order,
        )
        mark(*partials)
        state[unit] = {0: partials}

    def exchange_step(unit, bit):
        names = list(state[unit])
        if bit == chip_bits[0]:
            keep, leave = [state[unit][0][0]], ordered(state[unit][0][1])
        else:
            values = ordered(*state[unit].values())
            half = values[0].shape[0] // 2
            keep = [value[:half] for value in values]
            leave = [value[half:] for value in values]
        send = jnp.concatenate(leave, axis=0)
        mark(send)
        arrived = across_chips(send, bit)
        half = keep[0].shape[0]
        state[unit] = dict(zip(names, keep))
        for n, s in enumerate(names):
            state[unit][s | bit] = arrived[n * half : (n + 1) * half]

    def reduce_step(unit, bit, narrow_bit):
        now = dict(zip(state[unit], ordered(*state[unit].values())))
        same = ((chip // bit) & 1) == ((z // narrow_bit) & 1)
        names = [s for s in now if not s & bit]
        send = jnp.concatenate([jnp.where(same, now[s | bit], now[s]) for s in names], axis=0)
        mark(send)
        arrived = along(send, narrow_bit)
        size = now[0].shape[0]
        final = narrow_bit == narrow_bits[-1]
        state[unit] = {}
        for n, s in enumerate(names):
            kept = jnp.where(same, now[s], now[s | bit])
            came = arrived[n * size : (n + 1) * size]
            state[unit][s] = (kept, came) if final else kept + came

    def land(unit):
        names = list(state[unit])
        values = ordered(*[value for name in names for value in state[unit][name]])
        mark(values[-1])
        state[unit] = {name: (values[2 * n], values[2 * n + 1]) for n, name in enumerate(names)}

    steps = []
    for bit in chip_bits:
        if bit < group:
            steps.append(functools.partial(exchange_step, bit=bit))
    for narrow_bit in narrow_bits:
        bit = group * narrow_bit
        steps.append(functools.partial(exchange_step, bit=bit))
        steps.append(functools.partial(reduce_step, bit=bit, narrow_bit=narrow_bit))
    steps.append(land)

    gathers = [(chunk, number) for chunk in range(1, CHUNKS) for number in range(len(chip_bits))]
    spread_step(0)
    spread_step(1)
    split_step(0)
    pack_step(0)
    gather_step(0, 0)
    for number in range(1, len(chip_bits)):
        gather_step(0, number)
    for tick in range(len(UNITS) + len(steps) - 1):
        if tick < len(UNITS):
            multiply(tick)
            steps[0](tick)
            if tick == 0:
                pack_step(1)
                gather_step(*gathers.pop(0))
                spread_step(2)
                split_step(1)
                pack_step(2)
            late = UNITS[tick + 1][0] if tick + 1 < len(UNITS) else 0
            while gathers and (gathers[0][0] <= late or tick % CORES == gathers[0][1] - 1):
                gather_step(*gathers.pop(0))
        for number in (*range(len(steps) - 1, 1, -1), 1):
            if 0 <= tick - number < len(UNITS):
                steps[number](tick - number)

    spec = [(*UNITS[unit], s) for unit in range(len(UNITS)) for s in range(group)]
    pairs = [state[unit][s] for unit in range(len(UNITS)) for s in range(group)]
    return finish(
        spec,
        pairs,
        group,
        narrow_count,
        part,
        columns_local,
        place,
        bare_terms,
        occ_gap,
        virt_gap,
    )


def solution(mesh):
    placed = (
        P(("wide", "narrow"), None),
        P("narrow", "wide"),
        P("wide", "narrow"),
        P(),
        P(),
        P("wide"),
        P("narrow"),
    )
    return jax.shard_map(
        shards, mesh=mesh, in_specs=placed, out_specs=P("wide", "narrow"), check_vma=False
    )
```

```python
import functools

import jax
import jax.numpy as jnp
from jax import lax
from jax.experimental import pallas as pl
from jax.experimental.pallas import tpu as pltpu
from jax.sharding import PartitionSpec as P

TILE = 128
CHUNKS = 4
CORES = 2
GROUPS = ((0,), (1,), (2, 3))
UNITS = tuple((chunk, (half,)) for chunk in range(CHUNKS) for half in range(CORES))

ORDER = (
    "s0", "f0", "s1", "p0", "g00", "s2", "g01", "p1", "g10", "e0", "f1", "g11", "p2", "e1",
    "g20", "r0", "r1", "g30", "x0", "g21", "e3", "x1", "g31", "e2", "z0", "r3", "e5", "z1",
    "r2", "l0", "e4", "x3", "r5", "l1", "e6", "z3", "x2", "r4", "e7", "x5", "z2", "r6", "l3",
    "x4", "z5", "r7", "l2", "z4", "x6", "l5", "z6", "x7", "l4", "z7", "l6", "l7",
)

SMEM = pl.BlockSpec(memory_space=pltpu.SMEM)
VMEM = pl.BlockSpec(memory_space=pltpu.VMEM)
HBM = pl.BlockSpec(memory_space=pltpu.HBM)
SMALL = pl.CostEstimate(flops=1, bytes_accessed=1, transcendentals=0)


def after(value, *others):
    return lax.optimization_barrier((value, *others))[0]


def cut_kernel(count, bounds, place_ref, whole_ref, *outs):
    z = place_ref[2]
    depth = outs[0].shape[1]
    for g, (low, high) in enumerate(bounds):
        for m in range(count):
            start = pl.multiple_of((z ^ m) * depth, depth)
            outs[g * count + m][...] = whole_ref[low:high, pl.ds(start, depth)]


def cut(whole, count, depth, part, place):
    bounds = [(group[0] * part, (group[-1] + 1) * part) for group in GROUPS]
    shapes = [
        jax.ShapeDtypeStruct((high - low, depth), whole.dtype)
        for low, high in bounds
        for _ in range(count)
    ]
    outs = pl.pallas_call(
        functools.partial(cut_kernel, count, bounds),
        in_specs=[SMEM, VMEM],
        out_specs=[VMEM] * len(shapes),
        out_shape=shapes,
        cost_estimate=SMALL,
        compiler_params=pltpu.CompilerParams(vmem_limit_bytes=2**20),
        name="cut",
    )(place, whole)
    return [outs[g * count : (g + 1) * count] for g in range(len(bounds))]


def pack_kernel(count, part, place_ref, token_ref, *refs):
    del token_ref
    z = place_ref[2]
    for c, out in enumerate(refs[count:]):
        for m in range(count):
            rows = pl.ds(pl.multiple_of((z ^ m) * part, part), part)
            out[rows, :] = refs[m][c * part : (c + 1) * part, :]


def pack(blocks, part, place, token):
    count = len(blocks)
    rows, depth = blocks[0].shape
    shape = jax.ShapeDtypeStruct((count * part, depth), blocks[0].dtype)
    return pl.pallas_call(
        functools.partial(pack_kernel, count, part),
        in_specs=[SMEM, HBM] + [VMEM] * count,
        out_specs=[VMEM] * (rows // part),
        out_shape=[shape] * (rows // part),
        cost_estimate=SMALL,
        compiler_params=pltpu.CompilerParams(vmem_limit_bytes=2**20),
        name="pack",
    )(place, token, *blocks)


def split_kernel(step, whole_ref, high_ref, low_ref, token_ref, buffer, sems):
    count = whole_ref.shape[0] // step

    def copy(i):
        return pltpu.make_async_copy(
            whole_ref.at[pl.ds(i * step, step)], buffer.at[i % 2], sems.at[i % 2]
        )

    copy(0).start()
    token_ref[...] = jnp.zeros_like(token_ref)
    for i in range(count):
        if i + 1 < count:
            copy(i + 1).start()
        copy(i).wait()
        whole = buffer[i % 2]
        high = whole.astype(jnp.bfloat16)
        here = slice(i * step, (i + 1) * step)
        high_ref[here, :] = high
        low_ref[here, :] = (whole - high.astype(jnp.float32)).astype(jnp.bfloat16)


def split(whole):
    rows, columns = whole.shape
    step = min(256, rows)
    half = jax.ShapeDtypeStruct((rows, columns), jnp.bfloat16)
    return pl.pallas_call(
        functools.partial(split_kernel, step),
        in_specs=[HBM],
        out_specs=[VMEM, VMEM, VMEM],
        out_shape=[half, half, jax.ShapeDtypeStruct((8, 128), jnp.float32)],
        scratch_shapes=[
            pltpu.VMEM((2, step, columns), jnp.float32),
            pltpu.SemaphoreType.DMA((2,)),
        ],
        cost_estimate=SMALL,
        compiler_params=pltpu.CompilerParams(vmem_limit_bytes=3 * 2**20),
        name="split",
    )(whole)


def product_kernel(count, rows, layout, targets, halves, place_ref, pattern_ref, order_ref, *refs):
    lefts = refs[: len(layout)]
    factors = refs[len(layout) : len(layout) + 2 * halves]
    outs = refs[len(layout) + 2 * halves : -1]
    left = refs[-1]
    depth = lefts[0].shape[1]
    total = count * rows
    chip, core, z = place_ref[0], place_ref[1], place_ref[2]
    tiles = depth // TILE
    for held, pieces in zip(lefts, layout):
        start = 0
        for k, first, size in pieces:
            kind = order_ref[(chip ^ k) * CORES + core]
            high_rows = slice(k * rows + first, k * rows + first + size)
            low_rows = slice(total + k * rows + first, total + k * rows + first + size)
            for t in range(tiles):
                kept = pattern_ref[kind, z * tiles + t].astype(jnp.float32)
                here = slice(t * TILE, (t + 1) * TILE)
                value = held[start : start + size, here] * kept
                high = value.astype(jnp.bfloat16)
                left[high_rows, here] = high
                left[low_rows, here] = (value - high.astype(jnp.float32)).astype(jnp.bfloat16)
            start += size
    columns = factors[0].shape[1]
    width = min(512, columns)
    for half in range(halves):
        high_ref, low_ref = factors[2 * half : 2 * half + 2]
        for j in range(columns // width):
            here = slice(j * width, (j + 1) * width)
            both = jnp.dot(left[...], high_ref[:, here], preferred_element_type=jnp.float32)
            small = jnp.dot(
                left[:total, :], low_ref[:, here], preferred_element_type=jnp.float32
            )
            result = both[:total] + (both[total:] + small)
            there = slice(half * columns + j * width, half * columns + (j + 1) * width)
            for out, blocks in zip(outs, targets):
                for n, k in enumerate(blocks):
                    out[n * rows : (n + 1) * rows, there] = result[k * rows : (k + 1) * rows]


def product(lefts, layout, targets, factors, place, pattern, block_order):
    rows, depth = lefts[0].shape
    count = sum(held.shape[0] for held in lefts) // rows
    halves = len(factors)
    columns = factors[0][0].shape[1]
    total = count * rows
    return pl.pallas_call(
        functools.partial(product_kernel, count, rows, layout, targets, halves),
        in_specs=[SMEM] * 3 + [VMEM] * (len(lefts) + 2 * halves),
        out_specs=[VMEM] * len(targets),
        out_shape=[
            jax.ShapeDtypeStruct((len(blocks) * rows, halves * columns), jnp.float32)
            for blocks in targets
        ],
        scratch_shapes=[pltpu.VMEM((2 * total, depth), jnp.bfloat16)],
        cost_estimate=pl.CostEstimate(
            flops=12 * total * depth * halves * columns, bytes_accessed=1, transcendentals=0
        ),
        compiler_params=pltpu.CompilerParams(vmem_limit_bytes=8 * total * depth + 3 * 2**20),
        name="product",
    )(place, pattern, block_order, *lefts, *[part for pair in factors for part in pair])


def finish_kernel(spec, group, count, part, width, place_ref, bare_ref, occ_ref, virt_ref, *refs):
    out_ref = refs[-1]
    chip, core = place_ref[0], place_ref[1]
    rows_local = CHUNKS * part
    for number, (chunk, halves, s) in enumerate(spec):
        kept, arrived = refs[2 * number], refs[2 * number + 1]
        for position, half in enumerate(halves):
            column = (((chip % group) ^ s) * CORES + (half ^ core)) * width
            columns = pl.ds(pl.multiple_of(column, width), width)
            here = slice(position * width, (position + 1) * width)
            for m in range(count):
                rows = slice(m * rows_local + chunk * part, m * rows_local + (chunk + 1) * part)
                block = slice(m * part, (m + 1) * part)
                ladder = kept[block, here] + arrived[block, here]
                gap = occ_ref[rows, :] + virt_ref[:, columns]
                out_ref[rows, columns] = -(bare_ref[rows, columns] + ladder) / gap


def finish(spec, pairs, group, count, part, width, place, bare, occ, virt):
    return pl.pallas_call(
        functools.partial(finish_kernel, spec, group, count, part, width),
        in_specs=[SMEM] + [VMEM] * (3 + 2 * len(pairs)),
        out_specs=VMEM,
        out_shape=jax.ShapeDtypeStruct(bare.shape, bare.dtype),
        cost_estimate=SMALL,
        compiler_params=pltpu.CompilerParams(vmem_limit_bytes=2 * 2**20),
        name="finish",
    )(place, bare, occ[:, None], virt[None, :], *[part_in for pair in pairs for part_in in pair])


def shards(amplitudes, integrals, bare_terms, pattern, block_order, occ_gap, virt_gap):
    rows_local, columns = amplitudes.shape
    depth, columns_local = integrals.shape
    wide_count = lax.axis_size("wide")
    narrow_count = lax.axis_size("narrow")
    chips = wide_count // CORES
    wide = lax.axis_index("wide")
    z = lax.axis_index("narrow")
    chip = wide // CORES
    core = wide % CORES
    part = rows_local // CHUNKS
    rows = narrow_count * part
    group = chips // narrow_count
    place = jnp.stack([chip, core, z]).astype(jnp.int32)
    chip_bits = [1 << b for b in range(chips.bit_length() - 1)]
    narrow_bits = [1 << b for b in range(narrow_count.bit_length() - 1)]
    targets = [list(range(chips))]
    for bit in reversed(chip_bits):
        targets = [[k for k in targets[0] if not k & bit] + [k for k in targets[0] if k & bit]]
    targets = [targets[0][: chips // 2], targets[0][chips // 2 :]]

    def across(value, mask):
        return lax.ppermute(value, "wide", [(w, w ^ mask) for w in range(wide_count)])

    def across_chips(value, mask):
        return across(value, mask * CORES)

    def along(value, mask):
        return lax.ppermute(value, "narrow", [(n, n ^ mask) for n in range(narrow_count)])

    last = []
    token = []

    def ordered(*values):
        return list(lax.optimization_barrier((*values, *last))[: len(values)])

    def mark(*values):
        last[:] = values

    swapped = across(integrals, 1)
    pieces = cut(amplitudes, narrow_count, depth, part, place)
    spread = {}
    mine = {}
    held = {}
    layouts = {}
    factors = {}
    state = {}

    def spread_step(g):
        sends = ordered(*pieces[g][1:])
        mark(*sends)
        spread[g] = [pieces[g][0]] + [along(send, n + 1) for n, send in enumerate(sends)]

    def pack_step(g):
        packed = pack(ordered(*spread[g]), part, place, token[-1])
        mark(*packed)
        mine.update(zip(GROUPS[g], packed))

    def gather_step(chunk, number):
        if number == 0:
            held[chunk] = [mine[chunk]]
            layouts[chunk] = [[(0, 0, rows)]]
        direct = chunk == 0 and chips == 4
        if direct and number == 0:
            (send,) = ordered(mine[chunk])
            mark(send)
            held[chunk] += [across_chips(send, 1), across_chips(send, 2)]
            layouts[chunk] += [[(1, 0, rows)], [(2, 0, rows)]]
        elif direct:
            near, far = ordered(held[chunk][1], held[chunk][2])
            near, far = near[: rows // 2], far[rows // 2 :]
            mark(near, far)
            held[chunk] += [across_chips(near, 2), across_chips(far, 1)]
            layouts[chunk] += [[(3, 0, rows // 2)], [(3, rows // 2, rows // 2)]]
        else:
            bit = chip_bits[number]
            send = jnp.concatenate(ordered(*held[chunk]), axis=0)
            mark(send)
            held[chunk].append(across_chips(send, bit))
            layouts[chunk].append([(k | bit, 0, rows) for k in range(bit)])

    def split_step(half):
        *factors[half], done = split(*ordered(integrals if half == 0 else swapped))
        token.append(done)

    def multiply(unit):
        chunk, halves = UNITS[unit]
        partials = product(
            ordered(*held[chunk]),
            layouts[chunk],
            targets,
            [factors[half] for half in halves],
            place,
            pattern,
            block_order,
        )
        mark(*partials)
        state[unit] = {0: partials}

    def exchange_step(unit, bit):
        names = list(state[unit])
        if bit == chip_bits[0]:
            keep, leave = [state[unit][0][0]], ordered(state[unit][0][1])
        else:
            values = ordered(*state[unit].values())
            half = values[0].shape[0] // 2
            keep = [value[:half] for value in values]
            leave = [value[half:] for value in values]
        send = jnp.concatenate(leave, axis=0)
        mark(send)
        arrived = across_chips(send, bit)
        half = keep[0].shape[0]
        state[unit] = dict(zip(names, keep))
        for n, s in enumerate(names):
            state[unit][s | bit] = arrived[n * half : (n + 1) * half]

    def reduce_step(unit, bit, narrow_bit):
        now = dict(zip(state[unit], ordered(*state[unit].values())))
        same = ((chip // bit) & 1) == ((z // narrow_bit) & 1)
        names = [s for s in now if not s & bit]
        send = jnp.concatenate([jnp.where(same, now[s | bit], now[s]) for s in names], axis=0)
        mark(send)
        arrived = along(send, narrow_bit)
        size = now[0].shape[0]
        final = narrow_bit == narrow_bits[-1]
        state[unit] = {}
        for n, s in enumerate(names):
            kept = jnp.where(same, now[s], now[s | bit])
            came = arrived[n * size : (n + 1) * size]
            state[unit][s] = (kept, came) if final else kept + came

    def land(unit):
        names = list(state[unit])
        values = ordered(*[value for name in names for value in state[unit][name]])
        mark(values[-1])
        state[unit] = {name: (values[2 * n], values[2 * n + 1]) for n, name in enumerate(names)}

    steps = []
    for bit in chip_bits:
        if bit < group:
            steps.append(functools.partial(exchange_step, bit=bit))
    for narrow_bit in narrow_bits:
        bit = group * narrow_bit
        steps.append(functools.partial(exchange_step, bit=bit))
        steps.append(functools.partial(reduce_step, bit=bit, narrow_bit=narrow_bit))
    steps.append(land)

    def send_step(unit):
        multiply(unit)
        steps[0](unit)

    if chips == 4 and narrow_count == 4:
        actions = dict(s=spread_step, p=pack_step, f=split_step, g=gather_step, e=send_step)
        actions.update(r=steps[1], x=steps[2], z=steps[3], l=steps[4])
        for name in ORDER:
            actions[name[0]](*[int(number) for number in name[1:]])
    else:
        for half in range(CORES):
            split_step(half)
        for g in range(len(GROUPS)):
            spread_step(g)
            pack_step(g)
        for chunk in range(CHUNKS):
            for number in range(len(chip_bits)):
                gather_step(chunk, number)
        for tick in range(len(UNITS) + len(steps) - 1):
            if tick < len(UNITS):
                send_step(tick)
            for number in range(len(steps) - 1, 0, -1):
                if 0 <= tick - number < len(UNITS):
                    steps[number](tick - number)

    spec = [(*UNITS[unit], s) for unit in range(len(UNITS)) for s in range(group)]
    pairs = [state[unit][s] for unit in range(len(UNITS)) for s in range(group)]
    return finish(
        spec,
        pairs,
        group,
        narrow_count,
        part,
        columns_local,
        place,
        bare_terms,
        occ_gap,
        virt_gap,
    )


def solution(mesh):
    placed = (
        P(("wide", "narrow"), None),
        P("narrow", "wide"),
        P("wide", "narrow"),
        P(),
        P(),
        P("wide"),
        P("narrow"),
    )
    return jax.shard_map(
        shards, mesh=mesh, in_specs=placed, out_specs=P("wide", "narrow"), check_vma=False
    )
```

```python
import functools

import jax
import jax.numpy as jnp
from jax import lax
from jax.experimental import pallas as pl
from jax.experimental.pallas import tpu as pltpu
from jax.sharding import PartitionSpec as P

TILE = 128
CHUNKS = 4
CORES = 2
GROUPS = ((0,), (1,), (2, 3))
UNITS = tuple((chunk, (half,)) for chunk in range(CHUNKS) for half in range(CORES))

ORDER = (
    "s0", "s1", "p0", "g00", "g01", "f0", "e0", "p1", "g10", "s2", "f1", "r0", "e1", "g11",
    "p2", "g20", "x0", "r1", "g30", "e2", "x1", "e3", "z0", "g21", "r2", "r3", "z1", "l0",
    "e4", "x2", "e5", "g31", "x3", "r4", "z2", "r5", "l1", "z3", "x4", "e6", "l2", "x5", "e7",
    "r6", "z4", "l3", "r7", "z5", "x6", "l4", "x7", "z6", "l5", "z7", "l6", "l7",
)

SMEM = pl.BlockSpec(memory_space=pltpu.SMEM)
VMEM = pl.BlockSpec(memory_space=pltpu.VMEM)
HBM = pl.BlockSpec(memory_space=pltpu.HBM)
SMALL = pl.CostEstimate(flops=1, bytes_accessed=1, transcendentals=0)


def after(value, *others):
    return lax.optimization_barrier((value, *others))[0]


def cut_kernel(count, bounds, place_ref, whole_ref, *outs):
    z = place_ref[2]
    depth = outs[0].shape[1]
    for g, (low, high) in enumerate(bounds):
        for m in range(count):
            start = pl.multiple_of((z ^ m) * depth, depth)
            outs[g * count + m][...] = whole_ref[low:high, pl.ds(start, depth)]


def cut(whole, count, depth, part, place):
    bounds = [(group[0] * part, (group[-1] + 1) * part) for group in GROUPS]
    shapes = [
        jax.ShapeDtypeStruct((high - low, depth), whole.dtype)
        for low, high in bounds
        for _ in range(count)
    ]
    outs = pl.pallas_call(
        functools.partial(cut_kernel, count, bounds),
        in_specs=[SMEM, VMEM],
        out_specs=[VMEM] * len(shapes),
        out_shape=shapes,
        cost_estimate=SMALL,
        compiler_params=pltpu.CompilerParams(vmem_limit_bytes=2**20),
        name="cut",
    )(place, whole)
    return [outs[g * count : (g + 1) * count] for g in range(len(bounds))]


def pack_kernel(count, part, place_ref, *refs):
    z = place_ref[2]
    for c, out in enumerate(refs[count:]):
        for m in range(count):
            rows = pl.ds(pl.multiple_of((z ^ m) * part, part), part)
            out[rows, :] = refs[m][c * part : (c + 1) * part, :]


def pack(blocks, part, place):
    count = len(blocks)
    rows, depth = blocks[0].shape
    shape = jax.ShapeDtypeStruct((count * part, depth), blocks[0].dtype)
    return pl.pallas_call(
        functools.partial(pack_kernel, count, part),
        in_specs=[SMEM] + [VMEM] * count,
        out_specs=[VMEM] * (rows // part),
        out_shape=[shape] * (rows // part),
        cost_estimate=SMALL,
        compiler_params=pltpu.CompilerParams(vmem_limit_bytes=2**20),
        name="pack",
    )(place, *blocks)


def split_kernel(step, whole_ref, high_ref, low_ref, token_ref, buffer, sems):
    count = whole_ref.shape[0] // step
    slots = buffer.shape[0]

    def copy(i):
        return pltpu.make_async_copy(
            whole_ref.at[pl.ds(i * step, step)], buffer.at[i % slots], sems.at[i % slots]
        )

    for i in range(min(slots, count)):
        copy(i).start()
    token_ref[...] = jnp.zeros_like(token_ref)
    for i in range(count):
        copy(i).wait()
        whole = buffer[i % slots]
        high = whole.astype(jnp.bfloat16)
        here = slice(i * step, (i + 1) * step)
        high_ref[here, :] = high
        low_ref[here, :] = (whole - high.astype(jnp.float32)).astype(jnp.bfloat16)
        if i + slots < count:
            copy(i + slots).start()


def split(whole):
    rows, columns = whole.shape
    step = min(256, rows)
    slots = min(4, rows // step)
    half = jax.ShapeDtypeStruct((rows, columns), jnp.bfloat16)
    return pl.pallas_call(
        functools.partial(split_kernel, step),
        in_specs=[HBM],
        out_specs=[VMEM, VMEM, VMEM],
        out_shape=[half, half, jax.ShapeDtypeStruct((8, 128), jnp.float32)],
        scratch_shapes=[
            pltpu.VMEM((slots, step, columns), jnp.float32),
            pltpu.SemaphoreType.DMA((slots,)),
        ],
        cost_estimate=SMALL,
        compiler_params=pltpu.CompilerParams(vmem_limit_bytes=6 * 2**20),
        name="split",
    )(whole)


def product_kernel(count, rows, layout, targets, halves, place_ref, pattern_ref, order_ref, *refs):
    lefts = refs[: len(layout)]
    factors = refs[len(layout) : len(layout) + 2 * halves]
    outs = refs[len(layout) + 2 * halves : -1]
    left = refs[-1]
    depth = lefts[0].shape[1]
    total = count * rows
    chip, core, z = place_ref[0], place_ref[1], place_ref[2]
    tiles = depth // TILE
    for held, pieces in zip(lefts, layout):
        start = 0
        for k, first, size in pieces:
            kind = order_ref[(chip ^ k) * CORES + core]
            high_rows = slice(k * rows + first, k * rows + first + size)
            low_rows = slice(total + k * rows + first, total + k * rows + first + size)
            for t in range(tiles):
                kept = pattern_ref[kind, z * tiles + t].astype(jnp.float32)
                here = slice(t * TILE, (t + 1) * TILE)
                value = held[start : start + size, here] * kept
                high = value.astype(jnp.bfloat16)
                left[high_rows, here] = high
                left[low_rows, here] = (value - high.astype(jnp.float32)).astype(jnp.bfloat16)
            start += size
    columns = factors[0].shape[1]
    width = min(512, columns)
    for half in range(halves):
        high_ref, low_ref = factors[2 * half : 2 * half + 2]
        for j in range(columns // width):
            here = slice(j * width, (j + 1) * width)
            both = jnp.dot(left[...], high_ref[:, here], preferred_element_type=jnp.float32)
            small = jnp.dot(
                left[:total, :], low_ref[:, here], preferred_element_type=jnp.float32
            )
            result = both[:total] + (both[total:] + small)
            there = slice(half * columns + j * width, half * columns + (j + 1) * width)
            for out, blocks in zip(outs, targets):
                for n, k in enumerate(blocks):
                    out[n * rows : (n + 1) * rows, there] = result[k * rows : (k + 1) * rows]


def product(lefts, layout, targets, factors, place, pattern, block_order):
    rows, depth = lefts[0].shape
    count = sum(held.shape[0] for held in lefts) // rows
    halves = len(factors)
    columns = factors[0][0].shape[1]
    total = count * rows
    return pl.pallas_call(
        functools.partial(product_kernel, count, rows, layout, targets, halves),
        in_specs=[SMEM] * 3 + [VMEM] * (len(lefts) + 2 * halves),
        out_specs=[VMEM] * len(targets),
        out_shape=[
            jax.ShapeDtypeStruct((len(blocks) * rows, halves * columns), jnp.float32)
            for blocks in targets
        ],
        scratch_shapes=[pltpu.VMEM((2 * total, depth), jnp.bfloat16)],
        cost_estimate=pl.CostEstimate(
            flops=12 * total * depth * halves * columns, bytes_accessed=1, transcendentals=0
        ),
        compiler_params=pltpu.CompilerParams(vmem_limit_bytes=8 * total * depth + 3 * 2**20),
        name="product",
    )(place, pattern, block_order, *lefts, *[part for pair in factors for part in pair])


def finish_kernel(spec, group, count, part, width, place_ref, bare_ref, occ_ref, virt_ref, *refs):
    out_ref = refs[-1]
    chip, core = place_ref[0], place_ref[1]
    rows_local = CHUNKS * part
    for number, (chunk, halves, s) in enumerate(spec):
        kept, arrived = refs[2 * number], refs[2 * number + 1]
        for position, half in enumerate(halves):
            column = (((chip % group) ^ s) * CORES + (half ^ core)) * width
            columns = pl.ds(pl.multiple_of(column, width), width)
            here = slice(position * width, (position + 1) * width)
            for m in range(count):
                rows = slice(m * rows_local + chunk * part, m * rows_local + (chunk + 1) * part)
                block = slice(m * part, (m + 1) * part)
                ladder = kept[block, here] + arrived[block, here]
                gap = occ_ref[rows, :] + virt_ref[:, columns]
                out_ref[rows, columns] = -(bare_ref[rows, columns] + ladder) / gap


def finish(spec, pairs, group, count, part, width, place, bare, occ, virt):
    return pl.pallas_call(
        functools.partial(finish_kernel, spec, group, count, part, width),
        in_specs=[SMEM] + [VMEM] * (3 + 2 * len(pairs)),
        out_specs=VMEM,
        out_shape=jax.ShapeDtypeStruct(bare.shape, bare.dtype),
        cost_estimate=SMALL,
        compiler_params=pltpu.CompilerParams(vmem_limit_bytes=2 * 2**20),
        name="finish",
    )(place, bare, occ[:, None], virt[None, :], *[part_in for pair in pairs for part_in in pair])


def shards(amplitudes, integrals, bare_terms, pattern, block_order, occ_gap, virt_gap):
    rows_local, columns = amplitudes.shape
    depth, columns_local = integrals.shape
    wide_count = lax.axis_size("wide")
    narrow_count = lax.axis_size("narrow")
    chips = wide_count // CORES
    wide = lax.axis_index("wide")
    z = lax.axis_index("narrow")
    chip = wide // CORES
    core = wide % CORES
    part = rows_local // CHUNKS
    rows = narrow_count * part
    group = chips // narrow_count
    place = jnp.stack([chip, core, z]).astype(jnp.int32)
    chip_bits = [1 << b for b in range(chips.bit_length() - 1)]
    narrow_bits = [1 << b for b in range(narrow_count.bit_length() - 1)]
    targets = [list(range(chips))]
    for bit in reversed(chip_bits):
        targets = [[k for k in targets[0] if not k & bit] + [k for k in targets[0] if k & bit]]
    targets = [targets[0][: chips // 2], targets[0][chips // 2 :]]

    def across(value, mask):
        return lax.ppermute(value, "wide", [(w, w ^ mask) for w in range(wide_count)])

    def across_chips(value, mask):
        return across(value, mask * CORES)

    def along(value, mask):
        return lax.ppermute(value, "narrow", [(n, n ^ mask) for n in range(narrow_count)])

    last = []

    def ordered(*values):
        return list(lax.optimization_barrier((*values, *last))[: len(values)])

    def mark(*values):
        last[:] = values

    swapped = across(integrals, 1)
    pieces = cut(amplitudes, narrow_count, depth, part, place)
    spread = {}
    mine = {}
    held = {}
    layouts = {}
    factors = {}
    state = {}

    def spread_step(g):
        sends = ordered(*pieces[g][1:])
        mark(*sends)
        spread[g] = [pieces[g][0]] + [along(send, n + 1) for n, send in enumerate(sends)]

    def pack_step(g):
        packed = pack(ordered(*spread[g]), part, place)
        mark(*packed)
        mine.update(zip(GROUPS[g], packed))

    def gather_step(chunk, number):
        if number == 0:
            held[chunk] = [mine[chunk]]
            layouts[chunk] = [[(0, 0, rows)]]
        direct = chunk == 0 and chips == 4
        if direct and number == 0:
            (send,) = ordered(mine[chunk])
            mark(send)
            held[chunk] += [across_chips(send, 1), across_chips(send, 2)]
            layouts[chunk] += [[(1, 0, rows)], [(2, 0, rows)]]
        elif direct:
            near, far = ordered(held[chunk][1], held[chunk][2])
            near, far = near[: rows // 2], far[rows // 2 :]
            mark(near, far)
            held[chunk] += [across_chips(near, 2), across_chips(far, 1)]
            layouts[chunk] += [[(3, 0, rows // 2)], [(3, rows // 2, rows // 2)]]
        else:
            bit = chip_bits[number]
            send = jnp.concatenate(ordered(*held[chunk]), axis=0)
            mark(send)
            held[chunk].append(across_chips(send, bit))
            layouts[chunk].append([(k | bit, 0, rows) for k in range(bit)])

    def split_step(half):
        *factors[half], done = split(*ordered(integrals if half == 0 else swapped))
        mark(done)

    def multiply(unit):
        chunk, halves = UNITS[unit]
        partials = product(
            ordered(*held[chunk]),
            layouts[chunk],
            targets,
            [factors[half] for half in halves],
            place,
            pattern,
            block_order,
        )
        mark(*partials)
        state[unit] = {0: partials}

    def exchange_step(unit, bit):
        names = list(state[unit])
        if bit == chip_bits[0]:
            keep, leave = [state[unit][0][0]], ordered(state[unit][0][1])
        else:
            values = ordered(*state[unit].values())
            half = values[0].shape[0] // 2
            keep = [value[:half] for value in values]
            leave = [value[half:] for value in values]
        send = jnp.concatenate(leave, axis=0)
        mark(send)
        arrived = across_chips(send, bit)
        half = keep[0].shape[0]
        state[unit] = dict(zip(names, keep))
        for n, s in enumerate(names):
            state[unit][s | bit] = arrived[n * half : (n + 1) * half]

    def reduce_step(unit, bit, narrow_bit):
        now = dict(zip(state[unit], ordered(*state[unit].values())))
        same = ((chip // bit) & 1) == ((z // narrow_bit) & 1)
        names = [s for s in now if not s & bit]
        send = jnp.concatenate([jnp.where(same, now[s | bit], now[s]) for s in names], axis=0)
        mark(send)
        arrived = along(send, narrow_bit)
        size = now[0].shape[0]
        final = narrow_bit == narrow_bits[-1]
        state[unit] = {}
        for n, s in enumerate(names):
            kept = jnp.where(same, now[s], now[s | bit])
            came = arrived[n * size : (n + 1) * size]
            state[unit][s] = (kept, came) if final else kept + came

    def land(unit):
        names = list(state[unit])
        values = ordered(*[value for name in names for value in state[unit][name]])
        mark(values[-1])
        state[unit] = {name: (values[2 * n], values[2 * n + 1]) for n, name in enumerate(names)}

    steps = []
    for bit in chip_bits:
        if bit < group:
            steps.append(functools.partial(exchange_step, bit=bit))
    for narrow_bit in narrow_bits:
        bit = group * narrow_bit
        steps.append(functools.partial(exchange_step, bit=bit))
        steps.append(functools.partial(reduce_step, bit=bit, narrow_bit=narrow_bit))
    steps.append(land)

    def send_step(unit):
        multiply(unit)
        steps[0](unit)

    if chips == 4 and narrow_count == 4:
        actions = dict(s=spread_step, p=pack_step, f=split_step, g=gather_step, e=send_step)
        actions.update(r=steps[1], x=steps[2], z=steps[3], l=steps[4])
        for name in ORDER:
            actions[name[0]](*[int(number) for number in name[1:]])
    else:
        for half in range(CORES):
            split_step(half)
        for g in range(len(GROUPS)):
            spread_step(g)
            pack_step(g)
        for chunk in range(CHUNKS):
            for number in range(len(chip_bits)):
                gather_step(chunk, number)
        for tick in range(len(UNITS) + len(steps) - 1):
            if tick < len(UNITS):
                send_step(tick)
            for number in range(len(steps) - 1, 0, -1):
                if 0 <= tick - number < len(UNITS):
                    steps[number](tick - number)

    spec = [(*UNITS[unit], s) for unit in range(len(UNITS)) for s in range(group)]
    pairs = [state[unit][s] for unit in range(len(UNITS)) for s in range(group)]
    return finish(
        spec,
        pairs,
        group,
        narrow_count,
        part,
        columns_local,
        place,
        bare_terms,
        occ_gap,
        virt_gap,
    )


def solution(mesh):
    placed = (
        P(("wide", "narrow"), None),
        P("narrow", "wide"),
        P("wide", "narrow"),
        P(),
        P(),
        P("wide"),
        P("narrow"),
    )
    return jax.shard_map(
        shards, mesh=mesh, in_specs=placed, out_specs=P("wide", "narrow"), check_vma=False
    )
```

```python
import functools

import jax
import jax.numpy as jnp
from jax import lax
from jax.experimental import pallas as pl
from jax.experimental.pallas import tpu as pltpu
from jax.sharding import PartitionSpec as P

TILE = 128
CHUNKS = 4
CORES = 2
GROUPS = ((0,), (1,), (2, 3))
UNITS = tuple((chunk, (half,)) for chunk in range(CHUNKS) for half in range(CORES))

ORDER = (
    "s0", "s1", "p0", "g00", "p1", "g01", "g10", "s2", "f0", "e0", "g11", "p2", "g20", "f1",
    "e1", "r0", "g21", "e3", "g30", "r1", "x0", "e2", "r3", "x1", "z0", "g31", "e5", "z1",
    "x3", "r2", "l0", "e4", "r5", "e7", "z3", "x2", "l1", "r4", "e6", "x5", "z2", "r7", "x4",
    "z5", "l3", "r6", "l2", "z4", "x7", "z7", "l5", "x6", "l4", "z6", "l7", "l6",
)

SMEM = pl.BlockSpec(memory_space=pltpu.SMEM)
VMEM = pl.BlockSpec(memory_space=pltpu.VMEM)
HBM = pl.BlockSpec(memory_space=pltpu.HBM)
SMALL = pl.CostEstimate(flops=1, bytes_accessed=1, transcendentals=0)


def after(value, *others):
    return lax.optimization_barrier((value, *others))[0]


def cut_kernel(count, bounds, place_ref, whole_ref, *outs):
    z = place_ref[2]
    depth = outs[0].shape[1]
    for g, (low, high) in enumerate(bounds):
        for m in range(count):
            start = pl.multiple_of((z ^ m) * depth, depth)
            outs[g * count + m][...] = whole_ref[low:high, pl.ds(start, depth)]


def cut(whole, count, depth, part, place):
    bounds = [(group[0] * part, (group[-1] + 1) * part) for group in GROUPS]
    shapes = [
        jax.ShapeDtypeStruct((high - low, depth), whole.dtype)
        for low, high in bounds
        for _ in range(count)
    ]
    outs = pl.pallas_call(
        functools.partial(cut_kernel, count, bounds),
        in_specs=[SMEM, VMEM],
        out_specs=[VMEM] * len(shapes),
        out_shape=shapes,
        cost_estimate=SMALL,
        compiler_params=pltpu.CompilerParams(vmem_limit_bytes=2**20),
        name="cut",
    )(place, whole)
    return [outs[g * count : (g + 1) * count] for g in range(len(bounds))]


def pack_kernel(count, part, place_ref, *refs):
    z = place_ref[2]
    for c, out in enumerate(refs[count:]):
        for m in range(count):
            rows = pl.ds(pl.multiple_of((z ^ m) * part, part), part)
            out[rows, :] = refs[m][c * part : (c + 1) * part, :]


def pack(blocks, part, place):
    count = len(blocks)
    rows, depth = blocks[0].shape
    shape = jax.ShapeDtypeStruct((count * part, depth), blocks[0].dtype)
    return pl.pallas_call(
        functools.partial(pack_kernel, count, part),
        in_specs=[SMEM] + [VMEM] * count,
        out_specs=[VMEM] * (rows // part),
        out_shape=[shape] * (rows // part),
        cost_estimate=SMALL,
        compiler_params=pltpu.CompilerParams(vmem_limit_bytes=2**20),
        name="pack",
    )(place, *blocks)


def split_kernel(step, whole_ref, high_ref, low_ref, token_ref, buffer, sems):
    count = whole_ref.shape[0] // step
    slots = buffer.shape[0]

    def copy(i):
        return pltpu.make_async_copy(
            whole_ref.at[pl.ds(i * step, step)], buffer.at[i % slots], sems.at[i % slots]
        )

    for i in range(min(slots, count)):
        copy(i).start()
    token_ref[...] = jnp.zeros_like(token_ref)
    for i in range(count):
        copy(i).wait()
        whole = buffer[i % slots]
        high = whole.astype(jnp.bfloat16)
        here = slice(i * step, (i + 1) * step)
        high_ref[here, :] = high
        low_ref[here, :] = (whole - high.astype(jnp.float32)).astype(jnp.bfloat16)
        if i + slots < count:
            copy(i + slots).start()


def split(whole):
    rows, columns = whole.shape
    step = min(256, rows)
    slots = min(4, rows // step)
    half = jax.ShapeDtypeStruct((rows, columns), jnp.bfloat16)
    return pl.pallas_call(
        functools.partial(split_kernel, step),
        in_specs=[HBM],
        out_specs=[VMEM, VMEM, VMEM],
        out_shape=[half, half, jax.ShapeDtypeStruct((8, 128), jnp.float32)],
        scratch_shapes=[
            pltpu.VMEM((slots, step, columns), jnp.float32),
            pltpu.SemaphoreType.DMA((slots,)),
        ],
        cost_estimate=SMALL,
        compiler_params=pltpu.CompilerParams(vmem_limit_bytes=6 * 2**20),
        name="split",
    )(whole)


def product_kernel(count, rows, layout, targets, halves, place_ref, pattern_ref, order_ref, *refs):
    lefts = refs[: len(layout)]
    factors = refs[len(layout) : len(layout) + 2 * halves]
    outs = refs[len(layout) + 2 * halves : -1]
    left = refs[-1]
    depth = lefts[0].shape[1]
    total = count * rows
    chip, core, z = place_ref[0], place_ref[1], place_ref[2]
    tiles = depth // TILE
    for held, pieces in zip(lefts, layout):
        start = 0
        for k, first, size in pieces:
            kind = order_ref[(chip ^ k) * CORES + core]
            high_rows = slice(k * rows + first, k * rows + first + size)
            low_rows = slice(total + k * rows + first, total + k * rows + first + size)
            for t in range(tiles):
                kept = pattern_ref[kind, z * tiles + t].astype(jnp.float32)
                here = slice(t * TILE, (t + 1) * TILE)
                value = held[start : start + size, here] * kept
                high = value.astype(jnp.bfloat16)
                left[high_rows, here] = high
                left[low_rows, here] = (value - high.astype(jnp.float32)).astype(jnp.bfloat16)
            start += size
    columns = factors[0].shape[1]
    width = min(512, columns)
    for half in range(halves):
        high_ref, low_ref = factors[2 * half : 2 * half + 2]
        for j in range(columns // width):
            here = slice(j * width, (j + 1) * width)
            both = jnp.dot(left[...], high_ref[:, here], preferred_element_type=jnp.float32)
            small = jnp.dot(
                left[:total, :], low_ref[:, here], preferred_element_type=jnp.float32
            )
            result = both[:total] + (both[total:] + small)
            there = slice(half * columns + j * width, half * columns + (j + 1) * width)
            for out, blocks in zip(outs, targets):
                for n, k in enumerate(blocks):
                    out[n * rows : (n + 1) * rows, there] = result[k * rows : (k + 1) * rows]


def product(lefts, layout, targets, factors, place, pattern, block_order):
    rows, depth = lefts[0].shape
    count = sum(held.shape[0] for held in lefts) // rows
    halves = len(factors)
    columns = factors[0][0].shape[1]
    total = count * rows
    return pl.pallas_call(
        functools.partial(product_kernel, count, rows, layout, targets, halves),
        in_specs=[SMEM] * 3 + [VMEM] * (len(lefts) + 2 * halves),
        out_specs=[VMEM] * len(targets),
        out_shape=[
            jax.ShapeDtypeStruct((len(blocks) * rows, halves * columns), jnp.float32)
            for blocks in targets
        ],
        scratch_shapes=[pltpu.VMEM((2 * total, depth), jnp.bfloat16)],
        cost_estimate=pl.CostEstimate(
            flops=12 * total * depth * halves * columns, bytes_accessed=1, transcendentals=0
        ),
        compiler_params=pltpu.CompilerParams(vmem_limit_bytes=8 * total * depth + 3 * 2**20),
        name="product",
    )(place, pattern, block_order, *lefts, *[part for pair in factors for part in pair])


def finish_kernel(spec, group, count, part, width, place_ref, bare_ref, occ_ref, virt_ref, *refs):
    out_ref = refs[-1]
    chip, core = place_ref[0], place_ref[1]
    rows_local = CHUNKS * part
    for number, (chunk, halves, s) in enumerate(spec):
        kept, arrived = refs[2 * number], refs[2 * number + 1]
        for position, half in enumerate(halves):
            column = (((chip % group) ^ s) * CORES + (half ^ core)) * width
            columns = pl.ds(pl.multiple_of(column, width), width)
            here = slice(position * width, (position + 1) * width)
            for m in range(count):
                rows = slice(m * rows_local + chunk * part, m * rows_local + (chunk + 1) * part)
                block = slice(m * part, (m + 1) * part)
                ladder = kept[block, here] + arrived[block, here]
                gap = occ_ref[rows, :] + virt_ref[:, columns]
                out_ref[rows, columns] = -(bare_ref[rows, columns] + ladder) / gap


def finish(spec, pairs, group, count, part, width, place, bare, occ, virt):
    return pl.pallas_call(
        functools.partial(finish_kernel, spec, group, count, part, width),
        in_specs=[SMEM] + [VMEM] * (3 + 2 * len(pairs)),
        out_specs=VMEM,
        out_shape=jax.ShapeDtypeStruct(bare.shape, bare.dtype),
        cost_estimate=SMALL,
        compiler_params=pltpu.CompilerParams(vmem_limit_bytes=2 * 2**20),
        name="finish",
    )(place, bare, occ[:, None], virt[None, :], *[part_in for pair in pairs for part_in in pair])


def shards(amplitudes, integrals, bare_terms, pattern, block_order, occ_gap, virt_gap):
    rows_local, columns = amplitudes.shape
    depth, columns_local = integrals.shape
    wide_count = lax.axis_size("wide")
    narrow_count = lax.axis_size("narrow")
    chips = wide_count // CORES
    wide = lax.axis_index("wide")
    z = lax.axis_index("narrow")
    chip = wide // CORES
    core = wide % CORES
    part = rows_local // CHUNKS
    rows = narrow_count * part
    group = chips // narrow_count
    place = jnp.stack([chip, core, z]).astype(jnp.int32)
    chip_bits = [1 << b for b in range(chips.bit_length() - 1)]
    narrow_bits = [1 << b for b in range(narrow_count.bit_length() - 1)]
    targets = [list(range(chips))]
    for bit in reversed(chip_bits):
        targets = [[k for k in targets[0] if not k & bit] + [k for k in targets[0] if k & bit]]
    targets = [targets[0][: chips // 2], targets[0][chips // 2 :]]

    def across(value, mask):
        return lax.ppermute(value, "wide", [(w, w ^ mask) for w in range(wide_count)])

    def across_chips(value, mask):
        return across(value, mask * CORES)

    def along(value, mask):
        return lax.ppermute(value, "narrow", [(n, n ^ mask) for n in range(narrow_count)])

    last = []

    def ordered(*values):
        return list(lax.optimization_barrier((*values, *last))[: len(values)])

    def mark(*values):
        last[:] = values

    swapped = across(integrals, 1)
    pieces = cut(amplitudes, narrow_count, depth, part, place)
    spread = {}
    mine = {}
    held = {}
    layouts = {}
    factors = {}
    state = {}

    def spread_step(g):
        sends = ordered(*pieces[g][1:])
        mark(*sends)
        spread[g] = [pieces[g][0]] + [along(send, n + 1) for n, send in enumerate(sends)]

    def pack_step(g):
        packed = pack(ordered(*spread[g]), part, place)
        mark(*packed)
        mine.update(zip(GROUPS[g], packed))

    def gather_step(chunk, number):
        if number == 0:
            held[chunk] = [mine[chunk]]
            layouts[chunk] = [[(0, 0, rows)]]
        direct = chunk == 0 and chips == 4
        if direct and number == 0:
            (send,) = ordered(mine[chunk])
            mark(send)
            held[chunk] += [across_chips(send, 1), across_chips(send, 2)]
            layouts[chunk] += [[(1, 0, rows)], [(2, 0, rows)]]
        elif direct:
            near, far = ordered(held[chunk][1], held[chunk][2])
            near, far = near[: rows // 2], far[rows // 2 :]
            mark(near, far)
            held[chunk] += [across_chips(near, 2), across_chips(far, 1)]
            layouts[chunk] += [[(3, 0, rows // 2)], [(3, rows // 2, rows // 2)]]
        else:
            bit = chip_bits[number]
            send = jnp.concatenate(ordered(*held[chunk]), axis=0)
            mark(send)
            held[chunk].append(across_chips(send, bit))
            layouts[chunk].append([(k | bit, 0, rows) for k in range(bit)])

    def split_step(half):
        *factors[half], done = split(*ordered(integrals if half == 0 else swapped))
        mark(done)

    def multiply(unit):
        chunk, halves = UNITS[unit]
        partials = product(
            ordered(*held[chunk]),
            layouts[chunk],
            targets,
            [factors[half] for half in halves],
            place,
            pattern,
            block_order,
        )
        mark(*partials)
        state[unit] = {0: partials}

    def exchange_step(unit, bit):
        names = list(state[unit])
        if bit == chip_bits[0]:
            keep, leave = [state[unit][0][0]], ordered(state[unit][0][1])
        else:
            values = ordered(*state[unit].values())
            half = values[0].shape[0] // 2
            keep = [value[:half] for value in values]
            leave = [value[half:] for value in values]
        send = jnp.concatenate(leave, axis=0)
        mark(send)
        arrived = across_chips(send, bit)
        half = keep[0].shape[0]
        state[unit] = dict(zip(names, keep))
        for n, s in enumerate(names):
            state[unit][s | bit] = arrived[n * half : (n + 1) * half]

    def reduce_step(unit, bit, narrow_bit):
        now = dict(zip(state[unit], ordered(*state[unit].values())))
        same = ((chip // bit) & 1) == ((z // narrow_bit) & 1)
        names = [s for s in now if not s & bit]
        send = jnp.concatenate([jnp.where(same, now[s | bit], now[s]) for s in names], axis=0)
        mark(send)
        arrived = along(send, narrow_bit)
        size = now[0].shape[0]
        final = narrow_bit == narrow_bits[-1]
        state[unit] = {}
        for n, s in enumerate(names):
            kept = jnp.where(same, now[s], now[s | bit])
            came = arrived[n * size : (n + 1) * size]
            state[unit][s] = (kept, came) if final else kept + came

    def land(unit):
        names = list(state[unit])
        values = ordered(*[value for name in names for value in state[unit][name]])
        mark(values[-1])
        state[unit] = {name: (values[2 * n], values[2 * n + 1]) for n, name in enumerate(names)}

    steps = []
    for bit in chip_bits:
        if bit < group:
            steps.append(functools.partial(exchange_step, bit=bit))
    for narrow_bit in narrow_bits:
        bit = group * narrow_bit
        steps.append(functools.partial(exchange_step, bit=bit))
        steps.append(functools.partial(reduce_step, bit=bit, narrow_bit=narrow_bit))
    steps.append(land)

    def send_step(unit):
        multiply(unit)
        steps[0](unit)

    if chips == 4 and narrow_count == 4:
        actions = dict(s=spread_step, p=pack_step, f=split_step, g=gather_step, e=send_step)
        actions.update(r=steps[1], x=steps[2], z=steps[3], l=steps[4])
        for name in ORDER:
            actions[name[0]](*[int(number) for number in name[1:]])
    else:
        for half in range(CORES):
            split_step(half)
        for g in range(len(GROUPS)):
            spread_step(g)
            pack_step(g)
        for chunk in range(CHUNKS):
            for number in range(len(chip_bits)):
                gather_step(chunk, number)
        for tick in range(len(UNITS) + len(steps) - 1):
            if tick < len(UNITS):
                send_step(tick)
            for number in range(len(steps) - 1, 0, -1):
                if 0 <= tick - number < len(UNITS):
                    steps[number](tick - number)

    spec = [(*UNITS[unit], s) for unit in range(len(UNITS)) for s in range(group)]
    pairs = [state[unit][s] for unit in range(len(UNITS)) for s in range(group)]
    return finish(
        spec,
        pairs,
        group,
        narrow_count,
        part,
        columns_local,
        place,
        bare_terms,
        occ_gap,
        virt_gap,
    )


def solution(mesh):
    placed = (
        P(("wide", "narrow"), None),
        P("narrow", "wide"),
        P("wide", "narrow"),
        P(),
        P(),
        P("wide"),
        P("narrow"),
    )
    return jax.shard_map(
        shards, mesh=mesh, in_specs=placed, out_specs=P("wide", "narrow"), check_vma=False
    )
```

```python
import functools

import jax
import jax.numpy as jnp
from jax import lax
from jax.experimental import pallas as pl
from jax.experimental.pallas import tpu as pltpu
from jax.sharding import PartitionSpec as P

TILE = 128
CHUNKS = 4
CORES = 2
GROUPS = ((0,), (1,), (2, 3))
UNITS = tuple((chunk, (half,)) for chunk in range(CHUNKS) for half in range(CORES))

ORDER = (
    "s0", "s1", "p0", "g00", "p1", "g01", "g10", "s2", "f0", "e0", "g11", "f1", "e1", "r0",
    "p2", "g20", "e2", "x0", "r1", "g21", "g30", "z0", "r2", "x1", "e3", "g31", "e4", "z1",
    "x2", "r3", "l0", "e5", "r4", "l1", "e7", "z2", "x3", "r5", "e6", "z3", "r7", "x4", "l2",
    "x5", "z4", "r6", "l3", "z5", "x7", "l4", "z7", "x6", "l5", "z6", "l7", "l6",
)

SMEM = pl.BlockSpec(memory_space=pltpu.SMEM)
VMEM = pl.BlockSpec(memory_space=pltpu.VMEM)
HBM = pl.BlockSpec(memory_space=pltpu.HBM)
SMALL = pl.CostEstimate(flops=1, bytes_accessed=1, transcendentals=0)


def after(value, *others):
    return lax.optimization_barrier((value, *others))[0]


def cut_kernel(count, bounds, place_ref, whole_ref, *outs):
    z = place_ref[2]
    depth = outs[0].shape[1]
    for g, (low, high) in enumerate(bounds):
        for m in range(count):
            start = pl.multiple_of((z ^ m) * depth, depth)
            outs[g * count + m][...] = whole_ref[low:high, pl.ds(start, depth)]


def cut(whole, count, depth, part, place):
    bounds = [(group[0] * part, (group[-1] + 1) * part) for group in GROUPS]
    shapes = [
        jax.ShapeDtypeStruct((high - low, depth), whole.dtype)
        for low, high in bounds
        for _ in range(count)
    ]
    outs = pl.pallas_call(
        functools.partial(cut_kernel, count, bounds),
        in_specs=[SMEM, VMEM],
        out_specs=[VMEM] * len(shapes),
        out_shape=shapes,
        cost_estimate=SMALL,
        compiler_params=pltpu.CompilerParams(vmem_limit_bytes=2**20),
        name="cut",
    )(place, whole)
    return [outs[g * count : (g + 1) * count] for g in range(len(bounds))]


def pack_kernel(count, part, place_ref, *refs):
    z = place_ref[2]
    for c, out in enumerate(refs[count:]):
        for m in range(count):
            rows = pl.ds(pl.multiple_of((z ^ m) * part, part), part)
            out[rows, :] = refs[m][c * part : (c + 1) * part, :]


def pack(blocks, part, place):
    count = len(blocks)
    rows, depth = blocks[0].shape
    shape = jax.ShapeDtypeStruct((count * part, depth), blocks[0].dtype)
    return pl.pallas_call(
        functools.partial(pack_kernel, count, part),
        in_specs=[SMEM] + [VMEM] * count,
        out_specs=[VMEM] * (rows // part),
        out_shape=[shape] * (rows // part),
        cost_estimate=SMALL,
        compiler_params=pltpu.CompilerParams(vmem_limit_bytes=2**20),
        name="pack",
    )(place, *blocks)


def split_kernel(step, whole_ref, high_ref, low_ref, token_ref, buffer, sems):
    count = whole_ref.shape[0] // step
    slots = buffer.shape[0]

    def copy(i):
        return pltpu.make_async_copy(
            whole_ref.at[pl.ds(i * step, step)], buffer.at[i % slots], sems.at[i % slots]
        )

    for i in range(min(slots, count)):
        copy(i).start()
    token_ref[...] = jnp.zeros_like(token_ref)
    for i in range(count):
        copy(i).wait()
        whole = buffer[i % slots]
        high = whole.astype(jnp.bfloat16)
        here = slice(i * step, (i + 1) * step)
        high_ref[here, :] = high
        low_ref[here, :] = (whole - high.astype(jnp.float32)).astype(jnp.bfloat16)
        if i + slots < count:
            copy(i + slots).start()


def split(whole, limit):
    rows, columns = whole.shape
    step = min(128, rows)
    slots = min(8, rows // step)
    half = jax.ShapeDtypeStruct((rows, columns), jnp.bfloat16)
    return pl.pallas_call(
        functools.partial(split_kernel, step),
        in_specs=[HBM],
        out_specs=[VMEM, VMEM, VMEM],
        out_shape=[half, half, jax.ShapeDtypeStruct((8, 128), jnp.float32)],
        scratch_shapes=[
            pltpu.VMEM((slots, step, columns), jnp.float32),
            pltpu.SemaphoreType.DMA((slots,)),
        ],
        cost_estimate=SMALL,
        compiler_params=pltpu.CompilerParams(vmem_limit_bytes=limit * 2**20),
        name="split",
    )(whole)


def product_kernel(count, rows, layout, targets, halves, place_ref, pattern_ref, order_ref, *refs):
    lefts = refs[: len(layout)]
    factors = refs[len(layout) : len(layout) + 2 * halves]
    outs = refs[len(layout) + 2 * halves : -1]
    left = refs[-1]
    depth = lefts[0].shape[1]
    total = count * rows
    chip, core, z = place_ref[0], place_ref[1], place_ref[2]
    tiles = depth // TILE
    for held, pieces in zip(lefts, layout):
        start = 0
        for k, first, size in pieces:
            kind = order_ref[(chip ^ k) * CORES + core]
            high_rows = slice(k * rows + first, k * rows + first + size)
            low_rows = slice(total + k * rows + first, total + k * rows + first + size)
            for t in range(tiles):
                kept = pattern_ref[kind, z * tiles + t].astype(jnp.float32)
                here = slice(t * TILE, (t + 1) * TILE)
                value = held[start : start + size, here] * kept
                high = value.astype(jnp.bfloat16)
                left[high_rows, here] = high
                left[low_rows, here] = (value - high.astype(jnp.float32)).astype(jnp.bfloat16)
            start += size
    columns = factors[0].shape[1]
    width = min(512, columns)
    for half in range(halves):
        high_ref, low_ref = factors[2 * half : 2 * half + 2]
        for j in range(columns // width):
            here = slice(j * width, (j + 1) * width)
            both = jnp.dot(left[...], high_ref[:, here], preferred_element_type=jnp.float32)
            small = jnp.dot(
                left[:total, :], low_ref[:, here], preferred_element_type=jnp.float32
            )
            result = both[:total] + (both[total:] + small)
            there = slice(half * columns + j * width, half * columns + (j + 1) * width)
            for out, blocks in zip(outs, targets):
                for n, k in enumerate(blocks):
                    out[n * rows : (n + 1) * rows, there] = result[k * rows : (k + 1) * rows]


def product(lefts, layout, targets, factors, place, pattern, block_order):
    rows, depth = lefts[0].shape
    count = sum(held.shape[0] for held in lefts) // rows
    halves = len(factors)
    columns = factors[0][0].shape[1]
    total = count * rows
    return pl.pallas_call(
        functools.partial(product_kernel, count, rows, layout, targets, halves),
        in_specs=[SMEM] * 3 + [VMEM] * (len(lefts) + 2 * halves),
        out_specs=[VMEM] * len(targets),
        out_shape=[
            jax.ShapeDtypeStruct((len(blocks) * rows, halves * columns), jnp.float32)
            for blocks in targets
        ],
        scratch_shapes=[pltpu.VMEM((2 * total, depth), jnp.bfloat16)],
        cost_estimate=pl.CostEstimate(
            flops=12 * total * depth * halves * columns, bytes_accessed=1, transcendentals=0
        ),
        compiler_params=pltpu.CompilerParams(vmem_limit_bytes=8 * total * depth + 3 * 2**20),
        name="product",
    )(place, pattern, block_order, *lefts, *[part for pair in factors for part in pair])


def finish_kernel(spec, group, count, part, width, place_ref, bare_ref, occ_ref, virt_ref, *refs):
    out_ref = refs[-1]
    chip, core = place_ref[0], place_ref[1]
    rows_local = CHUNKS * part
    for number, (chunk, halves, s) in enumerate(spec):
        kept, arrived = refs[2 * number], refs[2 * number + 1]
        for position, half in enumerate(halves):
            column = (((chip % group) ^ s) * CORES + (half ^ core)) * width
            columns = pl.ds(pl.multiple_of(column, width), width)
            here = slice(position * width, (position + 1) * width)
            for m in range(count):
                rows = slice(m * rows_local + chunk * part, m * rows_local + (chunk + 1) * part)
                block = slice(m * part, (m + 1) * part)
                ladder = kept[block, here] + arrived[block, here]
                gap = occ_ref[rows, :] + virt_ref[:, columns]
                out_ref[rows, columns] = -(bare_ref[rows, columns] + ladder) / gap


def finish(spec, pairs, group, count, part, width, place, bare, occ, virt):
    return pl.pallas_call(
        functools.partial(finish_kernel, spec, group, count, part, width),
        in_specs=[SMEM] + [VMEM] * (3 + 2 * len(pairs)),
        out_specs=VMEM,
        out_shape=jax.ShapeDtypeStruct(bare.shape, bare.dtype),
        cost_estimate=SMALL,
        compiler_params=pltpu.CompilerParams(vmem_limit_bytes=2 * 2**20),
        name="finish",
    )(place, bare, occ[:, None], virt[None, :], *[part_in for pair in pairs for part_in in pair])


def shards(amplitudes, integrals, bare_terms, pattern, block_order, occ_gap, virt_gap):
    rows_local, columns = amplitudes.shape
    depth, columns_local = integrals.shape
    wide_count = lax.axis_size("wide")
    narrow_count = lax.axis_size("narrow")
    chips = wide_count // CORES
    wide = lax.axis_index("wide")
    z = lax.axis_index("narrow")
    chip = wide // CORES
    core = wide % CORES
    part = rows_local // CHUNKS
    rows = narrow_count * part
    group = chips // narrow_count
    place = jnp.stack([chip, core, z]).astype(jnp.int32)
    chip_bits = [1 << b for b in range(chips.bit_length() - 1)]
    narrow_bits = [1 << b for b in range(narrow_count.bit_length() - 1)]
    targets = [list(range(chips))]
    for bit in reversed(chip_bits):
        targets = [[k for k in targets[0] if not k & bit] + [k for k in targets[0] if k & bit]]
    targets = [targets[0][: chips // 2], targets[0][chips // 2 :]]

    def across(value, mask):
        return lax.ppermute(value, "wide", [(w, w ^ mask) for w in range(wide_count)])

    def across_chips(value, mask):
        return across(value, mask * CORES)

    def along(value, mask):
        return lax.ppermute(value, "narrow", [(n, n ^ mask) for n in range(narrow_count)])

    last = []

    def ordered(*values):
        return list(lax.optimization_barrier((*values, *last))[: len(values)])

    def mark(*values):
        last[:] = values

    swapped = across(integrals, 1)
    pieces = cut(amplitudes, narrow_count, depth, part, place)
    spread = {}
    mine = {}
    held = {}
    layouts = {}
    factors = {}
    state = {}

    def spread_step(g):
        sends = ordered(*pieces[g][1:])
        mark(*sends)
        spread[g] = [pieces[g][0]] + [along(send, n + 1) for n, send in enumerate(sends)]

    def pack_step(g):
        packed = pack(ordered(*spread[g]), part, place)
        mark(*packed)
        mine.update(zip(GROUPS[g], packed))

    def gather_step(chunk, number):
        if number == 0:
            held[chunk] = [mine[chunk]]
            layouts[chunk] = [[(0, 0, rows)]]
        direct = chunk == 0 and chips == 4
        if direct and number == 0:
            (send,) = ordered(mine[chunk])
            mark(send)
            held[chunk] += [across_chips(send, 1), across_chips(send, 2)]
            layouts[chunk] += [[(1, 0, rows)], [(2, 0, rows)]]
        elif direct:
            near, far = ordered(held[chunk][1], held[chunk][2])
            near, far = near[: rows // 2], far[rows // 2 :]
            mark(near, far)
            held[chunk] += [across_chips(near, 2), across_chips(far, 1)]
            layouts[chunk] += [[(3, 0, rows // 2)], [(3, rows // 2, rows // 2)]]
        else:
            bit = chip_bits[number]
            send = jnp.concatenate(ordered(*held[chunk]), axis=0)
            mark(send)
            held[chunk].append(across_chips(send, bit))
            layouts[chunk].append([(k | bit, 0, rows) for k in range(bit)])

    def split_step(half):
        source, limit = ((integrals, 42), (swapped, 6))[half]
        *factors[half], done = split(*ordered(source), limit)
        mark(done)

    def multiply(unit):
        chunk, halves = UNITS[unit]
        partials = product(
            ordered(*held[chunk]),
            layouts[chunk],
            targets,
            [factors[half] for half in halves],
            place,
            pattern,
            block_order,
        )
        mark(*partials)
        state[unit] = {0: partials}

    def exchange_step(unit, bit):
        names = list(state[unit])
        if bit == chip_bits[0]:
            keep, leave = [state[unit][0][0]], ordered(state[unit][0][1])
        else:
            values = ordered(*state[unit].values())
            half = values[0].shape[0] // 2
            keep = [value[:half] for value in values]
            leave = [value[half:] for value in values]
        send = jnp.concatenate(leave, axis=0)
        mark(send)
        arrived = across_chips(send, bit)
        half = keep[0].shape[0]
        state[unit] = dict(zip(names, keep))
        for n, s in enumerate(names):
            state[unit][s | bit] = arrived[n * half : (n + 1) * half]

    def reduce_step(unit, bit, narrow_bit):
        now = dict(zip(state[unit], ordered(*state[unit].values())))
        same = ((chip // bit) & 1) == ((z // narrow_bit) & 1)
        names = [s for s in now if not s & bit]
        send = jnp.concatenate([jnp.where(same, now[s | bit], now[s]) for s in names], axis=0)
        mark(send)
        arrived = along(send, narrow_bit)
        size = now[0].shape[0]
        final = narrow_bit == narrow_bits[-1]
        state[unit] = {}
        for n, s in enumerate(names):
            kept = jnp.where(same, now[s], now[s | bit])
            came = arrived[n * size : (n + 1) * size]
            state[unit][s] = (kept, came) if final else kept + came

    def land(unit):
        names = list(state[unit])
        values = ordered(*[value for name in names for value in state[unit][name]])
        mark(values[-1])
        state[unit] = {name: (values[2 * n], values[2 * n + 1]) for n, name in enumerate(names)}

    steps = []
    for bit in chip_bits:
        if bit < group:
            steps.append(functools.partial(exchange_step, bit=bit))
    for narrow_bit in narrow_bits:
        bit = group * narrow_bit
        steps.append(functools.partial(exchange_step, bit=bit))
        steps.append(functools.partial(reduce_step, bit=bit, narrow_bit=narrow_bit))
    steps.append(land)

    def send_step(unit):
        multiply(unit)
        steps[0](unit)

    if chips == 4 and narrow_count == 4:
        actions = dict(s=spread_step, p=pack_step, f=split_step, g=gather_step, e=send_step)
        actions.update(r=steps[1], x=steps[2], z=steps[3], l=steps[4])
        for name in ORDER:
            actions[name[0]](*[int(number) for number in name[1:]])
    else:
        for half in range(CORES):
            split_step(half)
        for g in range(len(GROUPS)):
            spread_step(g)
            pack_step(g)
        for chunk in range(CHUNKS):
            for number in range(len(chip_bits)):
                gather_step(chunk, number)
        for tick in range(len(UNITS) + len(steps) - 1):
            if tick < len(UNITS):
                send_step(tick)
            for number in range(len(steps) - 1, 0, -1):
                if 0 <= tick - number < len(UNITS):
                    steps[number](tick - number)

    spec = [(*UNITS[unit], s) for unit in range(len(UNITS)) for s in range(group)]
    pairs = [state[unit][s] for unit in range(len(UNITS)) for s in range(group)]
    return finish(
        spec,
        pairs,
        group,
        narrow_count,
        part,
        columns_local,
        place,
        bare_terms,
        occ_gap,
        virt_gap,
    )


def solution(mesh):
    placed = (
        P(("wide", "narrow"), None),
        P("narrow", "wide"),
        P("wide", "narrow"),
        P(),
        P(),
        P("wide"),
        P("narrow"),
    )
    return jax.shard_map(
        shards, mesh=mesh, in_specs=placed, out_specs=P("wide", "narrow"), check_vma=False
    )
```

```python
import functools

import jax
import jax.numpy as jnp
from jax import lax
from jax.experimental import pallas as pl
from jax.experimental.pallas import tpu as pltpu
from jax.sharding import PartitionSpec as P

TILE = 128
CHUNKS = 4
CORES = 2
DIRECT = (0,)
GROUPS = ((0,), (1,), (2, 3))
UNITS = tuple((chunk, (half,)) for chunk in range(CHUNKS) for half in range(CORES))

ORDER = (
    "s0", "s1", "p0", "g00", "p1", "g10", "s2", "f0", "e0", "f1", "e1", "g11", "r0", "p2",
    "g20", "g30", "r1", "x0", "g21", "e3", "z0", "x1", "e2", "g31", "r3", "l0", "e4", "z1",
    "r2", "e5", "x3", "r4", "l1", "e7", "z3", "x2", "r5", "e6", "z2", "x4", "l3", "r7", "x5",
    "z4", "r6", "z5", "x7", "l4", "l2", "x6", "z7", "l5", "z6", "l7", "l6",
)

SMEM = pl.BlockSpec(memory_space=pltpu.SMEM)
VMEM = pl.BlockSpec(memory_space=pltpu.VMEM)
HBM = pl.BlockSpec(memory_space=pltpu.HBM)
SMALL = pl.CostEstimate(flops=1, bytes_accessed=1, transcendentals=0)


def after(value, *others):
    return lax.optimization_barrier((value, *others))[0]


def cut_kernel(count, bounds, place_ref, whole_ref, *outs):
    z = place_ref[2]
    depth = outs[0].shape[1]
    for g, (low, high) in enumerate(bounds):
        for m in range(count):
            start = pl.multiple_of((z ^ m) * depth, depth)
            outs[g * count + m][...] = whole_ref[low:high, pl.ds(start, depth)]


def cut(whole, count, depth, part, place):
    bounds = [(group[0] * part, (group[-1] + 1) * part) for group in GROUPS]
    shapes = [
        jax.ShapeDtypeStruct((high - low, depth), whole.dtype)
        for low, high in bounds
        for _ in range(count)
    ]
    outs = pl.pallas_call(
        functools.partial(cut_kernel, count, bounds),
        in_specs=[SMEM, VMEM],
        out_specs=[VMEM] * len(shapes),
        out_shape=shapes,
        cost_estimate=SMALL,
        compiler_params=pltpu.CompilerParams(vmem_limit_bytes=2**20),
        name="cut",
    )(place, whole)
    return [outs[g * count : (g + 1) * count] for g in range(len(bounds))]


def pack_kernel(count, part, place_ref, *refs):
    z = place_ref[2]
    for c, out in enumerate(refs[count:]):
        for m in range(count):
            rows = pl.ds(pl.multiple_of((z ^ m) * part, part), part)
            out[rows, :] = refs[m][c * part : (c + 1) * part, :]


def pack(blocks, part, place):
    count = len(blocks)
    rows, depth = blocks[0].shape
    shape = jax.ShapeDtypeStruct((count * part, depth), blocks[0].dtype)
    return pl.pallas_call(
        functools.partial(pack_kernel, count, part),
        in_specs=[SMEM] + [VMEM] * count,
        out_specs=[VMEM] * (rows // part),
        out_shape=[shape] * (rows // part),
        cost_estimate=SMALL,
        compiler_params=pltpu.CompilerParams(vmem_limit_bytes=2**20),
        name="pack",
    )(place, *blocks)


def split_kernel(step, whole_ref, high_ref, low_ref, token_ref, buffer, sems):
    count = whole_ref.shape[0] // step
    slots = buffer.shape[0]

    def copy(i):
        return pltpu.make_async_copy(
            whole_ref.at[pl.ds(i * step, step)], buffer.at[i % slots], sems.at[i % slots]
        )

    for i in range(min(slots, count)):
        copy(i).start()
    token_ref[...] = jnp.zeros_like(token_ref)
    for i in range(count):
        copy(i).wait()
        whole = buffer[i % slots]
        high = whole.astype(jnp.bfloat16)
        here = slice(i * step, (i + 1) * step)
        high_ref[here, :] = high
        low_ref[here, :] = (whole - high.astype(jnp.float32)).astype(jnp.bfloat16)
        if i + slots < count:
            copy(i + slots).start()


def split(whole, limit):
    rows, columns = whole.shape
    step = min(128, rows)
    slots = min(8, rows // step)
    half = jax.ShapeDtypeStruct((rows, columns), jnp.bfloat16)
    return pl.pallas_call(
        functools.partial(split_kernel, step),
        in_specs=[HBM],
        out_specs=[VMEM, VMEM, VMEM],
        out_shape=[half, half, jax.ShapeDtypeStruct((8, 128), jnp.float32)],
        scratch_shapes=[
            pltpu.VMEM((slots, step, columns), jnp.float32),
            pltpu.SemaphoreType.DMA((slots,)),
        ],
        cost_estimate=SMALL,
        compiler_params=pltpu.CompilerParams(vmem_limit_bytes=limit * 2**20),
        name="split",
    )(whole)


def product_kernel(count, rows, layout, targets, halves, place_ref, pattern_ref, order_ref, *refs):
    lefts = refs[: len(layout)]
    factors = refs[len(layout) : len(layout) + 2 * halves]
    outs = refs[len(layout) + 2 * halves : -1]
    left = refs[-1]
    depth = lefts[0].shape[1]
    total = count * rows
    chip, core, z = place_ref[0], place_ref[1], place_ref[2]
    tiles = depth // TILE
    for held, pieces in zip(lefts, layout):
        start = 0
        for k, first, size in pieces:
            kind = order_ref[(chip ^ k) * CORES + core]
            high_rows = slice(k * rows + first, k * rows + first + size)
            low_rows = slice(total + k * rows + first, total + k * rows + first + size)
            for t in range(tiles):
                kept = pattern_ref[kind, z * tiles + t].astype(jnp.float32)
                here = slice(t * TILE, (t + 1) * TILE)
                value = held[start : start + size, here] * kept
                high = value.astype(jnp.bfloat16)
                left[high_rows, here] = high
                left[low_rows, here] = (value - high.astype(jnp.float32)).astype(jnp.bfloat16)
            start += size
    columns = factors[0].shape[1]
    width = min(512, columns)
    for half in range(halves):
        high_ref, low_ref = factors[2 * half : 2 * half + 2]
        for j in range(columns // width):
            here = slice(j * width, (j + 1) * width)
            both = jnp.dot(left[...], high_ref[:, here], preferred_element_type=jnp.float32)
            small = jnp.dot(
                left[:total, :], low_ref[:, here], preferred_element_type=jnp.float32
            )
            result = both[:total] + (both[total:] + small)
            there = slice(half * columns + j * width, half * columns + (j + 1) * width)
            for out, blocks in zip(outs, targets):
                for n, k in enumerate(blocks):
                    out[n * rows : (n + 1) * rows, there] = result[k * rows : (k + 1) * rows]


def product(lefts, layout, targets, factors, place, pattern, block_order):
    rows, depth = lefts[0].shape
    count = sum(held.shape[0] for held in lefts) // rows
    halves = len(factors)
    columns = factors[0][0].shape[1]
    total = count * rows
    return pl.pallas_call(
        functools.partial(product_kernel, count, rows, layout, targets, halves),
        in_specs=[SMEM] * 3 + [VMEM] * (len(lefts) + 2 * halves),
        out_specs=[VMEM] * len(targets),
        out_shape=[
            jax.ShapeDtypeStruct((len(blocks) * rows, halves * columns), jnp.float32)
            for blocks in targets
        ],
        scratch_shapes=[pltpu.VMEM((2 * total, depth), jnp.bfloat16)],
        cost_estimate=pl.CostEstimate(
            flops=12 * total * depth * halves * columns, bytes_accessed=1, transcendentals=0
        ),
        compiler_params=pltpu.CompilerParams(vmem_limit_bytes=8 * total * depth + 3 * 2**20),
        name="product",
    )(place, pattern, block_order, *lefts, *[part for pair in factors for part in pair])


def finish_kernel(spec, group, count, part, width, place_ref, bare_ref, occ_ref, virt_ref, *refs):
    out_ref = refs[-1]
    chip, core = place_ref[0], place_ref[1]
    rows_local = CHUNKS * part
    for number, (chunk, halves, s) in enumerate(spec):
        kept, arrived = refs[2 * number], refs[2 * number + 1]
        for position, half in enumerate(halves):
            column = (((chip % group) ^ s) * CORES + (half ^ core)) * width
            columns = pl.ds(pl.multiple_of(column, width), width)
            here = slice(position * width, (position + 1) * width)
            for m in range(count):
                rows = slice(m * rows_local + chunk * part, m * rows_local + (chunk + 1) * part)
                block = slice(m * part, (m + 1) * part)
                ladder = kept[block, here] + arrived[block, here]
                gap = occ_ref[rows, :] + virt_ref[:, columns]
                out_ref[rows, columns] = -(bare_ref[rows, columns] + ladder) / gap


def finish(spec, pairs, group, count, part, width, place, bare, occ, virt):
    return pl.pallas_call(
        functools.partial(finish_kernel, spec, group, count, part, width),
        in_specs=[SMEM] + [VMEM] * (3 + 2 * len(pairs)),
        out_specs=VMEM,
        out_shape=jax.ShapeDtypeStruct(bare.shape, bare.dtype),
        cost_estimate=SMALL,
        compiler_params=pltpu.CompilerParams(vmem_limit_bytes=2 * 2**20),
        name="finish",
    )(place, bare, occ[:, None], virt[None, :], *[part_in for pair in pairs for part_in in pair])


def shards(amplitudes, integrals, bare_terms, pattern, block_order, occ_gap, virt_gap):
    rows_local, columns = amplitudes.shape
    depth, columns_local = integrals.shape
    wide_count = lax.axis_size("wide")
    narrow_count = lax.axis_size("narrow")
    chips = wide_count // CORES
    wide = lax.axis_index("wide")
    z = lax.axis_index("narrow")
    chip = wide // CORES
    core = wide % CORES
    part = rows_local // CHUNKS
    rows = narrow_count * part
    group = chips // narrow_count
    place = jnp.stack([chip, core, z]).astype(jnp.int32)
    chip_bits = [1 << b for b in range(chips.bit_length() - 1)]
    narrow_bits = [1 << b for b in range(narrow_count.bit_length() - 1)]
    targets = [list(range(chips))]
    for bit in reversed(chip_bits):
        targets = [[k for k in targets[0] if not k & bit] + [k for k in targets[0] if k & bit]]
    targets = [targets[0][: chips // 2], targets[0][chips // 2 :]]

    def across(value, mask):
        return lax.ppermute(value, "wide", [(w, w ^ mask) for w in range(wide_count)])

    def across_chips(value, mask):
        return across(value, mask * CORES)

    def along(value, mask):
        return lax.ppermute(value, "narrow", [(n, n ^ mask) for n in range(narrow_count)])

    last = []

    def ordered(*values):
        return list(lax.optimization_barrier((*values, *last))[: len(values)])

    def mark(*values):
        last[:] = values

    swapped = across(integrals, 1)
    pieces = cut(amplitudes, narrow_count, depth, part, place)
    spread = {}
    mine = {}
    held = {}
    layouts = {}
    factors = {}
    state = {}

    def spread_step(g):
        sends = ordered(*pieces[g][1:])
        mark(*sends)
        spread[g] = [pieces[g][0]] + [along(send, n + 1) for n, send in enumerate(sends)]

    def pack_step(g):
        packed = pack(ordered(*spread[g]), part, place)
        mark(*packed)
        mine.update(zip(GROUPS[g], packed))

    def gather_step(chunk, number):
        if number == 0:
            held[chunk] = [mine[chunk]]
            layouts[chunk] = [[(0, 0, rows)]]
        if chunk in DIRECT and chips == 4:
            (send,) = ordered(mine[chunk])
            mark(send)
            held[chunk] += [across_chips(send, k) for k in (3, 1, 2)]
            layouts[chunk] += [[(k, 0, rows)] for k in (3, 1, 2)]
        else:
            bit = chip_bits[number]
            send = jnp.concatenate(ordered(*held[chunk]), axis=0)
            mark(send)
            held[chunk].append(across_chips(send, bit))
            layouts[chunk].append([(k | bit, 0, rows) for k in range(bit)])

    def split_step(half):
        source, limit = ((integrals, 42), (swapped, 6))[half]
        *factors[half], done = split(*ordered(source), limit)
        mark(done)

    def multiply(unit):
        chunk, halves = UNITS[unit]
        partials = product(
            ordered(*held[chunk]),
            layouts[chunk],
            targets,
            [factors[half] for half in halves],
            place,
            pattern,
            block_order,
        )
        mark(*partials)
        state[unit] = {0: partials}

    def exchange_step(unit, bit):
        names = list(state[unit])
        if bit == chip_bits[0]:
            keep, leave = [state[unit][0][0]], ordered(state[unit][0][1])
        else:
            values = ordered(*state[unit].values())
            half = values[0].shape[0] // 2
            keep = [value[:half] for value in values]
            leave = [value[half:] for value in values]
        send = jnp.concatenate(leave, axis=0)
        mark(send)
        arrived = across_chips(send, bit)
        half = keep[0].shape[0]
        state[unit] = dict(zip(names, keep))
        for n, s in enumerate(names):
            state[unit][s | bit] = arrived[n * half : (n + 1) * half]

    def reduce_step(unit, bit, narrow_bit):
        now = dict(zip(state[unit], ordered(*state[unit].values())))
        same = ((chip // bit) & 1) == ((z // narrow_bit) & 1)
        names = [s for s in now if not s & bit]
        send = jnp.concatenate([jnp.where(same, now[s | bit], now[s]) for s in names], axis=0)
        mark(send)
        arrived = along(send, narrow_bit)
        size = now[0].shape[0]
        final = narrow_bit == narrow_bits[-1]
        state[unit] = {}
        for n, s in enumerate(names):
            kept = jnp.where(same, now[s], now[s | bit])
            came = arrived[n * size : (n + 1) * size]
            state[unit][s] = (kept, came) if final else kept + came

    def land(unit):
        names = list(state[unit])
        values = ordered(*[value for name in names for value in state[unit][name]])
        mark(values[-1])
        state[unit] = {name: (values[2 * n], values[2 * n + 1]) for n, name in enumerate(names)}

    steps = []
    for bit in chip_bits:
        if bit < group:
            steps.append(functools.partial(exchange_step, bit=bit))
    for narrow_bit in narrow_bits:
        bit = group * narrow_bit
        steps.append(functools.partial(exchange_step, bit=bit))
        steps.append(functools.partial(reduce_step, bit=bit, narrow_bit=narrow_bit))
    steps.append(land)

    def send_step(unit):
        multiply(unit)
        steps[0](unit)

    if chips == 4 and narrow_count == 4:
        actions = dict(s=spread_step, p=pack_step, f=split_step, g=gather_step, e=send_step)
        actions.update(r=steps[1], x=steps[2], z=steps[3], l=steps[4])
        for name in ORDER:
            actions[name[0]](*[int(number) for number in name[1:]])
    else:
        for half in range(CORES):
            split_step(half)
        for g in range(len(GROUPS)):
            spread_step(g)
            pack_step(g)
        for chunk in range(CHUNKS):
            for number in range(len(chip_bits)):
                gather_step(chunk, number)
        for tick in range(len(UNITS) + len(steps) - 1):
            if tick < len(UNITS):
                send_step(tick)
            for number in range(len(steps) - 1, 0, -1):
                if 0 <= tick - number < len(UNITS):
                    steps[number](tick - number)

    spec = [(*UNITS[unit], s) for unit in range(len(UNITS)) for s in range(group)]
    pairs = [state[unit][s] for unit in range(len(UNITS)) for s in range(group)]
    return finish(
        spec,
        pairs,
        group,
        narrow_count,
        part,
        columns_local,
        place,
        bare_terms,
        occ_gap,
        virt_gap,
    )


def solution(mesh):
    placed = (
        P(("wide", "narrow"), None),
        P("narrow", "wide"),
        P("wide", "narrow"),
        P(),
        P(),
        P("wide"),
        P("narrow"),
    )
    return jax.shard_map(
        shards, mesh=mesh, in_specs=placed, out_specs=P("wide", "narrow"), check_vma=False
    )
```

```python
import functools

import jax
import jax.numpy as jnp
from jax import lax
from jax.experimental import pallas as pl
from jax.experimental.pallas import tpu as pltpu
from jax.sharding import PartitionSpec as P

TILE = 128
CHUNKS = 4
CORES = 2
DIRECT = (0,)
GROUPS = ((0,), (1,), (2, 3))
UNITS = tuple((chunk, (half,)) for chunk in range(CHUNKS) for half in range(CORES))

ORDER = (
    "s00", "s10", "s01", "s20", "s11", "p0", "g00", "s21", "p1", "g10", "f1", "e1", "p2",
    "g20", "g11", "f0", "e0", "g30", "g21", "r1", "r0", "e3", "x1", "e2", "x0", "z1", "r3",
    "g31", "e5", "r2", "z0", "e4", "x3", "l1", "r5", "e6", "z3", "x2", "r4", "l0", "e7", "z2",
    "x5", "l3", "r6", "z5", "x4", "l2", "r7", "x6", "z4", "x7", "z6", "l5", "z7", "l4", "l7",
    "l6",
)

SMEM = pl.BlockSpec(memory_space=pltpu.SMEM)
VMEM = pl.BlockSpec(memory_space=pltpu.VMEM)
HBM = pl.BlockSpec(memory_space=pltpu.HBM)
SMALL = pl.CostEstimate(flops=1, bytes_accessed=1, transcendentals=0)


def after(value, *others):
    return lax.optimization_barrier((value, *others))[0]


def cut_kernel(count, bounds, place_ref, whole_ref, *outs):
    z = place_ref[2]
    depth = outs[0].shape[1]
    for g, (low, high) in enumerate(bounds):
        size = high - low
        for m in range(count):
            start = pl.multiple_of((z ^ m) * depth, depth)
            here = slice(m // 2 * size, (m // 2 + 1) * size)
            outs[2 * g + m % 2][here, :] = whole_ref[low:high, pl.ds(start, depth)]


def cut(whole, count, depth, part, place):
    bounds = [(group[0] * part, (group[-1] + 1) * part) for group in GROUPS]
    shapes = [
        jax.ShapeDtypeStruct((count // 2 * (high - low), depth), whole.dtype)
        for low, high in bounds
        for _ in range(2)
    ]
    outs = pl.pallas_call(
        functools.partial(cut_kernel, count, bounds),
        in_specs=[SMEM, VMEM],
        out_specs=[VMEM] * len(shapes),
        out_shape=shapes,
        cost_estimate=SMALL,
        compiler_params=pltpu.CompilerParams(vmem_limit_bytes=2**20),
        name="cut",
    )(place, whole)
    return [outs[2 * g : 2 * g + 2] for g in range(len(bounds))]


def pack_kernel(part, starts, place_ref, *refs):
    z = place_ref[2]
    count = len(starts)
    for c, out in enumerate(refs[count:]):
        for m in range(count):
            rows = pl.ds(pl.multiple_of((z ^ m) * part, part), part)
            first = starts[m] + c * part
            out[rows, :] = refs[m][first : first + part, :]


def pack(blocks, starts, chunks, part, place):
    count = len(blocks)
    shape = jax.ShapeDtypeStruct((count * part, blocks[0].shape[1]), blocks[0].dtype)
    return pl.pallas_call(
        functools.partial(pack_kernel, part, starts),
        in_specs=[SMEM] + [VMEM] * count,
        out_specs=[VMEM] * chunks,
        out_shape=[shape] * chunks,
        cost_estimate=SMALL,
        compiler_params=pltpu.CompilerParams(vmem_limit_bytes=2**20),
        name="pack",
    )(place, *blocks)


def split_kernel(step, whole_ref, high_ref, low_ref, token_ref, buffer, sems):
    count = whole_ref.shape[0] // step
    slots = buffer.shape[0]

    def copy(i):
        return pltpu.make_async_copy(
            whole_ref.at[pl.ds(i * step, step)], buffer.at[i % slots], sems.at[i % slots]
        )

    for i in range(min(slots, count)):
        copy(i).start()
    token_ref[...] = jnp.zeros_like(token_ref)
    for i in range(count):
        copy(i).wait()
        whole = buffer[i % slots]
        high = whole.astype(jnp.bfloat16)
        here = slice(i * step, (i + 1) * step)
        high_ref[here, :] = high
        low_ref[here, :] = (whole - high.astype(jnp.float32)).astype(jnp.bfloat16)
        if i + slots < count:
            copy(i + slots).start()


def split(whole, limit):
    rows, columns = whole.shape
    step = min(128, rows)
    slots = min(8, rows // step)
    half = jax.ShapeDtypeStruct((rows, columns), jnp.bfloat16)
    return pl.pallas_call(
        functools.partial(split_kernel, step),
        in_specs=[HBM],
        out_specs=[VMEM, VMEM, VMEM],
        out_shape=[half, half, jax.ShapeDtypeStruct((8, 128), jnp.float32)],
        scratch_shapes=[
            pltpu.VMEM((slots, step, columns), jnp.float32),
            pltpu.SemaphoreType.DMA((slots,)),
        ],
        cost_estimate=SMALL,
        compiler_params=pltpu.CompilerParams(vmem_limit_bytes=limit * 2**20),
        name="split",
    )(whole)


def product_kernel(count, rows, layout, targets, halves, place_ref, pattern_ref, order_ref, *refs):
    lefts = refs[: len(layout)]
    factors = refs[len(layout) : len(layout) + 2 * halves]
    outs = refs[len(layout) + 2 * halves : -1]
    left = refs[-1]
    depth = lefts[0].shape[1]
    total = count * rows
    chip, core, z = place_ref[0], place_ref[1], place_ref[2]
    tiles = depth // TILE
    for held, pieces in zip(lefts, layout):
        start = 0
        for k, first, size in pieces:
            kind = order_ref[(chip ^ k) * CORES + core]
            high_rows = slice(k * rows + first, k * rows + first + size)
            low_rows = slice(total + k * rows + first, total + k * rows + first + size)
            for t in range(tiles):
                kept = pattern_ref[kind, z * tiles + t].astype(jnp.float32)
                here = slice(t * TILE, (t + 1) * TILE)
                value = held[start : start + size, here] * kept
                high = value.astype(jnp.bfloat16)
                left[high_rows, here] = high
                left[low_rows, here] = (value - high.astype(jnp.float32)).astype(jnp.bfloat16)
            start += size
    columns = factors[0].shape[1]
    width = min(512, columns)
    for half in range(halves):
        high_ref, low_ref = factors[2 * half : 2 * half + 2]
        for j in range(columns // width):
            here = slice(j * width, (j + 1) * width)
            both = jnp.dot(left[...], high_ref[:, here], preferred_element_type=jnp.float32)
            small = jnp.dot(
                left[:total, :], low_ref[:, here], preferred_element_type=jnp.float32
            )
            result = both[:total] + (both[total:] + small)
            there = slice(half * columns + j * width, half * columns + (j + 1) * width)
            for out, blocks in zip(outs, targets):
                for n, k in enumerate(blocks):
                    out[n * rows : (n + 1) * rows, there] = result[k * rows : (k + 1) * rows]


def product(lefts, layout, targets, factors, place, pattern, block_order):
    rows, depth = lefts[0].shape
    count = sum(held.shape[0] for held in lefts) // rows
    halves = len(factors)
    columns = factors[0][0].shape[1]
    total = count * rows
    return pl.pallas_call(
        functools.partial(product_kernel, count, rows, layout, targets, halves),
        in_specs=[SMEM] * 3 + [VMEM] * (len(lefts) + 2 * halves),
        out_specs=[VMEM] * len(targets),
        out_shape=[
            jax.ShapeDtypeStruct((len(blocks) * rows, halves * columns), jnp.float32)
            for blocks in targets
        ],
        scratch_shapes=[pltpu.VMEM((2 * total, depth), jnp.bfloat16)],
        cost_estimate=pl.CostEstimate(
            flops=12 * total * depth * halves * columns, bytes_accessed=1, transcendentals=0
        ),
        compiler_params=pltpu.CompilerParams(vmem_limit_bytes=8 * total * depth + 3 * 2**20),
        name="product",
    )(place, pattern, block_order, *lefts, *[part for pair in factors for part in pair])


def finish_kernel(spec, group, count, part, width, place_ref, bare_ref, occ_ref, virt_ref, *refs):
    out_ref = refs[-1]
    chip, core = place_ref[0], place_ref[1]
    rows_local = CHUNKS * part
    for number, (chunk, halves, s) in enumerate(spec):
        kept, arrived = refs[2 * number], refs[2 * number + 1]
        for position, half in enumerate(halves):
            column = (((chip % group) ^ s) * CORES + (half ^ core)) * width
            columns = pl.ds(pl.multiple_of(column, width), width)
            here = slice(position * width, (position + 1) * width)
            for m in range(count):
                rows = slice(m * rows_local + chunk * part, m * rows_local + (chunk + 1) * part)
                block = slice(m * part, (m + 1) * part)
                ladder = kept[block, here] + arrived[block, here]
                gap = occ_ref[rows, :] + virt_ref[:, columns]
                out_ref[rows, columns] = -(bare_ref[rows, columns] + ladder) / gap


def finish(spec, pairs, group, count, part, width, place, bare, occ, virt):
    return pl.pallas_call(
        functools.partial(finish_kernel, spec, group, count, part, width),
        in_specs=[SMEM] + [VMEM] * (3 + 2 * len(pairs)),
        out_specs=VMEM,
        out_shape=jax.ShapeDtypeStruct(bare.shape, bare.dtype),
        cost_estimate=SMALL,
        compiler_params=pltpu.CompilerParams(vmem_limit_bytes=2 * 2**20),
        name="finish",
    )(place, bare, occ[:, None], virt[None, :], *[part_in for pair in pairs for part_in in pair])


def shards(amplitudes, integrals, bare_terms, pattern, block_order, occ_gap, virt_gap):
    rows_local, columns = amplitudes.shape
    depth, columns_local = integrals.shape
    wide_count = lax.axis_size("wide")
    narrow_count = lax.axis_size("narrow")
    chips = wide_count // CORES
    wide = lax.axis_index("wide")
    z = lax.axis_index("narrow")
    chip = wide // CORES
    core = wide % CORES
    part = rows_local // CHUNKS
    rows = narrow_count * part
    group = chips // narrow_count
    place = jnp.stack([chip, core, z]).astype(jnp.int32)
    chip_bits = [1 << b for b in range(chips.bit_length() - 1)]
    narrow_bits = [1 << b for b in range(narrow_count.bit_length() - 1)]
    targets = [list(range(chips))]
    for bit in reversed(chip_bits):
        targets = [[k for k in targets[0] if not k & bit] + [k for k in targets[0] if k & bit]]
    targets = [targets[0][: chips // 2], targets[0][chips // 2 :]]

    def across(value, mask):
        return lax.ppermute(value, "wide", [(w, w ^ mask) for w in range(wide_count)])

    def across_chips(value, mask):
        return across(value, mask * CORES)

    def along(value, mask):
        return lax.ppermute(value, "narrow", [(n, n ^ mask) for n in range(narrow_count)])

    last = []

    def ordered(*values):
        return list(lax.optimization_barrier((*values, *last))[: len(values)])

    def mark(*values):
        last[:] = values

    swapped = across(integrals, 1)
    pieces = cut(amplitudes, narrow_count, depth, part, place)
    spread = {}
    mine = {}
    held = {}
    layouts = {}
    factors = {}
    state = {}

    def spread_step(g, number):
        size = len(GROUPS[g]) * part
        bit = narrow_bits[number]
        if number == 0:
            kept, send = pieces[g]
            (send,) = ordered(send)
            names = [(m, 0) for m in range(1, narrow_count, 2)]
            held_now = {(m, 0): (kept, m // 2 * size) for m in range(0, narrow_count, 2)}
        else:
            held_now = spread[g]
            names = [name for name in held_now if name[0] & bit]
            taken = ordered(*[held_now[name][0] for name in names])
            send = jnp.concatenate(
                [
                    value[held_now[name][1] : held_now[name][1] + size]
                    for name, value in zip(names, taken)
                ],
                axis=0,
            )
        mark(send)
        arrived = along(send, bit)
        spread[g] = {name: value for name, value in held_now.items() if not name[0] & bit}
        for n, (m, s) in enumerate(names):
            spread[g][m ^ bit, s | bit] = (arrived, n * size)

    def pack_step(g):
        blocks = [spread[g][0, s] for s in range(narrow_count)]
        values = ordered(*[value for value, _ in blocks])
        starts = [start for _, start in blocks]
        packed = pack(values, starts, len(GROUPS[g]), part, place)
        mark(*packed)
        mine.update(zip(GROUPS[g], packed))

    def gather_step(chunk, number):
        if number == 0:
            held[chunk] = [mine[chunk]]
            layouts[chunk] = [[(0, 0, rows)]]
        if chunk in DIRECT and chips == 4:
            (send,) = ordered(mine[chunk])
            mark(send)
            held[chunk] += [across_chips(send, k) for k in (3, 1, 2)]
            layouts[chunk] += [[(k, 0, rows)] for k in (3, 1, 2)]
        else:
            bit = chip_bits[number]
            send = jnp.concatenate(ordered(*held[chunk]), axis=0)
            mark(send)
            held[chunk].append(across_chips(send, bit))
            layouts[chunk].append([(k | bit, 0, rows) for k in range(bit)])

    def split_step(half):
        source, limit = ((integrals, 42), (swapped, 6))[half]
        *factors[half], done = split(*ordered(source), limit)
        mark(done)

    def multiply(unit):
        chunk, halves = UNITS[unit]
        partials = product(
            ordered(*held[chunk]),
            layouts[chunk],
            targets,
            [factors[half] for half in halves],
            place,
            pattern,
            block_order,
        )
        mark(*partials)
        state[unit] = {0: partials}

    def exchange_step(unit, bit):
        names = list(state[unit])
        if bit == chip_bits[0]:
            keep, leave = [state[unit][0][0]], ordered(state[unit][0][1])
        else:
            values = ordered(*state[unit].values())
            half = values[0].shape[0] // 2
            keep = [value[:half] for value in values]
            leave = [value[half:] for value in values]
        send = jnp.concatenate(leave, axis=0)
        mark(send)
        arrived = across_chips(send, bit)
        half = keep[0].shape[0]
        state[unit] = dict(zip(names, keep))
        for n, s in enumerate(names):
            state[unit][s | bit] = arrived[n * half : (n + 1) * half]

    def reduce_step(unit, bit, narrow_bit):
        now = dict(zip(state[unit], ordered(*state[unit].values())))
        same = ((chip // bit) & 1) == ((z // narrow_bit) & 1)
        names = [s for s in now if not s & bit]
        send = jnp.concatenate([jnp.where(same, now[s | bit], now[s]) for s in names], axis=0)
        mark(send)
        arrived = along(send, narrow_bit)
        size = now[0].shape[0]
        final = narrow_bit == narrow_bits[-1]
        state[unit] = {}
        for n, s in enumerate(names):
            kept = jnp.where(same, now[s], now[s | bit])
            came = arrived[n * size : (n + 1) * size]
            state[unit][s] = (kept, came) if final else kept + came

    def land(unit):
        names = list(state[unit])
        values = ordered(*[value for name in names for value in state[unit][name]])
        mark(values[-1])
        state[unit] = {name: (values[2 * n], values[2 * n + 1]) for n, name in enumerate(names)}

    steps = []
    for bit in chip_bits:
        if bit < group:
            steps.append(functools.partial(exchange_step, bit=bit))
    for narrow_bit in narrow_bits:
        bit = group * narrow_bit
        steps.append(functools.partial(exchange_step, bit=bit))
        steps.append(functools.partial(reduce_step, bit=bit, narrow_bit=narrow_bit))
    steps.append(land)

    def send_step(unit):
        multiply(unit)
        steps[0](unit)

    if chips == 4 and narrow_count == 4:
        actions = dict(s=spread_step, p=pack_step, f=split_step, g=gather_step, e=send_step)
        actions.update(r=steps[1], x=steps[2], z=steps[3], l=steps[4])
        for name in ORDER:
            actions[name[0]](*[int(number) for number in name[1:]])
    else:
        for half in range(CORES):
            split_step(half)
        for g in range(len(GROUPS)):
            for number in range(len(narrow_bits)):
                spread_step(g, number)
            pack_step(g)
        for chunk in range(CHUNKS):
            for number in range(len(chip_bits)):
                gather_step(chunk, number)
        for tick in range(len(UNITS) + len(steps) - 1):
            if tick < len(UNITS):
                send_step(tick)
            for number in range(len(steps) - 1, 0, -1):
                if 0 <= tick - number < len(UNITS):
                    steps[number](tick - number)

    spec = [(*UNITS[unit], s) for unit in range(len(UNITS)) for s in range(group)]
    pairs = [state[unit][s] for unit in range(len(UNITS)) for s in range(group)]
    return finish(
        spec,
        pairs,
        group,
        narrow_count,
        part,
        columns_local,
        place,
        bare_terms,
        occ_gap,
        virt_gap,
    )


def solution(mesh):
    placed = (
        P(("wide", "narrow"), None),
        P("narrow", "wide"),
        P("wide", "narrow"),
        P(),
        P(),
        P("wide"),
        P("narrow"),
    )
    return jax.shard_map(
        shards, mesh=mesh, in_specs=placed, out_specs=P("wide", "narrow"), check_vma=False
    )
```

```python
import functools

import jax
import jax.numpy as jnp
from jax import lax
from jax.experimental import pallas as pl
from jax.experimental.pallas import tpu as pltpu
from jax.sharding import PartitionSpec as P

TILE = 128
CHUNKS = 4
CORES = 2
DIRECT = (0,)
GROUPS = ((0,), (1,), (2, 3))
UNITS = tuple((chunk, (half,)) for chunk in range(CHUNKS) for half in range(CORES))

ORDER = (
    "s00", "s10", "s01", "s11", "p0", "s20", "g00", "p1", "g10", "s21", "f1", "e1", "p2",
    "g20", "g11", "f0", "e0", "g30", "g21", "r1", "e3", "r0", "x1", "g31", "e2", "z1", "r3",
    "x0", "e5", "r2", "l1", "e4", "z0", "x3", "r5", "e6", "z3", "x2", "l0", "r4", "e7", "z2",
    "x5", "l3", "r6", "x4", "z5", "l2", "r7", "z4", "x6", "l5", "z6", "x7", "l4", "z7", "l6",
    "l7",
)

SMEM = pl.BlockSpec(memory_space=pltpu.SMEM)
VMEM = pl.BlockSpec(memory_space=pltpu.VMEM)
HBM = pl.BlockSpec(memory_space=pltpu.HBM)
SMALL = pl.CostEstimate(flops=1, bytes_accessed=1, transcendentals=0)


def after(value, *others):
    return lax.optimization_barrier((value, *others))[0]


def cut_kernel(count, bounds, place_ref, whole_ref, *outs):
    z = place_ref[2]
    depth = outs[0].shape[1]
    for g, (low, high) in enumerate(bounds):
        size = high - low
        for m in range(count):
            start = pl.multiple_of((z ^ m) * depth, depth)
            here = slice(m // 2 * size, (m // 2 + 1) * size)
            outs[2 * g + m % 2][here, :] = whole_ref[low:high, pl.ds(start, depth)]


def cut(whole, count, depth, part, place):
    bounds = [(group[0] * part, (group[-1] + 1) * part) for group in GROUPS]
    shapes = [
        jax.ShapeDtypeStruct((count // 2 * (high - low), depth), whole.dtype)
        for low, high in bounds
        for _ in range(2)
    ]
    outs = pl.pallas_call(
        functools.partial(cut_kernel, count, bounds),
        in_specs=[SMEM, VMEM],
        out_specs=[VMEM] * len(shapes),
        out_shape=shapes,
        cost_estimate=SMALL,
        compiler_params=pltpu.CompilerParams(vmem_limit_bytes=2**20),
        name="cut",
    )(place, whole)
    return [outs[2 * g : 2 * g + 2] for g in range(len(bounds))]


def pack_kernel(part, starts, place_ref, *refs):
    z = place_ref[2]
    count = len(starts)
    for c, out in enumerate(refs[count:]):
        for m in range(count):
            rows = pl.ds(pl.multiple_of((z ^ m) * part, part), part)
            first = starts[m] + c * part
            out[rows, :] = refs[m][first : first + part, :]


def pack(blocks, starts, chunks, part, place):
    count = len(blocks)
    shape = jax.ShapeDtypeStruct((count * part, blocks[0].shape[1]), blocks[0].dtype)
    return pl.pallas_call(
        functools.partial(pack_kernel, part, starts),
        in_specs=[SMEM] + [VMEM] * count,
        out_specs=[VMEM] * chunks,
        out_shape=[shape] * chunks,
        cost_estimate=SMALL,
        compiler_params=pltpu.CompilerParams(vmem_limit_bytes=2**20),
        name="pack",
    )(place, *blocks)


def split_kernel(step, whole_ref, high_ref, low_ref, token_ref, buffer, sems):
    count = whole_ref.shape[0] // step
    slots = buffer.shape[0]

    def copy(i):
        return pltpu.make_async_copy(
            whole_ref.at[pl.ds(i * step, step)], buffer.at[i % slots], sems.at[i % slots]
        )

    for i in range(min(slots, count)):
        copy(i).start()
    token_ref[...] = jnp.zeros_like(token_ref)
    for i in range(count):
        copy(i).wait()
        whole = buffer[i % slots]
        high = whole.astype(jnp.bfloat16)
        here = slice(i * step, (i + 1) * step)
        high_ref[here, :] = high
        low_ref[here, :] = (whole - high.astype(jnp.float32)).astype(jnp.bfloat16)
        if i + slots < count:
            copy(i + slots).start()


def split(whole, limit):
    rows, columns = whole.shape
    step = min(128, rows)
    slots = min(8, rows // step)
    half = jax.ShapeDtypeStruct((rows, columns), jnp.bfloat16)
    return pl.pallas_call(
        functools.partial(split_kernel, step),
        in_specs=[HBM],
        out_specs=[VMEM, VMEM, VMEM],
        out_shape=[half, half, jax.ShapeDtypeStruct((8, 128), jnp.float32)],
        scratch_shapes=[
            pltpu.VMEM((slots, step, columns), jnp.float32),
            pltpu.SemaphoreType.DMA((slots,)),
        ],
        cost_estimate=SMALL,
        compiler_params=pltpu.CompilerParams(vmem_limit_bytes=limit * 2**20),
        name="split",
    )(whole)


def product_kernel(count, rows, layout, targets, halves, place_ref, pattern_ref, order_ref, *refs):
    lefts = refs[: len(layout)]
    factors = refs[len(layout) : len(layout) + 2 * halves]
    outs = refs[len(layout) + 2 * halves : -1]
    left = refs[-1]
    depth = lefts[0].shape[1]
    total = count * rows
    chip, core, z = place_ref[0], place_ref[1], place_ref[2]
    tiles = depth // TILE
    for held, pieces in zip(lefts, layout):
        start = 0
        for k, first, size in pieces:
            kind = order_ref[(chip ^ k) * CORES + core]
            high_rows = slice(k * rows + first, k * rows + first + size)
            low_rows = slice(total + k * rows + first, total + k * rows + first + size)
            for t in range(tiles):
                kept = pattern_ref[kind, z * tiles + t].astype(jnp.float32)
                here = slice(t * TILE, (t + 1) * TILE)
                value = held[start : start + size, here] * kept
                high = value.astype(jnp.bfloat16)
                left[high_rows, here] = high
                left[low_rows, here] = (value - high.astype(jnp.float32)).astype(jnp.bfloat16)
            start += size
    columns = factors[0].shape[1]
    width = min(512, columns)
    for half in range(halves):
        high_ref, low_ref = factors[2 * half : 2 * half + 2]
        for j in range(columns // width):
            here = slice(j * width, (j + 1) * width)
            both = jnp.dot(left[...], high_ref[:, here], preferred_element_type=jnp.float32)
            small = jnp.dot(
                left[:total, :], low_ref[:, here], preferred_element_type=jnp.float32
            )
            result = both[:total] + (both[total:] + small)
            there = slice(half * columns + j * width, half * columns + (j + 1) * width)
            for out, blocks in zip(outs, targets):
                for n, k in enumerate(blocks):
                    out[n * rows : (n + 1) * rows, there] = result[k * rows : (k + 1) * rows]


def product(lefts, layout, targets, factors, place, pattern, block_order):
    rows, depth = lefts[0].shape
    count = sum(held.shape[0] for held in lefts) // rows
    halves = len(factors)
    columns = factors[0][0].shape[1]
    total = count * rows
    return pl.pallas_call(
        functools.partial(product_kernel, count, rows, layout, targets, halves),
        in_specs=[SMEM] * 3 + [VMEM] * (len(lefts) + 2 * halves),
        out_specs=[VMEM] * len(targets),
        out_shape=[
            jax.ShapeDtypeStruct((len(blocks) * rows, halves * columns), jnp.float32)
            for blocks in targets
        ],
        scratch_shapes=[pltpu.VMEM((2 * total, depth), jnp.bfloat16)],
        cost_estimate=pl.CostEstimate(
            flops=12 * total * depth * halves * columns, bytes_accessed=1, transcendentals=0
        ),
        compiler_params=pltpu.CompilerParams(vmem_limit_bytes=8 * total * depth + 3 * 2**20),
        name="product",
    )(place, pattern, block_order, *lefts, *[part for pair in factors for part in pair])


def finish_kernel(spec, group, count, part, width, place_ref, bare_ref, occ_ref, virt_ref, *refs):
    out_ref = refs[-1]
    chip, core = place_ref[0], place_ref[1]
    rows_local = CHUNKS * part
    for number, (chunk, halves, s) in enumerate(spec):
        kept, arrived = refs[2 * number], refs[2 * number + 1]
        for position, half in enumerate(halves):
            column = (((chip % group) ^ s) * CORES + (half ^ core)) * width
            columns = pl.ds(pl.multiple_of(column, width), width)
            here = slice(position * width, (position + 1) * width)
            for m in range(count):
                rows = slice(m * rows_local + chunk * part, m * rows_local + (chunk + 1) * part)
                block = slice(m * part, (m + 1) * part)
                ladder = kept[block, here] + arrived[block, here]
                gap = occ_ref[rows, :] + virt_ref[:, columns]
                out_ref[rows, columns] = -(bare_ref[rows, columns] + ladder) / gap


def finish(spec, pairs, group, count, part, width, place, bare, occ, virt):
    return pl.pallas_call(
        functools.partial(finish_kernel, spec, group, count, part, width),
        in_specs=[SMEM] + [VMEM] * (3 + 2 * len(pairs)),
        out_specs=VMEM,
        out_shape=jax.ShapeDtypeStruct(bare.shape, bare.dtype),
        cost_estimate=SMALL,
        compiler_params=pltpu.CompilerParams(vmem_limit_bytes=2 * 2**20),
        name="finish",
    )(place, bare, occ[:, None], virt[None, :], *[part_in for pair in pairs for part_in in pair])


def shards(amplitudes, integrals, bare_terms, pattern, block_order, occ_gap, virt_gap):
    rows_local, columns = amplitudes.shape
    depth, columns_local = integrals.shape
    wide_count = lax.axis_size("wide")
    narrow_count = lax.axis_size("narrow")
    chips = wide_count // CORES
    wide = lax.axis_index("wide")
    z = lax.axis_index("narrow")
    chip = wide // CORES
    core = wide % CORES
    part = rows_local // CHUNKS
    rows = narrow_count * part
    group = chips // narrow_count
    place = jnp.stack([chip, core, z]).astype(jnp.int32)
    chip_bits = [1 << b for b in range(chips.bit_length() - 1)]
    narrow_bits = [1 << b for b in range(narrow_count.bit_length() - 1)]
    targets = [list(range(chips))]
    for bit in reversed(chip_bits):
        targets = [[k for k in targets[0] if not k & bit] + [k for k in targets[0] if k & bit]]
    targets = [targets[0][: chips // 2], targets[0][chips // 2 :]]

    def across(value, mask):
        return lax.ppermute(value, "wide", [(w, w ^ mask) for w in range(wide_count)])

    def across_chips(value, mask):
        return across(value, mask * CORES)

    def along(value, mask):
        return lax.ppermute(value, "narrow", [(n, n ^ mask) for n in range(narrow_count)])

    last = []

    def ordered(*values):
        return list(lax.optimization_barrier((*values, *last))[: len(values)])

    def mark(*values):
        last[:] = values

    swapped = across(integrals, 1)
    pieces = cut(amplitudes, narrow_count, depth, part, place)
    spread = {}
    mine = {}
    held = {}
    layouts = {}
    factors = {}
    state = {}

    def spread_step(g, number):
        size = len(GROUPS[g]) * part
        bit = narrow_bits[number]
        if number == 0:
            kept, send = pieces[g]
            (send,) = ordered(send)
            names = [(m, 0) for m in range(1, narrow_count, 2)]
            held_now = {(m, 0): (kept, m // 2 * size) for m in range(0, narrow_count, 2)}
        else:
            held_now = spread[g]
            names = [name for name in held_now if name[0] & bit]
            taken = ordered(*[held_now[name][0] for name in names])
            send = jnp.concatenate(
                [
                    value[held_now[name][1] : held_now[name][1] + size]
                    for name, value in zip(names, taken)
                ],
                axis=0,
            )
        mark(send)
        arrived = along(send, bit)
        spread[g] = {name: value for name, value in held_now.items() if not name[0] & bit}
        for n, (m, s) in enumerate(names):
            spread[g][m ^ bit, s | bit] = (arrived, n * size)

    def pack_step(g):
        blocks = [spread[g][0, s] for s in range(narrow_count)]
        values = ordered(*[value for value, _ in blocks])
        starts = [start for _, start in blocks]
        packed = pack(values, starts, len(GROUPS[g]), part, place)
        mark(*packed)
        mine.update(zip(GROUPS[g], packed))

    def gather_step(chunk, number):
        if number == 0:
            held[chunk] = [mine[chunk]]
            layouts[chunk] = [[(0, 0, rows)]]
        if chunk in DIRECT and chips == 4:
            (send,) = ordered(mine[chunk])
            mark(send)
            held[chunk] += [across_chips(send, k) for k in (3, 1, 2)]
            layouts[chunk] += [[(k, 0, rows)] for k in (3, 1, 2)]
        else:
            bit = chip_bits[number]
            send = jnp.concatenate(ordered(*held[chunk]), axis=0)
            mark(send)
            held[chunk].append(across_chips(send, bit))
            layouts[chunk].append([(k | bit, 0, rows) for k in range(bit)])

    def split_step(half):
        source, limit = ((integrals, 42), (swapped, 6))[half]
        *factors[half], done = split(*ordered(source), limit)
        mark(done)

    def multiply(unit):
        chunk, halves = UNITS[unit]
        partials = product(
            ordered(*held[chunk]),
            layouts[chunk],
            targets,
            [factors[half] for half in halves],
            place,
            pattern,
            block_order,
        )
        mark(*partials)
        state[unit] = {0: partials}

    def exchange_step(unit, bit):
        names = list(state[unit])
        if bit == chip_bits[0]:
            keep, leave = [state[unit][0][0]], ordered(state[unit][0][1])
        else:
            values = ordered(*state[unit].values())
            half = values[0].shape[0] // 2
            keep = [value[:half] for value in values]
            leave = [value[half:] for value in values]
        send = jnp.concatenate(leave, axis=0)
        mark(send)
        arrived = across_chips(send, bit)
        half = keep[0].shape[0]
        state[unit] = dict(zip(names, keep))
        for n, s in enumerate(names):
            state[unit][s | bit] = arrived[n * half : (n + 1) * half]

    def reduce_step(unit, bit, narrow_bit):
        now = dict(zip(state[unit], ordered(*state[unit].values())))
        same = ((chip // bit) & 1) == ((z // narrow_bit) & 1)
        names = [s for s in now if not s & bit]
        send = jnp.concatenate([jnp.where(same, now[s | bit], now[s]) for s in names], axis=0)
        mark(send)
        arrived = along(send, narrow_bit)
        size = now[0].shape[0]
        final = narrow_bit == narrow_bits[-1]
        state[unit] = {}
        for n, s in enumerate(names):
            kept = jnp.where(same, now[s], now[s | bit])
            came = arrived[n * size : (n + 1) * size]
            state[unit][s] = (kept, came) if final else kept + came

    def land(unit):
        names = list(state[unit])
        values = ordered(*[value for name in names for value in state[unit][name]])
        mark(values[-1])
        state[unit] = {name: (values[2 * n], values[2 * n + 1]) for n, name in enumerate(names)}

    steps = []
    for bit in chip_bits:
        if bit < group:
            steps.append(functools.partial(exchange_step, bit=bit))
    for narrow_bit in narrow_bits:
        bit = group * narrow_bit
        steps.append(functools.partial(exchange_step, bit=bit))
        steps.append(functools.partial(reduce_step, bit=bit, narrow_bit=narrow_bit))
    steps.append(land)

    def send_step(unit):
        multiply(unit)
        steps[0](unit)

    if chips == 4 and narrow_count == 4:
        actions = dict(s=spread_step, p=pack_step, f=split_step, g=gather_step, e=send_step)
        actions.update(r=steps[1], x=steps[2], z=steps[3], l=steps[4])
        for name in ORDER:
            actions[name[0]](*[int(number) for number in name[1:]])
    else:
        for half in range(CORES):
            split_step(half)
        for g in range(len(GROUPS)):
            for number in range(len(narrow_bits)):
                spread_step(g, number)
            pack_step(g)
        for chunk in range(CHUNKS):
            for number in range(len(chip_bits)):
                gather_step(chunk, number)
        for tick in range(len(UNITS) + len(steps) - 1):
            if tick < len(UNITS):
                send_step(tick)
            for number in range(len(steps) - 1, 0, -1):
                if 0 <= tick - number < len(UNITS):
                    steps[number](tick - number)

    spec = [(*UNITS[unit], s) for unit in range(len(UNITS)) for s in range(group)]
    pairs = [state[unit][s] for unit in range(len(UNITS)) for s in range(group)]
    return finish(
        spec,
        pairs,
        group,
        narrow_count,
        part,
        columns_local,
        place,
        bare_terms,
        occ_gap,
        virt_gap,
    )


def solution(mesh):
    placed = (
        P(("wide", "narrow"), None),
        P("narrow", "wide"),
        P("wide", "narrow"),
        P(),
        P(),
        P("wide"),
        P("narrow"),
    )
    return jax.shard_map(
        shards, mesh=mesh, in_specs=placed, out_specs=P("wide", "narrow"), check_vma=False
    )
```

```python
import functools

import jax
import jax.numpy as jnp
from jax import lax
from jax.experimental import pallas as pl
from jax.experimental.pallas import tpu as pltpu
from jax.sharding import PartitionSpec as P

TILE = 128
CHUNKS = 4
CORES = 2
DIRECT = ()
FORWARD = (0,)
GROUPS = ((0,), (1,), (2, 3))
UNITS = tuple((chunk, (half,)) for chunk in range(CHUNKS) for half in range(CORES))

ORDER = (
    "s00", "p0", "s10", "g00", "s11", "s20", "g01", "p1", "g10", "s21", "f0", "e0", "g11",
    "p2", "g30", "f1", "e1", "g20", "g31", "r0", "e3", "r1", "x0", "g21", "e6", "z0", "r3",
    "x1", "e2", "r6", "l0", "e4", "z1", "x3", "r2", "e7", "z3", "l1", "x6", "r4", "e5", "z6",
    "l3", "x2", "r7", "x4", "z2", "r5", "x7", "z4", "l2", "z7", "l6", "x5", "z5", "l4", "l7",
    "l5",
)

SMEM = pl.BlockSpec(memory_space=pltpu.SMEM)
VMEM = pl.BlockSpec(memory_space=pltpu.VMEM)
HBM = pl.BlockSpec(memory_space=pltpu.HBM)
SMALL = pl.CostEstimate(flops=1, bytes_accessed=1, transcendentals=0)


def after(value, *others):
    return lax.optimization_barrier((value, *others))[0]


def cut_kernel(count, bounds, place_ref, whole_ref, *outs):
    z = place_ref[2]
    depth = outs[0].shape[1]
    outs = list(outs)
    for low, high, stacks in bounds:
        size = high - low
        for m in range(count):
            start = pl.multiple_of((z ^ m) * depth, depth)
            here = slice(m // stacks * size, (m // stacks + 1) * size)
            outs[m % stacks][here, :] = whole_ref[low:high, pl.ds(start, depth)]
        del outs[:stacks]


def cut(whole, count, depth, part, place):
    bounds = [
        (group[0] * part, (group[-1] + 1) * part, 2 if g else count)
        for g, group in enumerate(GROUPS)
    ]
    shapes = [
        jax.ShapeDtypeStruct((count // stacks * (high - low), depth), whole.dtype)
        for low, high, stacks in bounds
        for _ in range(stacks)
    ]
    outs = list(pl.pallas_call(
        functools.partial(cut_kernel, count, bounds),
        in_specs=[SMEM, VMEM],
        out_specs=[VMEM] * len(shapes),
        out_shape=shapes,
        cost_estimate=SMALL,
        compiler_params=pltpu.CompilerParams(vmem_limit_bytes=2**20),
        name="cut",
    )(place, whole))
    return [[outs.pop(0) for _ in range(stacks)] for _, _, stacks in bounds]


def pack_kernel(part, starts, place_ref, *refs):
    z = place_ref[2]
    count = len(starts)
    for c, out in enumerate(refs[count:]):
        for m in range(count):
            rows = pl.ds(pl.multiple_of((z ^ m) * part, part), part)
            first = starts[m] + c * part
            out[rows, :] = refs[m][first : first + part, :]


def pack(blocks, starts, chunks, part, place):
    count = len(blocks)
    shape = jax.ShapeDtypeStruct((count * part, blocks[0].shape[1]), blocks[0].dtype)
    return pl.pallas_call(
        functools.partial(pack_kernel, part, starts),
        in_specs=[SMEM] + [VMEM] * count,
        out_specs=[VMEM] * chunks,
        out_shape=[shape] * chunks,
        cost_estimate=SMALL,
        compiler_params=pltpu.CompilerParams(vmem_limit_bytes=2**20),
        name="pack",
    )(place, *blocks)


def split_kernel(step, whole_ref, high_ref, low_ref, token_ref, buffer, sems):
    count = whole_ref.shape[0] // step
    slots = buffer.shape[0]

    def copy(i):
        return pltpu.make_async_copy(
            whole_ref.at[pl.ds(i * step, step)], buffer.at[i % slots], sems.at[i % slots]
        )

    for i in range(min(slots, count)):
        copy(i).start()
    token_ref[...] = jnp.zeros_like(token_ref)
    for i in range(count):
        copy(i).wait()
        whole = buffer[i % slots]
        high = whole.astype(jnp.bfloat16)
        here = slice(i * step, (i + 1) * step)
        high_ref[here, :] = high
        low_ref[here, :] = (whole - high.astype(jnp.float32)).astype(jnp.bfloat16)
        if i + slots < count:
            copy(i + slots).start()


def split(whole, limit):
    rows, columns = whole.shape
    step = min(128, rows)
    slots = min(8, rows // step)
    half = jax.ShapeDtypeStruct((rows, columns), jnp.bfloat16)
    return pl.pallas_call(
        functools.partial(split_kernel, step),
        in_specs=[HBM],
        out_specs=[VMEM, VMEM, VMEM],
        out_shape=[half, half, jax.ShapeDtypeStruct((8, 128), jnp.float32)],
        scratch_shapes=[
            pltpu.VMEM((slots, step, columns), jnp.float32),
            pltpu.SemaphoreType.DMA((slots,)),
        ],
        cost_estimate=SMALL,
        compiler_params=pltpu.CompilerParams(vmem_limit_bytes=limit * 2**20),
        name="split",
    )(whole)


def product_kernel(count, rows, layout, targets, halves, place_ref, pattern_ref, order_ref, *refs):
    lefts = refs[: len(layout)]
    factors = refs[len(layout) : len(layout) + 2 * halves]
    outs = refs[len(layout) + 2 * halves : -1]
    left = refs[-1]
    depth = lefts[0].shape[1]
    total = count * rows
    chip, core, z = place_ref[0], place_ref[1], place_ref[2]
    tiles = depth // TILE
    for held, pieces in zip(lefts, layout):
        start = 0
        for k, first, size in pieces:
            kind = order_ref[(chip ^ k) * CORES + core]
            high_rows = slice(k * rows + first, k * rows + first + size)
            low_rows = slice(total + k * rows + first, total + k * rows + first + size)
            for t in range(tiles):
                kept = pattern_ref[kind, z * tiles + t].astype(jnp.float32)
                here = slice(t * TILE, (t + 1) * TILE)
                value = held[start : start + size, here] * kept
                high = value.astype(jnp.bfloat16)
                left[high_rows, here] = high
                left[low_rows, here] = (value - high.astype(jnp.float32)).astype(jnp.bfloat16)
            start += size
    columns = factors[0].shape[1]
    width = min(512, columns)
    for half in range(halves):
        high_ref, low_ref = factors[2 * half : 2 * half + 2]
        for j in range(columns // width):
            here = slice(j * width, (j + 1) * width)
            both = jnp.dot(left[...], high_ref[:, here], preferred_element_type=jnp.float32)
            small = jnp.dot(
                left[:total, :], low_ref[:, here], preferred_element_type=jnp.float32
            )
            result = both[:total] + (both[total:] + small)
            there = slice(half * columns + j * width, half * columns + (j + 1) * width)
            for out, blocks in zip(outs, targets):
                for n, k in enumerate(blocks):
                    out[n * rows : (n + 1) * rows, there] = result[k * rows : (k + 1) * rows]


def product(lefts, layout, targets, factors, place, pattern, block_order):
    rows, depth = lefts[0].shape
    count = sum(held.shape[0] for held in lefts) // rows
    halves = len(factors)
    columns = factors[0][0].shape[1]
    total = count * rows
    return pl.pallas_call(
        functools.partial(product_kernel, count, rows, layout, targets, halves),
        in_specs=[SMEM] * 3 + [VMEM] * (len(lefts) + 2 * halves),
        out_specs=[VMEM] * len(targets),
        out_shape=[
            jax.ShapeDtypeStruct((len(blocks) * rows, halves * columns), jnp.float32)
            for blocks in targets
        ],
        scratch_shapes=[pltpu.VMEM((2 * total, depth), jnp.bfloat16)],
        cost_estimate=pl.CostEstimate(
            flops=12 * total * depth * halves * columns, bytes_accessed=1, transcendentals=0
        ),
        compiler_params=pltpu.CompilerParams(vmem_limit_bytes=8 * total * depth + 3 * 2**20),
        name="product",
    )(place, pattern, block_order, *lefts, *[part for pair in factors for part in pair])


def finish_kernel(spec, group, count, part, width, place_ref, bare_ref, occ_ref, virt_ref, *refs):
    out_ref = refs[-1]
    chip, core = place_ref[0], place_ref[1]
    rows_local = CHUNKS * part
    for number, (chunk, halves, s) in enumerate(spec):
        kept, arrived = refs[2 * number], refs[2 * number + 1]
        for position, half in enumerate(halves):
            column = (((chip % group) ^ s) * CORES + (half ^ core)) * width
            columns = pl.ds(pl.multiple_of(column, width), width)
            here = slice(position * width, (position + 1) * width)
            for m in range(count):
                rows = slice(m * rows_local + chunk * part, m * rows_local + (chunk + 1) * part)
                block = slice(m * part, (m + 1) * part)
                ladder = kept[block, here] + arrived[block, here]
                gap = occ_ref[rows, :] + virt_ref[:, columns]
                out_ref[rows, columns] = -(bare_ref[rows, columns] + ladder) / gap


def finish(spec, pairs, group, count, part, width, place, bare, occ, virt):
    return pl.pallas_call(
        functools.partial(finish_kernel, spec, group, count, part, width),
        in_specs=[SMEM] + [VMEM] * (3 + 2 * len(pairs)),
        out_specs=VMEM,
        out_shape=jax.ShapeDtypeStruct(bare.shape, bare.dtype),
        cost_estimate=SMALL,
        compiler_params=pltpu.CompilerParams(vmem_limit_bytes=2 * 2**20),
        name="finish",
    )(place, bare, occ[:, None], virt[None, :], *[part_in for pair in pairs for part_in in pair])


def shards(amplitudes, integrals, bare_terms, pattern, block_order, occ_gap, virt_gap):
    rows_local, columns = amplitudes.shape
    depth, columns_local = integrals.shape
    wide_count = lax.axis_size("wide")
    narrow_count = lax.axis_size("narrow")
    chips = wide_count // CORES
    wide = lax.axis_index("wide")
    z = lax.axis_index("narrow")
    chip = wide // CORES
    core = wide % CORES
    part = rows_local // CHUNKS
    rows = narrow_count * part
    group = chips // narrow_count
    place = jnp.stack([chip, core, z]).astype(jnp.int32)
    chip_bits = [1 << b for b in range(chips.bit_length() - 1)]
    narrow_bits = [1 << b for b in range(narrow_count.bit_length() - 1)]
    targets = [list(range(chips))]
    for bit in reversed(chip_bits):
        targets = [[k for k in targets[0] if not k & bit] + [k for k in targets[0] if k & bit]]
    targets = [targets[0][: chips // 2], targets[0][chips // 2 :]]

    def across(value, mask):
        return lax.ppermute(value, "wide", [(w, w ^ mask) for w in range(wide_count)])

    def across_chips(value, mask):
        return across(value, mask * CORES)

    def along(value, mask):
        return lax.ppermute(value, "narrow", [(n, n ^ mask) for n in range(narrow_count)])

    last = []

    def ordered(*values):
        return list(lax.optimization_barrier((*values, *last))[: len(values)])

    def mark(*values):
        last[:] = values

    swapped = across(integrals, 1)
    pieces = cut(amplitudes, narrow_count, depth, part, place)
    spread = {}
    mine = {}
    held = {}
    layouts = {}
    factors = {}
    state = {}

    def spread_step(g, number):
        size = len(GROUPS[g]) * part
        bit = narrow_bits[number]
        if g == 0:
            if number == 0:
                sends = ordered(*pieces[g][1:])
                mark(*sends)
                spread[g] = {(0, 0): (pieces[g][0], 0)}
                for n, send in enumerate(sends):
                    spread[g][0, n + 1] = (along(send, n + 1), 0)
            return
        if number == 0:
            kept, send = pieces[g]
            (send,) = ordered(send)
            names = [(m, 0) for m in range(1, narrow_count, 2)]
            held_now = {(m, 0): (kept, m // 2 * size) for m in range(0, narrow_count, 2)}
        else:
            held_now = spread[g]
            names = [name for name in held_now if name[0] & bit]
            taken = ordered(*[held_now[name][0] for name in names])
            send = jnp.concatenate(
                [
                    value[held_now[name][1] : held_now[name][1] + size]
                    for name, value in zip(names, taken)
                ],
                axis=0,
            )
        mark(send)
        arrived = along(send, bit)
        spread[g] = {name: value for name, value in held_now.items() if not name[0] & bit}
        for n, (m, s) in enumerate(names):
            spread[g][m ^ bit, s | bit] = (arrived, n * size)

    def pack_step(g):
        blocks = [spread[g][0, s] for s in range(narrow_count)]
        values = ordered(*[value for value, _ in blocks])
        starts = [start for _, start in blocks]
        packed = pack(values, starts, len(GROUPS[g]), part, place)
        mark(*packed)
        mine.update(zip(GROUPS[g], packed))

    def gather_step(chunk, number):
        if number == 0:
            held[chunk] = [mine[chunk]]
            layouts[chunk] = [[(0, 0, rows)]]
        if chunk in FORWARD and chips == 4:
            if number == 0:
                (send,) = ordered(mine[chunk])
                mark(send)
                held[chunk] += [across_chips(send, 1), across_chips(send, 2)]
                layouts[chunk] += [[(1, 0, rows)], [(2, 0, rows)]]
            else:
                near, far = ordered(held[chunk][1], held[chunk][2])
                near, far = near[: rows // 2], far[rows // 2 :]
                mark(near, far)
                held[chunk] += [across_chips(near, 2), across_chips(far, 1)]
                layouts[chunk] += [[(3, 0, rows // 2)], [(3, rows // 2, rows // 2)]]
        elif chunk in DIRECT and chips == 4:
            (send,) = ordered(mine[chunk])
            mark(send)
            held[chunk] += [across_chips(send, k) for k in (3, 1, 2)]
            layouts[chunk] += [[(k, 0, rows)] for k in (3, 1, 2)]
        else:
            bit = chip_bits[number]
            send = jnp.concatenate(ordered(*held[chunk]), axis=0)
            mark(send)
            held[chunk].append(across_chips(send, bit))
            layouts[chunk].append([(k | bit, 0, rows) for k in range(bit)])

    def split_step(half):
        source, limit = ((integrals, 42), (swapped, 6))[half]
        *factors[half], done = split(*ordered(source), limit)
        mark(done)

    def multiply(unit):
        chunk, halves = UNITS[unit]
        partials = product(
            ordered(*held[chunk]),
            layouts[chunk],
            targets,
            [factors[half] for half in halves],
            place,
            pattern,
            block_order,
        )
        mark(*partials)
        state[unit] = {0: partials}

    def exchange_step(unit, bit):
        names = list(state[unit])
        if bit == chip_bits[0]:
            keep, leave = [state[unit][0][0]], ordered(state[unit][0][1])
        else:
            values = ordered(*state[unit].values())
            half = values[0].shape[0] // 2
            keep = [value[:half] for value in values]
            leave = [value[half:] for value in values]
        send = jnp.concatenate(leave, axis=0)
        mark(send)
        arrived = across_chips(send, bit)
        half = keep[0].shape[0]
        state[unit] = dict(zip(names, keep))
        for n, s in enumerate(names):
            state[unit][s | bit] = arrived[n * half : (n + 1) * half]

    def reduce_step(unit, bit, narrow_bit):
        now = dict(zip(state[unit], ordered(*state[unit].values())))
        same = ((chip // bit) & 1) == ((z // narrow_bit) & 1)
        names = [s for s in now if not s & bit]
        send = jnp.concatenate([jnp.where(same, now[s | bit], now[s]) for s in names], axis=0)
        mark(send)
        arrived = along(send, narrow_bit)
        size = now[0].shape[0]
        final = narrow_bit == narrow_bits[-1]
        state[unit] = {}
        for n, s in enumerate(names):
            kept = jnp.where(same, now[s], now[s | bit])
            came = arrived[n * size : (n + 1) * size]
            state[unit][s] = (kept, came) if final else kept + came

    def land(unit):
        names = list(state[unit])
        values = ordered(*[value for name in names for value in state[unit][name]])
        mark(values[-1])
        state[unit] = {name: (values[2 * n], values[2 * n + 1]) for n, name in enumerate(names)}

    steps = []
    for bit in chip_bits:
        if bit < group:
            steps.append(functools.partial(exchange_step, bit=bit))
    for narrow_bit in narrow_bits:
        bit = group * narrow_bit
        steps.append(functools.partial(exchange_step, bit=bit))
        steps.append(functools.partial(reduce_step, bit=bit, narrow_bit=narrow_bit))
    steps.append(land)

    def send_step(unit):
        multiply(unit)
        steps[0](unit)

    if chips == 4 and narrow_count == 4:
        actions = dict(s=spread_step, p=pack_step, f=split_step, g=gather_step, e=send_step)
        actions.update(r=steps[1], x=steps[2], z=steps[3], l=steps[4])
        for name in ORDER:
            actions[name[0]](*[int(number) for number in name[1:]])
    else:
        for half in range(CORES):
            split_step(half)
        for g in range(len(GROUPS)):
            for number in range(len(narrow_bits)):
                spread_step(g, number)
            pack_step(g)
        for chunk in range(CHUNKS):
            for number in range(len(chip_bits)):
                gather_step(chunk, number)
        for tick in range(len(UNITS) + len(steps) - 1):
            if tick < len(UNITS):
                send_step(tick)
            for number in range(len(steps) - 1, 0, -1):
                if 0 <= tick - number < len(UNITS):
                    steps[number](tick - number)

    spec = [(*UNITS[unit], s) for unit in range(len(UNITS)) for s in range(group)]
    pairs = [state[unit][s] for unit in range(len(UNITS)) for s in range(group)]
    return finish(
        spec,
        pairs,
        group,
        narrow_count,
        part,
        columns_local,
        place,
        bare_terms,
        occ_gap,
        virt_gap,
    )


def solution(mesh):
    placed = (
        P(("wide", "narrow"), None),
        P("narrow", "wide"),
        P("wide", "narrow"),
        P(),
        P(),
        P("wide"),
        P("narrow"),
    )
    return jax.shard_map(
        shards, mesh=mesh, in_specs=placed, out_specs=P("wide", "narrow"), check_vma=False
    )
```

```python
import functools

import jax
import jax.numpy as jnp
from jax import lax
from jax.experimental import pallas as pl
from jax.experimental.pallas import tpu as pltpu
from jax.sharding import PartitionSpec as P

TILE = 128
CHUNKS = 4
CORES = 2
DIRECT = ()
FORWARD = (0,)
GROUPS = ((0,), (1,), (2, 3))
UNITS = tuple((chunk, (half,)) for chunk in range(CHUNKS) for half in range(CORES))

ORDER = (
    "s00", "p0", "s10", "g00", "s11", "s20", "g01", "f0", "p1", "g10", "s21", "e0", "g11",
    "p2", "g30", "f1", "e1", "g20", "g31", "r0", "e3", "r1", "x0", "g21", "e6", "z0", "r3",
    "x1", "e2", "r6", "l0", "e4", "z1", "x3", "r2", "e7", "z3", "l1", "x6", "r4", "e5", "z6",
    "l3", "x2", "r7", "x4", "z2", "r5", "x7", "z4", "l2", "z7", "l6", "x5", "z5", "l4", "l7",
    "l5",
)

SMEM = pl.BlockSpec(memory_space=pltpu.SMEM)
VMEM = pl.BlockSpec(memory_space=pltpu.VMEM)
HBM = pl.BlockSpec(memory_space=pltpu.HBM)
SMALL = pl.CostEstimate(flops=1, bytes_accessed=1, transcendentals=0)


def after(value, *others):
    return lax.optimization_barrier((value, *others))[0]


def cut_kernel(count, bounds, place_ref, whole_ref, *outs):
    z = place_ref[2]
    depth = outs[0].shape[1]
    outs = list(outs)
    for low, high, stacks in bounds:
        size = high - low
        for m in range(count):
            start = pl.multiple_of((z ^ m) * depth, depth)
            here = slice(m // stacks * size, (m // stacks + 1) * size)
            outs[m % stacks][here, :] = whole_ref[low:high, pl.ds(start, depth)]
        del outs[:stacks]


def cut(whole, count, depth, part, place):
    bounds = [
        (group[0] * part, (group[-1] + 1) * part, 2 if g else count)
        for g, group in enumerate(GROUPS)
    ]
    shapes = [
        jax.ShapeDtypeStruct((count // stacks * (high - low), depth), whole.dtype)
        for low, high, stacks in bounds
        for _ in range(stacks)
    ]
    outs = list(pl.pallas_call(
        functools.partial(cut_kernel, count, bounds),
        in_specs=[SMEM, VMEM],
        out_specs=[VMEM] * len(shapes),
        out_shape=shapes,
        cost_estimate=SMALL,
        compiler_params=pltpu.CompilerParams(vmem_limit_bytes=2**20),
        name="cut",
    )(place, whole))
    return [[outs.pop(0) for _ in range(stacks)] for _, _, stacks in bounds]


def pack_kernel(part, starts, place_ref, *refs):
    z = place_ref[2]
    count = len(starts)
    for c, out in enumerate(refs[count:]):
        for m in range(count):
            rows = pl.ds(pl.multiple_of((z ^ m) * part, part), part)
            first = starts[m] + c * part
            out[rows, :] = refs[m][first : first + part, :]


def pack(blocks, starts, chunks, part, place):
    count = len(blocks)
    shape = jax.ShapeDtypeStruct((count * part, blocks[0].shape[1]), blocks[0].dtype)
    return pl.pallas_call(
        functools.partial(pack_kernel, part, starts),
        in_specs=[SMEM] + [VMEM] * count,
        out_specs=[VMEM] * chunks,
        out_shape=[shape] * chunks,
        cost_estimate=SMALL,
        compiler_params=pltpu.CompilerParams(vmem_limit_bytes=2**20),
        name="pack",
    )(place, *blocks)


def split_kernel(step, whole_ref, high_ref, low_ref, token_ref, buffer, sems):
    count = whole_ref.shape[0] // step
    slots = buffer.shape[0]

    def copy(i):
        return pltpu.make_async_copy(
            whole_ref.at[pl.ds(i * step, step)], buffer.at[i % slots], sems.at[i % slots]
        )

    for i in range(min(slots, count)):
        copy(i).start()
    token_ref[...] = jnp.zeros_like(token_ref)
    for i in range(count):
        copy(i).wait()
        whole = buffer[i % slots]
        high = whole.astype(jnp.bfloat16)
        here = slice(i * step, (i + 1) * step)
        high_ref[here, :] = high
        low_ref[here, :] = (whole - high.astype(jnp.float32)).astype(jnp.bfloat16)
        if i + slots < count:
            copy(i + slots).start()


def split(whole, limit):
    rows, columns = whole.shape
    step = min(128, rows)
    slots = min(8, rows // step)
    half = jax.ShapeDtypeStruct((rows, columns), jnp.bfloat16)
    return pl.pallas_call(
        functools.partial(split_kernel, step),
        in_specs=[HBM],
        out_specs=[VMEM, VMEM, VMEM],
        out_shape=[half, half, jax.ShapeDtypeStruct((8, 128), jnp.float32)],
        scratch_shapes=[
            pltpu.VMEM((slots, step, columns), jnp.float32),
            pltpu.SemaphoreType.DMA((slots,)),
        ],
        cost_estimate=SMALL,
        compiler_params=pltpu.CompilerParams(vmem_limit_bytes=limit * 2**20),
        name="split",
    )(whole)


def product_kernel(count, rows, layout, targets, halves, place_ref, pattern_ref, order_ref, *refs):
    lefts = refs[: len(layout)]
    factors = refs[len(layout) : len(layout) + 2 * halves]
    outs = refs[len(layout) + 2 * halves : -1]
    left = refs[-1]
    depth = lefts[0].shape[1]
    total = count * rows
    chip, core, z = place_ref[0], place_ref[1], place_ref[2]
    tiles = depth // TILE
    for held, pieces in zip(lefts, layout):
        start = 0
        for k, first, size in pieces:
            kind = order_ref[(chip ^ k) * CORES + core]
            high_rows = slice(k * rows + first, k * rows + first + size)
            low_rows = slice(total + k * rows + first, total + k * rows + first + size)
            for t in range(tiles):
                kept = pattern_ref[kind, z * tiles + t].astype(jnp.float32)
                here = slice(t * TILE, (t + 1) * TILE)
                value = held[start : start + size, here] * kept
                high = value.astype(jnp.bfloat16)
                left[high_rows, here] = high
                left[low_rows, here] = (value - high.astype(jnp.float32)).astype(jnp.bfloat16)
            start += size
    columns = factors[0].shape[1]
    width = min(512, columns)
    for half in range(halves):
        high_ref, low_ref = factors[2 * half : 2 * half + 2]
        for j in range(columns // width):
            here = slice(j * width, (j + 1) * width)
            both = jnp.dot(left[...], high_ref[:, here], preferred_element_type=jnp.float32)
            small = jnp.dot(
                left[:total, :], low_ref[:, here], preferred_element_type=jnp.float32
            )
            result = both[:total] + (both[total:] + small)
            there = slice(half * columns + j * width, half * columns + (j + 1) * width)
            for out, blocks in zip(outs, targets):
                for n, k in enumerate(blocks):
                    out[n * rows : (n + 1) * rows, there] = result[k * rows : (k + 1) * rows]


def product(lefts, layout, targets, factors, place, pattern, block_order):
    rows, depth = lefts[0].shape
    count = sum(held.shape[0] for held in lefts) // rows
    halves = len(factors)
    columns = factors[0][0].shape[1]
    total = count * rows
    return pl.pallas_call(
        functools.partial(product_kernel, count, rows, layout, targets, halves),
        in_specs=[SMEM] * 3 + [VMEM] * (len(lefts) + 2 * halves),
        out_specs=[VMEM] * len(targets),
        out_shape=[
            jax.ShapeDtypeStruct((len(blocks) * rows, halves * columns), jnp.float32)
            for blocks in targets
        ],
        scratch_shapes=[pltpu.VMEM((2 * total, depth), jnp.bfloat16)],
        cost_estimate=pl.CostEstimate(
            flops=12 * total * depth * halves * columns, bytes_accessed=1, transcendentals=0
        ),
        compiler_params=pltpu.CompilerParams(vmem_limit_bytes=8 * total * depth + 3 * 2**20),
        name="product",
    )(place, pattern, block_order, *lefts, *[part for pair in factors for part in pair])


def finish_kernel(spec, group, count, part, width, place_ref, bare_ref, occ_ref, virt_ref, *refs):
    out_ref = refs[-1]
    chip, core = place_ref[0], place_ref[1]
    rows_local = CHUNKS * part
    for number, (chunk, halves, s) in enumerate(spec):
        kept, arrived = refs[2 * number], refs[2 * number + 1]
        for position, half in enumerate(halves):
            column = (((chip % group) ^ s) * CORES + (half ^ core)) * width
            columns = pl.ds(pl.multiple_of(column, width), width)
            here = slice(position * width, (position + 1) * width)
            for m in range(count):
                rows = slice(m * rows_local + chunk * part, m * rows_local + (chunk + 1) * part)
                block = slice(m * part, (m + 1) * part)
                ladder = kept[block, here] + arrived[block, here]
                gap = occ_ref[rows, :] + virt_ref[:, columns]
                out_ref[rows, columns] = -(bare_ref[rows, columns] + ladder) / gap


def finish(spec, pairs, group, count, part, width, place, bare, occ, virt):
    return pl.pallas_call(
        functools.partial(finish_kernel, spec, group, count, part, width),
        in_specs=[SMEM] + [VMEM] * (3 + 2 * len(pairs)),
        out_specs=VMEM,
        out_shape=jax.ShapeDtypeStruct(bare.shape, bare.dtype),
        cost_estimate=SMALL,
        compiler_params=pltpu.CompilerParams(vmem_limit_bytes=2 * 2**20),
        name="finish",
    )(place, bare, occ[:, None], virt[None, :], *[part_in for pair in pairs for part_in in pair])


def shards(amplitudes, integrals, bare_terms, pattern, block_order, occ_gap, virt_gap):
    rows_local, columns = amplitudes.shape
    depth, columns_local = integrals.shape
    wide_count = lax.axis_size("wide")
    narrow_count = lax.axis_size("narrow")
    chips = wide_count // CORES
    wide = lax.axis_index("wide")
    z = lax.axis_index("narrow")
    chip = wide // CORES
    core = wide % CORES
    part = rows_local // CHUNKS
    rows = narrow_count * part
    group = chips // narrow_count
    place = jnp.stack([chip, core, z]).astype(jnp.int32)
    chip_bits = [1 << b for b in range(chips.bit_length() - 1)]
    narrow_bits = [1 << b for b in range(narrow_count.bit_length() - 1)]
    targets = [list(range(chips))]
    for bit in reversed(chip_bits):
        targets = [[k for k in targets[0] if not k & bit] + [k for k in targets[0] if k & bit]]
    targets = [targets[0][: chips // 2], targets[0][chips // 2 :]]

    def across(value, mask):
        return lax.ppermute(value, "wide", [(w, w ^ mask) for w in range(wide_count)])

    def across_chips(value, mask):
        return across(value, mask * CORES)

    def along(value, mask):
        return lax.ppermute(value, "narrow", [(n, n ^ mask) for n in range(narrow_count)])

    last = []

    def ordered(*values):
        return list(lax.optimization_barrier((*values, *last))[: len(values)])

    def mark(*values):
        last[:] = values

    swapped = across(integrals, 1)
    pieces = cut(amplitudes, narrow_count, depth, part, place)
    spread = {}
    mine = {}
    held = {}
    layouts = {}
    factors = {}
    state = {}

    def spread_step(g, number):
        size = len(GROUPS[g]) * part
        bit = narrow_bits[number]
        if g == 0:
            if number == 0:
                sends = ordered(*pieces[g][1:])
                mark(*sends)
                spread[g] = {(0, 0): (pieces[g][0], 0)}
                for n, send in enumerate(sends):
                    spread[g][0, n + 1] = (along(send, n + 1), 0)
            return
        if number == 0:
            kept, send = pieces[g]
            (send,) = ordered(send)
            names = [(m, 0) for m in range(1, narrow_count, 2)]
            held_now = {(m, 0): (kept, m // 2 * size) for m in range(0, narrow_count, 2)}
        else:
            held_now = spread[g]
            names = [name for name in held_now if name[0] & bit]
            taken = ordered(*[held_now[name][0] for name in names])
            send = jnp.concatenate(
                [
                    value[held_now[name][1] : held_now[name][1] + size]
                    for name, value in zip(names, taken)
                ],
                axis=0,
            )
        mark(send)
        arrived = along(send, bit)
        spread[g] = {name: value for name, value in held_now.items() if not name[0] & bit}
        for n, (m, s) in enumerate(names):
            spread[g][m ^ bit, s | bit] = (arrived, n * size)

    def pack_step(g):
        blocks = [spread[g][0, s] for s in range(narrow_count)]
        values = ordered(*[value for value, _ in blocks])
        starts = [start for _, start in blocks]
        packed = pack(values, starts, len(GROUPS[g]), part, place)
        mark(*packed)
        mine.update(zip(GROUPS[g], packed))

    def gather_step(chunk, number):
        if number == 0:
            held[chunk] = [mine[chunk]]
            layouts[chunk] = [[(0, 0, rows)]]
        if chunk in FORWARD and chips == 4:
            if number == 0:
                (send,) = ordered(mine[chunk])
                mark(send)
                held[chunk] += [across_chips(send, 1), across_chips(send, 2)]
                layouts[chunk] += [[(1, 0, rows)], [(2, 0, rows)]]
            else:
                near, far = ordered(held[chunk][1], held[chunk][2])
                near, far = near[: rows // 2], far[rows // 2 :]
                mark(near, far)
                held[chunk] += [across_chips(near, 2), across_chips(far, 1)]
                layouts[chunk] += [[(3, 0, rows // 2)], [(3, rows // 2, rows // 2)]]
        elif chunk in DIRECT and chips == 4:
            (send,) = ordered(mine[chunk])
            mark(send)
            held[chunk] += [across_chips(send, k) for k in (3, 1, 2)]
            layouts[chunk] += [[(k, 0, rows)] for k in (3, 1, 2)]
        else:
            bit = chip_bits[number]
            send = jnp.concatenate(ordered(*held[chunk]), axis=0)
            mark(send)
            held[chunk].append(across_chips(send, bit))
            layouts[chunk].append([(k | bit, 0, rows) for k in range(bit)])

    def split_step(half):
        source, limit = ((integrals, 42), (swapped, 6))[half]
        *factors[half], done = split(*ordered(source), limit)
        mark(done)

    def multiply(unit):
        chunk, halves = UNITS[unit]
        partials = product(
            ordered(*held[chunk]),
            layouts[chunk],
            targets,
            [factors[half] for half in halves],
            place,
            pattern,
            block_order,
        )
        mark(*partials)
        state[unit] = {0: partials}

    def exchange_step(unit, bit):
        names = list(state[unit])
        if bit == chip_bits[0]:
            keep, leave = [state[unit][0][0]], ordered(state[unit][0][1])
        else:
            values = ordered(*state[unit].values())
            half = values[0].shape[0] // 2
            keep = [value[:half] for value in values]
            leave = [value[half:] for value in values]
        send = jnp.concatenate(leave, axis=0)
        mark(send)
        arrived = across_chips(send, bit)
        half = keep[0].shape[0]
        state[unit] = dict(zip(names, keep))
        for n, s in enumerate(names):
            state[unit][s | bit] = arrived[n * half : (n + 1) * half]

    def reduce_step(unit, bit, narrow_bit):
        now = dict(zip(state[unit], ordered(*state[unit].values())))
        same = ((chip // bit) & 1) == ((z // narrow_bit) & 1)
        names = [s for s in now if not s & bit]
        send = jnp.concatenate([jnp.where(same, now[s | bit], now[s]) for s in names], axis=0)
        mark(send)
        arrived = along(send, narrow_bit)
        size = now[0].shape[0]
        final = narrow_bit == narrow_bits[-1]
        state[unit] = {}
        for n, s in enumerate(names):
            kept = jnp.where(same, now[s], now[s | bit])
            came = arrived[n * size : (n + 1) * size]
            state[unit][s] = (kept, came) if final else kept + came

    def land(unit):
        names = list(state[unit])
        values = ordered(*[value for name in names for value in state[unit][name]])
        mark(values[-1])
        state[unit] = {name: (values[2 * n], values[2 * n + 1]) for n, name in enumerate(names)}

    steps = []
    for bit in chip_bits:
        if bit < group:
            steps.append(functools.partial(exchange_step, bit=bit))
    for narrow_bit in narrow_bits:
        bit = group * narrow_bit
        steps.append(functools.partial(exchange_step, bit=bit))
        steps.append(functools.partial(reduce_step, bit=bit, narrow_bit=narrow_bit))
    steps.append(land)

    def send_step(unit):
        multiply(unit)
        steps[0](unit)

    if chips == 4 and narrow_count == 4:
        actions = dict(s=spread_step, p=pack_step, f=split_step, g=gather_step, e=send_step)
        actions.update(r=steps[1], x=steps[2], z=steps[3], l=steps[4])
        for name in ORDER:
            actions[name[0]](*[int(number) for number in name[1:]])
    else:
        for half in range(CORES):
            split_step(half)
        for g in range(len(GROUPS)):
            for number in range(len(narrow_bits)):
                spread_step(g, number)
            pack_step(g)
        for chunk in range(CHUNKS):
            for number in range(len(chip_bits)):
                gather_step(chunk, number)
        for tick in range(len(UNITS) + len(steps) - 1):
            if tick < len(UNITS):
                send_step(tick)
            for number in range(len(steps) - 1, 0, -1):
                if 0 <= tick - number < len(UNITS):
                    steps[number](tick - number)

    spec = [(*UNITS[unit], s) for unit in range(len(UNITS)) for s in range(group)]
    pairs = [state[unit][s] for unit in range(len(UNITS)) for s in range(group)]
    return finish(
        spec,
        pairs,
        group,
        narrow_count,
        part,
        columns_local,
        place,
        bare_terms,
        occ_gap,
        virt_gap,
    )


def solution(mesh):
    placed = (
        P(("wide", "narrow"), None),
        P("narrow", "wide"),
        P("wide", "narrow"),
        P(),
        P(),
        P("wide"),
        P("narrow"),
    )
    return jax.shard_map(
        shards, mesh=mesh, in_specs=placed, out_specs=P("wide", "narrow"), check_vma=False
    )
```

```python
import functools

import jax
import jax.numpy as jnp
from jax import lax
from jax.experimental import pallas as pl
from jax.experimental.pallas import tpu as pltpu
from jax.sharding import PartitionSpec as P

TILE = 128
CHUNKS = 4
CORES = 2
DIRECT = ()
FORWARD = (0,)
GROUPS = ((0,), (1,), (2, 3))
UNITS = tuple((chunk, (half,)) for chunk in range(CHUNKS) for half in range(CORES))

ORDER = (
    "s00", "p0", "s10", "g00", "s11", "s20", "g01", "f0", "p1", "g10", "s21", "e0", "f1", "e1",
    "g11", "r0", "p2", "g20", "r1", "g30", "x0", "g21", "e3", "z0", "e2", "x1", "g31", "r3",
    "l0", "e4", "z1", "r2", "e5", "x3", "r4", "l1", "e7", "z3", "x2", "r5", "e6", "z2", "x4",
    "r7", "l3", "x5", "z4", "l2", "r6", "z5", "x7", "l4", "x6", "z7", "l5", "z6", "l7", "l6",
)

SMEM = pl.BlockSpec(memory_space=pltpu.SMEM)
VMEM = pl.BlockSpec(memory_space=pltpu.VMEM)
HBM = pl.BlockSpec(memory_space=pltpu.HBM)
SMALL = pl.CostEstimate(flops=1, bytes_accessed=1, transcendentals=0)


def after(value, *others):
    return lax.optimization_barrier((value, *others))[0]


def cut_kernel(count, bounds, place_ref, whole_ref, *outs):
    z = place_ref[2]
    depth = outs[0].shape[1]
    outs = list(outs)
    for low, high, stacks in bounds:
        size = high - low
        for m in range(count):
            start = pl.multiple_of((z ^ m) * depth, depth)
            here = slice(m // stacks * size, (m // stacks + 1) * size)
            outs[m % stacks][here, :] = whole_ref[low:high, pl.ds(start, depth)]
        del outs[:stacks]


def cut(whole, count, depth, part, place):
    bounds = [
        (group[0] * part, (group[-1] + 1) * part, 2 if g else count)
        for g, group in enumerate(GROUPS)
    ]
    shapes = [
        jax.ShapeDtypeStruct((count // stacks * (high - low), depth), whole.dtype)
        for low, high, stacks in bounds
        for _ in range(stacks)
    ]
    outs = list(pl.pallas_call(
        functools.partial(cut_kernel, count, bounds),
        in_specs=[SMEM, VMEM],
        out_specs=[VMEM] * len(shapes),
        out_shape=shapes,
        cost_estimate=SMALL,
        compiler_params=pltpu.CompilerParams(vmem_limit_bytes=2**20),
        name="cut",
    )(place, whole))
    return [[outs.pop(0) for _ in range(stacks)] for _, _, stacks in bounds]


def pack_kernel(part, starts, place_ref, *refs):
    z = place_ref[2]
    count = len(starts)
    for c, out in enumerate(refs[count:]):
        for m in range(count):
            rows = pl.ds(pl.multiple_of((z ^ m) * part, part), part)
            first = starts[m] + c * part
            out[rows, :] = refs[m][first : first + part, :]


def pack(blocks, starts, chunks, part, place):
    count = len(blocks)
    shape = jax.ShapeDtypeStruct((count * part, blocks[0].shape[1]), blocks[0].dtype)
    return pl.pallas_call(
        functools.partial(pack_kernel, part, starts),
        in_specs=[SMEM] + [VMEM] * count,
        out_specs=[VMEM] * chunks,
        out_shape=[shape] * chunks,
        cost_estimate=SMALL,
        compiler_params=pltpu.CompilerParams(vmem_limit_bytes=2**20),
        name="pack",
    )(place, *blocks)


def split_kernel(step, whole_ref, high_ref, low_ref, token_ref, buffer, sems):
    count = whole_ref.shape[0] // step
    slots = buffer.shape[0]

    def copy(i):
        return pltpu.make_async_copy(
            whole_ref.at[pl.ds(i * step, step)], buffer.at[i % slots], sems.at[i % slots]
        )

    for i in range(min(slots, count)):
        copy(i).start()
    token_ref[...] = jnp.zeros_like(token_ref)
    for i in range(count):
        copy(i).wait()
        whole = buffer[i % slots]
        high = whole.astype(jnp.bfloat16)
        here = slice(i * step, (i + 1) * step)
        high_ref[here, :] = high
        low_ref[here, :] = (whole - high.astype(jnp.float32)).astype(jnp.bfloat16)
        if i + slots < count:
            copy(i + slots).start()


def split(whole, limit):
    rows, columns = whole.shape
    step = min(128, rows)
    slots = min(8, rows // step)
    half = jax.ShapeDtypeStruct((rows, columns), jnp.bfloat16)
    return pl.pallas_call(
        functools.partial(split_kernel, step),
        in_specs=[HBM],
        out_specs=[VMEM, VMEM, VMEM],
        out_shape=[half, half, jax.ShapeDtypeStruct((8, 128), jnp.float32)],
        scratch_shapes=[
            pltpu.VMEM((slots, step, columns), jnp.float32),
            pltpu.SemaphoreType.DMA((slots,)),
        ],
        cost_estimate=SMALL,
        compiler_params=pltpu.CompilerParams(vmem_limit_bytes=limit * 2**20),
        name="split",
    )(whole)


def product_kernel(count, rows, layout, targets, halves, place_ref, pattern_ref, order_ref, *refs):
    lefts = refs[: len(layout)]
    factors = refs[len(layout) : len(layout) + 2 * halves]
    outs = refs[len(layout) + 2 * halves : -1]
    left = refs[-1]
    depth = lefts[0].shape[1]
    total = count * rows
    chip, core, z = place_ref[0], place_ref[1], place_ref[2]
    tiles = depth // TILE
    for held, pieces in zip(lefts, layout):
        start = 0
        for k, first, size in pieces:
            kind = order_ref[(chip ^ k) * CORES + core]
            high_rows = slice(k * rows + first, k * rows + first + size)
            low_rows = slice(total + k * rows + first, total + k * rows + first + size)
            for t in range(tiles):
                kept = pattern_ref[kind, z * tiles + t].astype(jnp.float32)
                here = slice(t * TILE, (t + 1) * TILE)
                value = held[start : start + size, here] * kept
                high = value.astype(jnp.bfloat16)
                left[high_rows, here] = high
                left[low_rows, here] = (value - high.astype(jnp.float32)).astype(jnp.bfloat16)
            start += size
    columns = factors[0].shape[1]
    width = min(512, columns)
    for half in range(halves):
        high_ref, low_ref = factors[2 * half : 2 * half + 2]
        for j in range(columns // width):
            here = slice(j * width, (j + 1) * width)
            both = jnp.dot(left[...], high_ref[:, here], preferred_element_type=jnp.float32)
            small = jnp.dot(
                left[:total, :], low_ref[:, here], preferred_element_type=jnp.float32
            )
            result = both[:total] + (both[total:] + small)
            there = slice(half * columns + j * width, half * columns + (j + 1) * width)
            for out, blocks in zip(outs, targets):
                for n, k in enumerate(blocks):
                    out[n * rows : (n + 1) * rows, there] = result[k * rows : (k + 1) * rows]


def product(lefts, layout, targets, factors, place, pattern, block_order):
    rows, depth = lefts[0].shape
    count = sum(held.shape[0] for held in lefts) // rows
    halves = len(factors)
    columns = factors[0][0].shape[1]
    total = count * rows
    return pl.pallas_call(
        functools.partial(product_kernel, count, rows, layout, targets, halves),
        in_specs=[SMEM] * 3 + [VMEM] * (len(lefts) + 2 * halves),
        out_specs=[VMEM] * len(targets),
        out_shape=[
            jax.ShapeDtypeStruct((len(blocks) * rows, halves * columns), jnp.float32)
            for blocks in targets
        ],
        scratch_shapes=[pltpu.VMEM((2 * total, depth), jnp.bfloat16)],
        cost_estimate=pl.CostEstimate(
            flops=12 * total * depth * halves * columns, bytes_accessed=1, transcendentals=0
        ),
        compiler_params=pltpu.CompilerParams(vmem_limit_bytes=8 * total * depth + 3 * 2**20),
        name="product",
    )(place, pattern, block_order, *lefts, *[part for pair in factors for part in pair])


def finish_kernel(spec, group, count, part, width, place_ref, bare_ref, occ_ref, virt_ref, *refs):
    out_ref = refs[-1]
    chip, core = place_ref[0], place_ref[1]
    rows_local = CHUNKS * part
    for number, (chunk, halves, s) in enumerate(spec):
        kept, arrived = refs[2 * number], refs[2 * number + 1]
        for position, half in enumerate(halves):
            column = (((chip % group) ^ s) * CORES + (half ^ core)) * width
            columns = pl.ds(pl.multiple_of(column, width), width)
            here = slice(position * width, (position + 1) * width)
            for m in range(count):
                rows = slice(m * rows_local + chunk * part, m * rows_local + (chunk + 1) * part)
                block = slice(m * part, (m + 1) * part)
                ladder = kept[block, here] + arrived[block, here]
                gap = occ_ref[rows, :] + virt_ref[:, columns]
                out_ref[rows, columns] = -(bare_ref[rows, columns] + ladder) / gap


def finish(spec, pairs, group, count, part, width, place, bare, occ, virt):
    return pl.pallas_call(
        functools.partial(finish_kernel, spec, group, count, part, width),
        in_specs=[SMEM] + [VMEM] * (3 + 2 * len(pairs)),
        out_specs=VMEM,
        out_shape=jax.ShapeDtypeStruct(bare.shape, bare.dtype),
        cost_estimate=SMALL,
        compiler_params=pltpu.CompilerParams(vmem_limit_bytes=2 * 2**20),
        name="finish",
    )(place, bare, occ[:, None], virt[None, :], *[part_in for pair in pairs for part_in in pair])


def shards(amplitudes, integrals, bare_terms, pattern, block_order, occ_gap, virt_gap):
    rows_local, columns = amplitudes.shape
    depth, columns_local = integrals.shape
    wide_count = lax.axis_size("wide")
    narrow_count = lax.axis_size("narrow")
    chips = wide_count // CORES
    wide = lax.axis_index("wide")
    z = lax.axis_index("narrow")
    chip = wide // CORES
    core = wide % CORES
    part = rows_local // CHUNKS
    rows = narrow_count * part
    group = chips // narrow_count
    place = jnp.stack([chip, core, z]).astype(jnp.int32)
    chip_bits = [1 << b for b in range(chips.bit_length() - 1)]
    narrow_bits = [1 << b for b in range(narrow_count.bit_length() - 1)]
    targets = [list(range(chips))]
    for bit in reversed(chip_bits):
        targets = [[k for k in targets[0] if not k & bit] + [k for k in targets[0] if k & bit]]
    targets = [targets[0][: chips // 2], targets[0][chips // 2 :]]

    def across(value, mask):
        return lax.ppermute(value, "wide", [(w, w ^ mask) for w in range(wide_count)])

    def across_chips(value, mask):
        return across(value, mask * CORES)

    def along(value, mask):
        return lax.ppermute(value, "narrow", [(n, n ^ mask) for n in range(narrow_count)])

    last = []

    def ordered(*values):
        return list(lax.optimization_barrier((*values, *last))[: len(values)])

    def mark(*values):
        last[:] = values

    swapped = across(integrals, 1)
    pieces = cut(amplitudes, narrow_count, depth, part, place)
    spread = {}
    mine = {}
    held = {}
    layouts = {}
    factors = {}
    state = {}

    def spread_step(g, number):
        size = len(GROUPS[g]) * part
        bit = narrow_bits[number]
        if g == 0:
            if number == 0:
                sends = ordered(*pieces[g][1:])
                mark(*sends)
                spread[g] = {(0, 0): (pieces[g][0], 0)}
                for n, send in enumerate(sends):
                    spread[g][0, n + 1] = (along(send, n + 1), 0)
            return
        if number == 0:
            kept, send = pieces[g]
            (send,) = ordered(send)
            names = [(m, 0) for m in range(1, narrow_count, 2)]
            held_now = {(m, 0): (kept, m // 2 * size) for m in range(0, narrow_count, 2)}
        else:
            held_now = spread[g]
            names = [name for name in held_now if name[0] & bit]
            taken = ordered(*[held_now[name][0] for name in names])
            send = jnp.concatenate(
                [
                    value[held_now[name][1] : held_now[name][1] + size]
                    for name, value in zip(names, taken)
                ],
                axis=0,
            )
        mark(send)
        arrived = along(send, bit)
        spread[g] = {name: value for name, value in held_now.items() if not name[0] & bit}
        for n, (m, s) in enumerate(names):
            spread[g][m ^ bit, s | bit] = (arrived, n * size)

    def pack_step(g):
        blocks = [spread[g][0, s] for s in range(narrow_count)]
        values = ordered(*[value for value, _ in blocks])
        starts = [start for _, start in blocks]
        packed = pack(values, starts, len(GROUPS[g]), part, place)
        mark(*packed)
        mine.update(zip(GROUPS[g], packed))

    def gather_step(chunk, number):
        if number == 0:
            held[chunk] = [mine[chunk]]
            layouts[chunk] = [[(0, 0, rows)]]
        if chunk in FORWARD and chips == 4:
            if number == 0:
                (send,) = ordered(mine[chunk])
                mark(send)
                held[chunk] += [across_chips(send, 1), across_chips(send, 2)]
                layouts[chunk] += [[(1, 0, rows)], [(2, 0, rows)]]
            else:
                near, far = ordered(held[chunk][1], held[chunk][2])
                near, far = near[: rows // 2], far[rows // 2 :]
                mark(near, far)
                held[chunk] += [across_chips(near, 2), across_chips(far, 1)]
                layouts[chunk] += [[(3, 0, rows // 2)], [(3, rows // 2, rows // 2)]]
        elif chunk in DIRECT and chips == 4:
            (send,) = ordered(mine[chunk])
            mark(send)
            held[chunk] += [across_chips(send, k) for k in (3, 1, 2)]
            layouts[chunk] += [[(k, 0, rows)] for k in (3, 1, 2)]
        else:
            bit = chip_bits[number]
            send = jnp.concatenate(ordered(*held[chunk]), axis=0)
            mark(send)
            held[chunk].append(across_chips(send, bit))
            layouts[chunk].append([(k | bit, 0, rows) for k in range(bit)])

    def split_step(half):
        source, limit = ((integrals, 42), (swapped, 6))[half]
        *factors[half], done = split(*ordered(source), limit)
        mark(done)

    def multiply(unit):
        chunk, halves = UNITS[unit]
        partials = product(
            ordered(*held[chunk]),
            layouts[chunk],
            targets,
            [factors[half] for half in halves],
            place,
            pattern,
            block_order,
        )
        mark(*partials)
        state[unit] = {0: partials}

    def exchange_step(unit, bit):
        names = list(state[unit])
        if bit == chip_bits[0]:
            keep, leave = [state[unit][0][0]], ordered(state[unit][0][1])
        else:
            values = ordered(*state[unit].values())
            half = values[0].shape[0] // 2
            keep = [value[:half] for value in values]
            leave = [value[half:] for value in values]
        send = jnp.concatenate(leave, axis=0)
        mark(send)
        arrived = across_chips(send, bit)
        half = keep[0].shape[0]
        state[unit] = dict(zip(names, keep))
        for n, s in enumerate(names):
            state[unit][s | bit] = arrived[n * half : (n + 1) * half]

    def reduce_step(unit, bit, narrow_bit):
        now = dict(zip(state[unit], ordered(*state[unit].values())))
        same = ((chip // bit) & 1) == ((z // narrow_bit) & 1)
        names = [s for s in now if not s & bit]
        send = jnp.concatenate([jnp.where(same, now[s | bit], now[s]) for s in names], axis=0)
        mark(send)
        arrived = along(send, narrow_bit)
        size = now[0].shape[0]
        final = narrow_bit == narrow_bits[-1]
        state[unit] = {}
        for n, s in enumerate(names):
            kept = jnp.where(same, now[s], now[s | bit])
            came = arrived[n * size : (n + 1) * size]
            state[unit][s] = (kept, came) if final else kept + came

    def land(unit):
        names = list(state[unit])
        values = ordered(*[value for name in names for value in state[unit][name]])
        mark(values[-1])
        state[unit] = {name: (values[2 * n], values[2 * n + 1]) for n, name in enumerate(names)}

    steps = []
    for bit in chip_bits:
        if bit < group:
            steps.append(functools.partial(exchange_step, bit=bit))
    for narrow_bit in narrow_bits:
        bit = group * narrow_bit
        steps.append(functools.partial(exchange_step, bit=bit))
        steps.append(functools.partial(reduce_step, bit=bit, narrow_bit=narrow_bit))
    steps.append(land)

    def send_step(unit):
        multiply(unit)
        steps[0](unit)

    if chips == 4 and narrow_count == 4:
        actions = dict(s=spread_step, p=pack_step, f=split_step, g=gather_step, e=send_step)
        actions.update(r=steps[1], x=steps[2], z=steps[3], l=steps[4])
        for name in ORDER:
            actions[name[0]](*[int(number) for number in name[1:]])
    else:
        for half in range(CORES):
            split_step(half)
        for g in range(len(GROUPS)):
            for number in range(len(narrow_bits)):
                spread_step(g, number)
            pack_step(g)
        for chunk in range(CHUNKS):
            for number in range(len(chip_bits)):
                gather_step(chunk, number)
        for tick in range(len(UNITS) + len(steps) - 1):
            if tick < len(UNITS):
                send_step(tick)
            for number in range(len(steps) - 1, 0, -1):
                if 0 <= tick - number < len(UNITS):
                    steps[number](tick - number)

    spec = [(*UNITS[unit], s) for unit in range(len(UNITS)) for s in range(group)]
    pairs = [state[unit][s] for unit in range(len(UNITS)) for s in range(group)]
    return finish(
        spec,
        pairs,
        group,
        narrow_count,
        part,
        columns_local,
        place,
        bare_terms,
        occ_gap,
        virt_gap,
    )


def solution(mesh):
    placed = (
        P(("wide", "narrow"), None),
        P("narrow", "wide"),
        P("wide", "narrow"),
        P(),
        P(),
        P("wide"),
        P("narrow"),
    )
    return jax.shard_map(
        shards, mesh=mesh, in_specs=placed, out_specs=P("wide", "narrow"), check_vma=False
    )
```

```python
import functools

import jax
import jax.numpy as jnp
from jax import lax
from jax.experimental import pallas as pl
from jax.experimental.pallas import tpu as pltpu
from jax.sharding import PartitionSpec as P

TILE = 128
CHUNKS = 4
CORES = 2
DIRECT = ()
FORWARD = (0,)
GROUPS = ((0,), (1,), (2, 3))
UNITS = tuple((chunk, (half,)) for chunk in range(CHUNKS) for half in range(CORES))

ORDER = (
    "s00", "p0", "s10", "g00", "s11", "s20", "g01", "f0", "p1", "g10", "s21", "e0", "f1", "e1",
    "g11", "r0", "p2", "g30", "r1", "g20", "e3", "g31", "x0", "g21", "e6", "z0", "r3", "x1",
    "e2", "r6", "l0", "e4", "z1", "x3", "r2", "e7", "z3", "l1", "x6", "r4", "e5", "z6", "l3",
    "x2", "r7", "x4", "z2", "r5", "x7", "z4", "l2", "z7", "l6", "x5", "z5", "l4", "l7", "l5",
)

SMEM = pl.BlockSpec(memory_space=pltpu.SMEM)
VMEM = pl.BlockSpec(memory_space=pltpu.VMEM)
HBM = pl.BlockSpec(memory_space=pltpu.HBM)
SMALL = pl.CostEstimate(flops=1, bytes_accessed=1, transcendentals=0)


def after(value, *others):
    return lax.optimization_barrier((value, *others))[0]


def cut_kernel(count, bounds, place_ref, whole_ref, *outs):
    z = place_ref[2]
    depth = outs[0].shape[1]
    outs = list(outs)
    for low, high, stacks in bounds:
        size = high - low
        for m in range(count):
            start = pl.multiple_of((z ^ m) * depth, depth)
            here = slice(m // stacks * size, (m // stacks + 1) * size)
            outs[m % stacks][here, :] = whole_ref[low:high, pl.ds(start, depth)]
        del outs[:stacks]


def cut(whole, count, depth, part, place):
    bounds = [
        (group[0] * part, (group[-1] + 1) * part, 2 if g else count)
        for g, group in enumerate(GROUPS)
    ]
    shapes = [
        jax.ShapeDtypeStruct((count // stacks * (high - low), depth), whole.dtype)
        for low, high, stacks in bounds
        for _ in range(stacks)
    ]
    outs = list(pl.pallas_call(
        functools.partial(cut_kernel, count, bounds),
        in_specs=[SMEM, VMEM],
        out_specs=[VMEM] * len(shapes),
        out_shape=shapes,
        cost_estimate=SMALL,
        compiler_params=pltpu.CompilerParams(vmem_limit_bytes=2**20),
        name="cut",
    )(place, whole))
    return [[outs.pop(0) for _ in range(stacks)] for _, _, stacks in bounds]


def pack_kernel(part, starts, place_ref, *refs):
    z = place_ref[2]
    count = len(starts)
    for c, out in enumerate(refs[count:]):
        for m in range(count):
            rows = pl.ds(pl.multiple_of((z ^ m) * part, part), part)
            first = starts[m] + c * part
            out[rows, :] = refs[m][first : first + part, :]


def pack(blocks, starts, chunks, part, place):
    count = len(blocks)
    shape = jax.ShapeDtypeStruct((count * part, blocks[0].shape[1]), blocks[0].dtype)
    return pl.pallas_call(
        functools.partial(pack_kernel, part, starts),
        in_specs=[SMEM] + [VMEM] * count,
        out_specs=[VMEM] * chunks,
        out_shape=[shape] * chunks,
        cost_estimate=SMALL,
        compiler_params=pltpu.CompilerParams(vmem_limit_bytes=2**20),
        name="pack",
    )(place, *blocks)


def split_kernel(step, whole_ref, high_ref, low_ref, token_ref, buffer, sems):
    count = whole_ref.shape[0] // step
    slots = buffer.shape[0]

    def copy(i):
        return pltpu.make_async_copy(
            whole_ref.at[pl.ds(i * step, step)], buffer.at[i % slots], sems.at[i % slots]
        )

    for i in range(min(slots, count)):
        copy(i).start()
    token_ref[...] = jnp.zeros_like(token_ref)
    for i in range(count):
        copy(i).wait()
        whole = buffer[i % slots]
        high = whole.astype(jnp.bfloat16)
        here = slice(i * step, (i + 1) * step)
        high_ref[here, :] = high
        low_ref[here, :] = (whole - high.astype(jnp.float32)).astype(jnp.bfloat16)
        if i + slots < count:
            copy(i + slots).start()


def split(whole, limit):
    rows, columns = whole.shape
    step = min(128, rows)
    slots = min(8, rows // step)
    half = jax.ShapeDtypeStruct((rows, columns), jnp.bfloat16)
    return pl.pallas_call(
        functools.partial(split_kernel, step),
        in_specs=[HBM],
        out_specs=[VMEM, VMEM, VMEM],
        out_shape=[half, half, jax.ShapeDtypeStruct((8, 128), jnp.float32)],
        scratch_shapes=[
            pltpu.VMEM((slots, step, columns), jnp.float32),
            pltpu.SemaphoreType.DMA((slots,)),
        ],
        cost_estimate=SMALL,
        compiler_params=pltpu.CompilerParams(vmem_limit_bytes=limit * 2**20),
        name="split",
    )(whole)


def product_kernel(count, rows, layout, targets, halves, place_ref, pattern_ref, order_ref, *refs):
    lefts = refs[: len(layout)]
    factors = refs[len(layout) : len(layout) + 2 * halves]
    outs = refs[len(layout) + 2 * halves : -1]
    left = refs[-1]
    depth = lefts[0].shape[1]
    total = count * rows
    chip, core, z = place_ref[0], place_ref[1], place_ref[2]
    tiles = depth // TILE
    for held, pieces in zip(lefts, layout):
        start = 0
        for k, first, size in pieces:
            kind = order_ref[(chip ^ k) * CORES + core]
            high_rows = slice(k * rows + first, k * rows + first + size)
            low_rows = slice(total + k * rows + first, total + k * rows + first + size)
            for t in range(tiles):
                kept = pattern_ref[kind, z * tiles + t].astype(jnp.float32)
                here = slice(t * TILE, (t + 1) * TILE)
                value = held[start : start + size, here] * kept
                high = value.astype(jnp.bfloat16)
                left[high_rows, here] = high
                left[low_rows, here] = (value - high.astype(jnp.float32)).astype(jnp.bfloat16)
            start += size
    columns = factors[0].shape[1]
    width = min(512, columns)
    for half in range(halves):
        high_ref, low_ref = factors[2 * half : 2 * half + 2]
        for j in range(columns // width):
            here = slice(j * width, (j + 1) * width)
            both = jnp.dot(left[...], high_ref[:, here], preferred_element_type=jnp.float32)
            small = jnp.dot(
                left[:total, :], low_ref[:, here], preferred_element_type=jnp.float32
            )
            result = both[:total] + (both[total:] + small)
            there = slice(half * columns + j * width, half * columns + (j + 1) * width)
            for out, blocks in zip(outs, targets):
                for n, k in enumerate(blocks):
                    out[n * rows : (n + 1) * rows, there] = result[k * rows : (k + 1) * rows]


def product(lefts, layout, targets, factors, place, pattern, block_order):
    rows, depth = lefts[0].shape
    count = sum(held.shape[0] for held in lefts) // rows
    halves = len(factors)
    columns = factors[0][0].shape[1]
    total = count * rows
    return pl.pallas_call(
        functools.partial(product_kernel, count, rows, layout, targets, halves),
        in_specs=[SMEM] * 3 + [VMEM] * (len(lefts) + 2 * halves),
        out_specs=[VMEM] * len(targets),
        out_shape=[
            jax.ShapeDtypeStruct((len(blocks) * rows, halves * columns), jnp.float32)
            for blocks in targets
        ],
        scratch_shapes=[pltpu.VMEM((2 * total, depth), jnp.bfloat16)],
        cost_estimate=pl.CostEstimate(
            flops=12 * total * depth * halves * columns, bytes_accessed=1, transcendentals=0
        ),
        compiler_params=pltpu.CompilerParams(vmem_limit_bytes=8 * total * depth + 3 * 2**20),
        name="product",
    )(place, pattern, block_order, *lefts, *[part for pair in factors for part in pair])


def finish_kernel(spec, group, count, part, width, place_ref, bare_ref, occ_ref, virt_ref, *refs):
    out_ref = refs[-1]
    chip, core = place_ref[0], place_ref[1]
    rows_local = CHUNKS * part
    for number, (chunk, halves, s) in enumerate(spec):
        kept, arrived = refs[2 * number], refs[2 * number + 1]
        for position, half in enumerate(halves):
            column = (((chip % group) ^ s) * CORES + (half ^ core)) * width
            columns = pl.ds(pl.multiple_of(column, width), width)
            here = slice(position * width, (position + 1) * width)
            for m in range(count):
                rows = slice(m * rows_local + chunk * part, m * rows_local + (chunk + 1) * part)
                block = slice(m * part, (m + 1) * part)
                ladder = kept[block, here] + arrived[block, here]
                gap = occ_ref[rows, :] + virt_ref[:, columns]
                out_ref[rows, columns] = -(bare_ref[rows, columns] + ladder) / gap


def finish(spec, pairs, group, count, part, width, place, bare, occ, virt):
    return pl.pallas_call(
        functools.partial(finish_kernel, spec, group, count, part, width),
        in_specs=[SMEM] + [VMEM] * (3 + 2 * len(pairs)),
        out_specs=VMEM,
        out_shape=jax.ShapeDtypeStruct(bare.shape, bare.dtype),
        cost_estimate=SMALL,
        compiler_params=pltpu.CompilerParams(vmem_limit_bytes=2 * 2**20),
        name="finish",
    )(place, bare, occ[:, None], virt[None, :], *[part_in for pair in pairs for part_in in pair])


def shards(amplitudes, integrals, bare_terms, pattern, block_order, occ_gap, virt_gap):
    rows_local, columns = amplitudes.shape
    depth, columns_local = integrals.shape
    wide_count = lax.axis_size("wide")
    narrow_count = lax.axis_size("narrow")
    chips = wide_count // CORES
    wide = lax.axis_index("wide")
    z = lax.axis_index("narrow")
    chip = wide // CORES
    core = wide % CORES
    part = rows_local // CHUNKS
    rows = narrow_count * part
    group = chips // narrow_count
    place = jnp.stack([chip, core, z]).astype(jnp.int32)
    chip_bits = [1 << b for b in range(chips.bit_length() - 1)]
    narrow_bits = [1 << b for b in range(narrow_count.bit_length() - 1)]
    targets = [list(range(chips))]
    for bit in reversed(chip_bits):
        targets = [[k for k in targets[0] if not k & bit] + [k for k in targets[0] if k & bit]]
    targets = [targets[0][: chips // 2], targets[0][chips // 2 :]]

    def across(value, mask):
        return lax.ppermute(value, "wide", [(w, w ^ mask) for w in range(wide_count)])

    def across_chips(value, mask):
        return across(value, mask * CORES)

    def along(value, mask):
        return lax.ppermute(value, "narrow", [(n, n ^ mask) for n in range(narrow_count)])

    last = []

    def ordered(*values):
        return list(lax.optimization_barrier((*values, *last))[: len(values)])

    def mark(*values):
        last[:] = values

    swapped = across(integrals, 1)
    pieces = cut(amplitudes, narrow_count, depth, part, place)
    spread = {}
    mine = {}
    held = {}
    layouts = {}
    factors = {}
    state = {}

    def spread_step(g, number):
        size = len(GROUPS[g]) * part
        bit = narrow_bits[number]
        if g == 0:
            if number == 0:
                sends = ordered(*pieces[g][1:])
                mark(*sends)
                spread[g] = {(0, 0): (pieces[g][0], 0)}
                for n, send in enumerate(sends):
                    spread[g][0, n + 1] = (along(send, n + 1), 0)
            return
        if number == 0:
            kept, send = pieces[g]
            (send,) = ordered(send)
            names = [(m, 0) for m in range(1, narrow_count, 2)]
            held_now = {(m, 0): (kept, m // 2 * size) for m in range(0, narrow_count, 2)}
        else:
            held_now = spread[g]
            names = [name for name in held_now if name[0] & bit]
            taken = ordered(*[held_now[name][0] for name in names])
            send = jnp.concatenate(
                [
                    value[held_now[name][1] : held_now[name][1] + size]
                    for name, value in zip(names, taken)
                ],
                axis=0,
            )
        mark(send)
        arrived = along(send, bit)
        spread[g] = {name: value for name, value in held_now.items() if not name[0] & bit}
        for n, (m, s) in enumerate(names):
            spread[g][m ^ bit, s | bit] = (arrived, n * size)

    def pack_step(g):
        blocks = [spread[g][0, s] for s in range(narrow_count)]
        values = ordered(*[value for value, _ in blocks])
        starts = [start for _, start in blocks]
        packed = pack(values, starts, len(GROUPS[g]), part, place)
        mark(*packed)
        mine.update(zip(GROUPS[g], packed))

    def gather_step(chunk, number):
        if number == 0:
            held[chunk] = [mine[chunk]]
            layouts[chunk] = [[(0, 0, rows)]]
        if chunk in FORWARD and chips == 4:
            if number == 0:
                (send,) = ordered(mine[chunk])
                mark(send)
                held[chunk] += [across_chips(send, 1), across_chips(send, 2)]
                layouts[chunk] += [[(1, 0, rows)], [(2, 0, rows)]]
            else:
                near, far = ordered(held[chunk][1], held[chunk][2])
                near, far = near[: rows // 2], far[rows // 2 :]
                mark(near, far)
                held[chunk] += [across_chips(near, 2), across_chips(far, 1)]
                layouts[chunk] += [[(3, 0, rows // 2)], [(3, rows // 2, rows // 2)]]
        elif chunk in DIRECT and chips == 4:
            (send,) = ordered(mine[chunk])
            mark(send)
            held[chunk] += [across_chips(send, k) for k in (3, 1, 2)]
            layouts[chunk] += [[(k, 0, rows)] for k in (3, 1, 2)]
        else:
            bit = chip_bits[number]
            send = jnp.concatenate(ordered(*held[chunk]), axis=0)
            mark(send)
            held[chunk].append(across_chips(send, bit))
            layouts[chunk].append([(k | bit, 0, rows) for k in range(bit)])

    def split_step(half):
        source, limit = ((integrals, 42), (swapped, 6))[half]
        *factors[half], done = split(*ordered(source), limit)
        mark(done)

    def multiply(unit):
        chunk, halves = UNITS[unit]
        partials = product(
            ordered(*held[chunk]),
            layouts[chunk],
            targets,
            [factors[half] for half in halves],
            place,
            pattern,
            block_order,
        )
        mark(*partials)
        state[unit] = {0: partials}

    def exchange_step(unit, bit):
        names = list(state[unit])
        if bit == chip_bits[0]:
            keep, leave = [state[unit][0][0]], ordered(state[unit][0][1])
        else:
            values = ordered(*state[unit].values())
            half = values[0].shape[0] // 2
            keep = [value[:half] for value in values]
            leave = [value[half:] for value in values]
        send = jnp.concatenate(leave, axis=0)
        mark(send)
        arrived = across_chips(send, bit)
        half = keep[0].shape[0]
        state[unit] = dict(zip(names, keep))
        for n, s in enumerate(names):
            state[unit][s | bit] = arrived[n * half : (n + 1) * half]

    def reduce_step(unit, bit, narrow_bit):
        now = dict(zip(state[unit], ordered(*state[unit].values())))
        same = ((chip // bit) & 1) == ((z // narrow_bit) & 1)
        names = [s for s in now if not s & bit]
        send = jnp.concatenate([jnp.where(same, now[s | bit], now[s]) for s in names], axis=0)
        mark(send)
        arrived = along(send, narrow_bit)
        size = now[0].shape[0]
        final = narrow_bit == narrow_bits[-1]
        state[unit] = {}
        for n, s in enumerate(names):
            kept = jnp.where(same, now[s], now[s | bit])
            came = arrived[n * size : (n + 1) * size]
            state[unit][s] = (kept, came) if final else kept + came

    def land(unit):
        names = list(state[unit])
        values = ordered(*[value for name in names for value in state[unit][name]])
        mark(values[-1])
        state[unit] = {name: (values[2 * n], values[2 * n + 1]) for n, name in enumerate(names)}

    steps = []
    for bit in chip_bits:
        if bit < group:
            steps.append(functools.partial(exchange_step, bit=bit))
    for narrow_bit in narrow_bits:
        bit = group * narrow_bit
        steps.append(functools.partial(exchange_step, bit=bit))
        steps.append(functools.partial(reduce_step, bit=bit, narrow_bit=narrow_bit))
    steps.append(land)

    def send_step(unit):
        multiply(unit)
        steps[0](unit)

    if chips == 4 and narrow_count == 4:
        actions = dict(s=spread_step, p=pack_step, f=split_step, g=gather_step, e=send_step)
        actions.update(r=steps[1], x=steps[2], z=steps[3], l=steps[4])
        for name in ORDER:
            actions[name[0]](*[int(number) for number in name[1:]])
    else:
        for half in range(CORES):
            split_step(half)
        for g in range(len(GROUPS)):
            for number in range(len(narrow_bits)):
                spread_step(g, number)
            pack_step(g)
        for chunk in range(CHUNKS):
            for number in range(len(chip_bits)):
                gather_step(chunk, number)
        for tick in range(len(UNITS) + len(steps) - 1):
            if tick < len(UNITS):
                send_step(tick)
            for number in range(len(steps) - 1, 0, -1):
                if 0 <= tick - number < len(UNITS):
                    steps[number](tick - number)

    spec = [(*UNITS[unit], s) for unit in range(len(UNITS)) for s in range(group)]
    pairs = [state[unit][s] for unit in range(len(UNITS)) for s in range(group)]
    return finish(
        spec,
        pairs,
        group,
        narrow_count,
        part,
        columns_local,
        place,
        bare_terms,
        occ_gap,
        virt_gap,
    )


def solution(mesh):
    placed = (
        P(("wide", "narrow"), None),
        P("narrow", "wide"),
        P("wide", "narrow"),
        P(),
        P(),
        P("wide"),
        P("narrow"),
    )
    return jax.shard_map(
        shards, mesh=mesh, in_specs=placed, out_specs=P("wide", "narrow"), check_vma=False
    )
```

```python
import functools

import jax
import jax.numpy as jnp
from jax import lax
from jax.experimental import pallas as pl
from jax.experimental.pallas import tpu as pltpu
from jax.sharding import PartitionSpec as P

TILE = 128
CHUNKS = 4
CORES = 2
DIRECT = ()
FORWARD = (0,)
GROUPS = ((0,), (1,), (2, 3))
UNITS = tuple((chunk, (half,)) for chunk in range(CHUNKS) for half in range(CORES))

ORDER = (
    "s00", "p0", "s10", "g00", "s11", "s20", "g01", "f0", "p1", "g10", "s21", "e0", "f1", "e1",
    "g11", "r0", "p2", "g20", "r1", "x0", "g30", "g21", "e2", "z0", "e3", "x1", "g31", "r2",
    "l0", "e5", "z1", "r3", "e4", "x2", "r5", "l1", "e6", "z2", "x3", "r4", "e7", "z3", "x5",
    "l2", "r6", "x4", "z5", "r7", "l3", "z4", "x6", "l5", "z6", "x7", "l4", "z7", "l6", "l7",
)

SMEM = pl.BlockSpec(memory_space=pltpu.SMEM)
VMEM = pl.BlockSpec(memory_space=pltpu.VMEM)
HBM = pl.BlockSpec(memory_space=pltpu.HBM)
SMALL = pl.CostEstimate(flops=1, bytes_accessed=1, transcendentals=0)


def after(value, *others):
    return lax.optimization_barrier((value, *others))[0]


def cut_kernel(count, bounds, place_ref, whole_ref, *outs):
    z = place_ref[2]
    depth = outs[0].shape[1]
    outs = list(outs)
    for low, high, stacks in bounds:
        size = high - low
        for m in range(count):
            start = pl.multiple_of((z ^ m) * depth, depth)
            here = slice(m // stacks * size, (m // stacks + 1) * size)
            outs[m % stacks][here, :] = whole_ref[low:high, pl.ds(start, depth)]
        del outs[:stacks]


def cut(whole, count, depth, part, place):
    bounds = [
        (group[0] * part, (group[-1] + 1) * part, 2 if g else count)
        for g, group in enumerate(GROUPS)
    ]
    shapes = [
        jax.ShapeDtypeStruct((count // stacks * (high - low), depth), whole.dtype)
        for low, high, stacks in bounds
        for _ in range(stacks)
    ]
    outs = list(pl.pallas_call(
        functools.partial(cut_kernel, count, bounds),
        in_specs=[SMEM, VMEM],
        out_specs=[VMEM] * len(shapes),
        out_shape=shapes,
        cost_estimate=SMALL,
        compiler_params=pltpu.CompilerParams(vmem_limit_bytes=2**20),
        name="cut",
    )(place, whole))
    return [[outs.pop(0) for _ in range(stacks)] for _, _, stacks in bounds]


def pack_kernel(part, starts, place_ref, *refs):
    z = place_ref[2]
    count = len(starts)
    for c, out in enumerate(refs[count:]):
        for m in range(count):
            rows = pl.ds(pl.multiple_of((z ^ m) * part, part), part)
            first = starts[m] + c * part
            out[rows, :] = refs[m][first : first + part, :]


def pack(blocks, starts, chunks, part, place):
    count = len(blocks)
    shape = jax.ShapeDtypeStruct((count * part, blocks[0].shape[1]), blocks[0].dtype)
    return pl.pallas_call(
        functools.partial(pack_kernel, part, starts),
        in_specs=[SMEM] + [VMEM] * count,
        out_specs=[VMEM] * chunks,
        out_shape=[shape] * chunks,
        cost_estimate=SMALL,
        compiler_params=pltpu.CompilerParams(vmem_limit_bytes=2**20),
        name="pack",
    )(place, *blocks)


def split_kernel(step, whole_ref, high_ref, low_ref, token_ref, buffer, sems):
    count = whole_ref.shape[0] // step
    slots = buffer.shape[0]

    def copy(i):
        return pltpu.make_async_copy(
            whole_ref.at[pl.ds(i * step, step)], buffer.at[i % slots], sems.at[i % slots]
        )

    for i in range(min(slots, count)):
        copy(i).start()
    token_ref[...] = jnp.zeros_like(token_ref)
    for i in range(count):
        copy(i).wait()
        whole = buffer[i % slots]
        high = whole.astype(jnp.bfloat16)
        here = slice(i * step, (i + 1) * step)
        high_ref[here, :] = high
        low_ref[here, :] = (whole - high.astype(jnp.float32)).astype(jnp.bfloat16)
        if i + slots < count:
            copy(i + slots).start()


def split(whole, limit):
    rows, columns = whole.shape
    step = min(128, rows)
    slots = min(8, rows // step)
    half = jax.ShapeDtypeStruct((rows, columns), jnp.bfloat16)
    return pl.pallas_call(
        functools.partial(split_kernel, step),
        in_specs=[HBM],
        out_specs=[VMEM, VMEM, VMEM],
        out_shape=[half, half, jax.ShapeDtypeStruct((8, 128), jnp.float32)],
        scratch_shapes=[
            pltpu.VMEM((slots, step, columns), jnp.float32),
            pltpu.SemaphoreType.DMA((slots,)),
        ],
        cost_estimate=SMALL,
        compiler_params=pltpu.CompilerParams(vmem_limit_bytes=limit * 2**20),
        name="split",
    )(whole)


def product_kernel(count, rows, layout, targets, halves, place_ref, pattern_ref, order_ref, *refs):
    lefts = refs[: len(layout)]
    factors = refs[len(layout) : len(layout) + 2 * halves]
    outs = refs[len(layout) + 2 * halves : -1]
    left = refs[-1]
    depth = lefts[0].shape[1]
    total = count * rows
    chip, core, z = place_ref[0], place_ref[1], place_ref[2]
    tiles = depth // TILE
    for held, pieces in zip(lefts, layout):
        start = 0
        for k, first, size in pieces:
            kind = order_ref[(chip ^ k) * CORES + core]
            high_rows = slice(k * rows + first, k * rows + first + size)
            low_rows = slice(total + k * rows + first, total + k * rows + first + size)
            for t in range(tiles):
                kept = pattern_ref[kind, z * tiles + t].astype(jnp.float32)
                here = slice(t * TILE, (t + 1) * TILE)
                value = held[start : start + size, here] * kept
                high = value.astype(jnp.bfloat16)
                left[high_rows, here] = high
                left[low_rows, here] = (value - high.astype(jnp.float32)).astype(jnp.bfloat16)
            start += size
    columns = factors[0].shape[1]
    width = min(512, columns)
    for half in range(halves):
        high_ref, low_ref = factors[2 * half : 2 * half + 2]
        for j in range(columns // width):
            here = slice(j * width, (j + 1) * width)
            both = jnp.dot(left[...], high_ref[:, here], preferred_element_type=jnp.float32)
            small = jnp.dot(
                left[:total, :], low_ref[:, here], preferred_element_type=jnp.float32
            )
            result = both[:total] + (both[total:] + small)
            there = slice(half * columns + j * width, half * columns + (j + 1) * width)
            for out, blocks in zip(outs, targets):
                for n, k in enumerate(blocks):
                    out[n * rows : (n + 1) * rows, there] = result[k * rows : (k + 1) * rows]


def product(lefts, layout, targets, factors, place, pattern, block_order):
    rows, depth = lefts[0].shape
    count = sum(held.shape[0] for held in lefts) // rows
    halves = len(factors)
    columns = factors[0][0].shape[1]
    total = count * rows
    return pl.pallas_call(
        functools.partial(product_kernel, count, rows, layout, targets, halves),
        in_specs=[SMEM] * 3 + [VMEM] * (len(lefts) + 2 * halves),
        out_specs=[VMEM] * len(targets),
        out_shape=[
            jax.ShapeDtypeStruct((len(blocks) * rows, halves * columns), jnp.float32)
            for blocks in targets
        ],
        scratch_shapes=[pltpu.VMEM((2 * total, depth), jnp.bfloat16)],
        cost_estimate=pl.CostEstimate(
            flops=12 * total * depth * halves * columns, bytes_accessed=1, transcendentals=0
        ),
        compiler_params=pltpu.CompilerParams(vmem_limit_bytes=8 * total * depth + 3 * 2**20),
        name="product",
    )(place, pattern, block_order, *lefts, *[part for pair in factors for part in pair])


def finish_kernel(spec, group, count, part, width, place_ref, bare_ref, occ_ref, virt_ref, *refs):
    out_ref = refs[-1]
    chip, core = place_ref[0], place_ref[1]
    rows_local = CHUNKS * part
    for number, (chunk, halves, s) in enumerate(spec):
        kept, arrived = refs[2 * number], refs[2 * number + 1]
        for position, half in enumerate(halves):
            column = (((chip % group) ^ s) * CORES + (half ^ core)) * width
            columns = pl.ds(pl.multiple_of(column, width), width)
            here = slice(position * width, (position + 1) * width)
            for m in range(count):
                rows = slice(m * rows_local + chunk * part, m * rows_local + (chunk + 1) * part)
                block = slice(m * part, (m + 1) * part)
                ladder = kept[block, here] + arrived[block, here]
                gap = occ_ref[rows, :] + virt_ref[:, columns]
                out_ref[rows, columns] = -(bare_ref[rows, columns] + ladder) / gap


def finish(spec, pairs, group, count, part, width, place, bare, occ, virt):
    return pl.pallas_call(
        functools.partial(finish_kernel, spec, group, count, part, width),
        in_specs=[SMEM] + [VMEM] * (3 + 2 * len(pairs)),
        out_specs=VMEM,
        out_shape=jax.ShapeDtypeStruct(bare.shape, bare.dtype),
        cost_estimate=SMALL,
        compiler_params=pltpu.CompilerParams(vmem_limit_bytes=2 * 2**20),
        name="finish",
    )(place, bare, occ[:, None], virt[None, :], *[part_in for pair in pairs for part_in in pair])


def shards(amplitudes, integrals, bare_terms, pattern, block_order, occ_gap, virt_gap):
    rows_local, columns = amplitudes.shape
    depth, columns_local = integrals.shape
    wide_count = lax.axis_size("wide")
    narrow_count = lax.axis_size("narrow")
    chips = wide_count // CORES
    wide = lax.axis_index("wide")
    z = lax.axis_index("narrow")
    chip = wide // CORES
    core = wide % CORES
    part = rows_local // CHUNKS
    rows = narrow_count * part
    group = chips // narrow_count
    place = jnp.stack([chip, core, z]).astype(jnp.int32)
    chip_bits = [1 << b for b in range(chips.bit_length() - 1)]
    narrow_bits = [1 << b for b in range(narrow_count.bit_length() - 1)]
    targets = [list(range(chips))]
    for bit in reversed(chip_bits):
        targets = [[k for k in targets[0] if not k & bit] + [k for k in targets[0] if k & bit]]
    targets = [targets[0][: chips // 2], targets[0][chips // 2 :]]

    def across(value, mask):
        return lax.ppermute(value, "wide", [(w, w ^ mask) for w in range(wide_count)])

    def across_chips(value, mask):
        return across(value, mask * CORES)

    def along(value, mask):
        return lax.ppermute(value, "narrow", [(n, n ^ mask) for n in range(narrow_count)])

    last = []

    def ordered(*values):
        return list(lax.optimization_barrier((*values, *last))[: len(values)])

    def mark(*values):
        last[:] = values

    swapped = across(integrals, 1)
    pieces = cut(amplitudes, narrow_count, depth, part, place)
    spread = {}
    mine = {}
    held = {}
    layouts = {}
    factors = {}
    state = {}

    def spread_step(g, number):
        size = len(GROUPS[g]) * part
        bit = narrow_bits[number]
        if g == 0:
            if number == 0:
                sends = ordered(*pieces[g][1:])
                mark(*sends)
                spread[g] = {(0, 0): (pieces[g][0], 0)}
                for n, send in enumerate(sends):
                    spread[g][0, n + 1] = (along(send, n + 1), 0)
            return
        if number == 0:
            kept, send = pieces[g]
            (send,) = ordered(send)
            names = [(m, 0) for m in range(1, narrow_count, 2)]
            held_now = {(m, 0): (kept, m // 2 * size) for m in range(0, narrow_count, 2)}
        else:
            held_now = spread[g]
            names = [name for name in held_now if name[0] & bit]
            taken = ordered(*[held_now[name][0] for name in names])
            send = jnp.concatenate(
                [
                    value[held_now[name][1] : held_now[name][1] + size]
                    for name, value in zip(names, taken)
                ],
                axis=0,
            )
        mark(send)
        arrived = along(send, bit)
        spread[g] = {name: value for name, value in held_now.items() if not name[0] & bit}
        for n, (m, s) in enumerate(names):
            spread[g][m ^ bit, s | bit] = (arrived, n * size)

    def pack_step(g):
        blocks = [spread[g][0, s] for s in range(narrow_count)]
        values = ordered(*[value for value, _ in blocks])
        starts = [start for _, start in blocks]
        packed = pack(values, starts, len(GROUPS[g]), part, place)
        mark(*packed)
        mine.update(zip(GROUPS[g], packed))

    def gather_step(chunk, number):
        if number == 0:
            held[chunk] = [mine[chunk]]
            layouts[chunk] = [[(0, 0, rows)]]
        if chunk in FORWARD and chips == 4:
            if number == 0:
                (send,) = ordered(mine[chunk])
                mark(send)
                held[chunk] += [across_chips(send, 1), across_chips(send, 2)]
                layouts[chunk] += [[(1, 0, rows)], [(2, 0, rows)]]
            else:
                near, far = ordered(held[chunk][1], held[chunk][2])
                near, far = near[: rows // 2], far[rows // 2 :]
                mark(near, far)
                held[chunk] += [across_chips(near, 2), across_chips(far, 1)]
                layouts[chunk] += [[(3, 0, rows // 2)], [(3, rows // 2, rows // 2)]]
        elif chunk in DIRECT and chips == 4:
            (send,) = ordered(mine[chunk])
            mark(send)
            held[chunk] += [across_chips(send, k) for k in (3, 1, 2)]
            layouts[chunk] += [[(k, 0, rows)] for k in (3, 1, 2)]
        else:
            bit = chip_bits[number]
            send = jnp.concatenate(ordered(*held[chunk]), axis=0)
            mark(send)
            held[chunk].append(across_chips(send, bit))
            layouts[chunk].append([(k | bit, 0, rows) for k in range(bit)])

    def split_step(half):
        source, limit = ((integrals, 42), (swapped, 6))[half]
        *factors[half], done = split(*ordered(source), limit)
        mark(done)

    def multiply(unit):
        chunk, halves = UNITS[unit]
        partials = product(
            ordered(*held[chunk]),
            layouts[chunk],
            targets,
            [factors[half] for half in halves],
            place,
            pattern,
            block_order,
        )
        mark(*partials)
        state[unit] = {0: partials}

    def exchange_step(unit, bit):
        names = list(state[unit])
        if bit == chip_bits[0]:
            keep, leave = [state[unit][0][0]], ordered(state[unit][0][1])
        else:
            values = ordered(*state[unit].values())
            half = values[0].shape[0] // 2
            keep = [value[:half] for value in values]
            leave = [value[half:] for value in values]
        send = jnp.concatenate(leave, axis=0)
        mark(send)
        arrived = across_chips(send, bit)
        half = keep[0].shape[0]
        state[unit] = dict(zip(names, keep))
        for n, s in enumerate(names):
            state[unit][s | bit] = arrived[n * half : (n + 1) * half]

    def reduce_step(unit, bit, narrow_bit):
        now = dict(zip(state[unit], ordered(*state[unit].values())))
        same = ((chip // bit) & 1) == ((z // narrow_bit) & 1)
        names = [s for s in now if not s & bit]
        send = jnp.concatenate([jnp.where(same, now[s | bit], now[s]) for s in names], axis=0)
        mark(send)
        arrived = along(send, narrow_bit)
        size = now[0].shape[0]
        final = narrow_bit == narrow_bits[-1]
        state[unit] = {}
        for n, s in enumerate(names):
            kept = jnp.where(same, now[s], now[s | bit])
            came = arrived[n * size : (n + 1) * size]
            state[unit][s] = (kept, came) if final else kept + came

    def land(unit):
        names = list(state[unit])
        values = ordered(*[value for name in names for value in state[unit][name]])
        mark(values[-1])
        state[unit] = {name: (values[2 * n], values[2 * n + 1]) for n, name in enumerate(names)}

    steps = []
    for bit in chip_bits:
        if bit < group:
            steps.append(functools.partial(exchange_step, bit=bit))
    for narrow_bit in narrow_bits:
        bit = group * narrow_bit
        steps.append(functools.partial(exchange_step, bit=bit))
        steps.append(functools.partial(reduce_step, bit=bit, narrow_bit=narrow_bit))
    steps.append(land)

    def send_step(unit):
        multiply(unit)
        steps[0](unit)

    if chips == 4 and narrow_count == 4:
        actions = dict(s=spread_step, p=pack_step, f=split_step, g=gather_step, e=send_step)
        actions.update(r=steps[1], x=steps[2], z=steps[3], l=steps[4])
        for name in ORDER:
            actions[name[0]](*[int(number) for number in name[1:]])
    else:
        for half in range(CORES):
            split_step(half)
        for g in range(len(GROUPS)):
            for number in range(len(narrow_bits)):
                spread_step(g, number)
            pack_step(g)
        for chunk in range(CHUNKS):
            for number in range(len(chip_bits)):
                gather_step(chunk, number)
        for tick in range(len(UNITS) + len(steps) - 1):
            if tick < len(UNITS):
                send_step(tick)
            for number in range(len(steps) - 1, 0, -1):
                if 0 <= tick - number < len(UNITS):
                    steps[number](tick - number)

    spec = [(*UNITS[unit], s) for unit in range(len(UNITS)) for s in range(group)]
    pairs = [state[unit][s] for unit in range(len(UNITS)) for s in range(group)]
    return finish(
        spec,
        pairs,
        group,
        narrow_count,
        part,
        columns_local,
        place,
        bare_terms,
        occ_gap,
        virt_gap,
    )


def solution(mesh):
    placed = (
        P(("wide", "narrow"), None),
        P("narrow", "wide"),
        P("wide", "narrow"),
        P(),
        P(),
        P("wide"),
        P("narrow"),
    )
    return jax.shard_map(
        shards, mesh=mesh, in_specs=placed, out_specs=P("wide", "narrow"), check_vma=False
    )
```
